32 devices in a mesh: dp: 8 (over z, x), blk: 4 (over y, core).
Axes of the slice: x: 2, y: 2, z: 4, core: 2. Of those that a mesh axis runs over, the one named last changes fastest.
Arguments:
- inputs: bfloat16 [16, 2048, 768], P('dp', 'blk'), may hold values from -6 to 6
- doc_lengths: int32 [16, 8], P('dp'), may hold values from 0 to 2048, as said below
- norm1_gain: float32 [768], replicated, may hold values from 0.25 to 1.75
- w_query: bfloat16 [768, 768], replicated, may hold values from -0.21875 to 0.21875
- w_key: bfloat16 [768, 768], replicated, may hold values from -0.21875 to 0.21875
- w_value: bfloat16 [768, 768], replicated, may hold values from -0.21875 to 0.21875
- head_mix_pre: float32 [12, 12], replicated, may hold values from -3.5 to 3.5
- head_mix_post: float32 [12, 12], replicated, may hold values from -1.75 to 1.75
- w_attn_out: bfloat16 [768, 768], replicated, may hold values from -1.25 to 1.25
- norm2_gain: float32 [768], replicated, may hold values from 0.25 to 1.75
- w_ff_in: bfloat16 [768, 3072], replicated, may hold values from -0.21875 to 0.21875
- w_ff_out: bfloat16 [3072, 768], replicated, may hold values from -0.109375 to 0.109375
- out_cotangent: bfloat16 [16, 2048, 768], P('dp', 'blk'), may hold values from -6 to 6
Outputs:
- output: bfloat16 [16, 2048, 768], P('dp', 'blk')
- input_grad: bfloat16 [16, 2048, 768], P('dp', 'blk')
- grad_norm1_gain: float32 [768], P(('dp', 'blk'))
- grad_w_query: float32 [768, 768], P(('dp', 'blk'))
- grad_w_key: float32 [768, 768], P(('dp', 'blk'))
- grad_w_value: float32 [768, 768], P(('dp', 'blk'))
- grad_head_mix_pre: float32 [12, 12], replicated
- grad_head_mix_post: float32 [12, 12], replicated
- grad_w_attn_out: float32 [768, 768], P(('dp', 'blk'))
- grad_norm2_gain: float32 [768], P(('dp', 'blk'))
- grad_w_ff_in: float32 [768, 3072], P(('dp', 'blk'))
- grad_w_ff_out: float32 [3072, 768], P(('dp', 'blk'))
The draws below stay inside these ranges and needn't reach their ends.
Inputs may be any that keep to these rules, and one draw needn't show every extreme that they name: `doc_lengths`: each row lists its documents' lengths in order, multiples of 256 that sum to 2048, with zeros after the last document. Among the rows of one index of dp, one is a single document of 2048 tokens.
All inputs are finite; a program needn't handle non-finite values.
Results may differ from the reference program's by a relative error of at most 0.015.
The reference program's roundings to bfloat16 on the way count: a program that leaves them out, or rounds other values in their place, can miss the bound.
Values may be sent and summed in bfloat16 or wider, within the bound.
No kernel may reach another device: no remote copies, remote signals or barrier semaphores. Data moves between devices by JAX's collectives and lax.ppermute only.
A program may use at most 384 MiB of HBM per device.

```python
import jax
import jax.numpy as jnp
from jax import lax

D = 768
HEADS = 12
HEAD_DIM = 64
FF = 3072
ROW_LEN = 2048
UNITS = 8
ROWS_DEV = 2
NROWS = 16


def draw_doc_lengths(key, part):
    key = jax.random.fold_in(key, 11)
    cut_key, pick_key = jax.random.split(key)
    groups = NROWS // ROWS_DEV
    cuts = jax.random.randint(cut_key, (NROWS, UNITS - 1), 0, 2).astype(jnp.int32)
    picks = jax.random.randint(pick_key, (groups,), 0, ROWS_DEV).astype(jnp.int32)
    row_ids = jnp.arange(NROWS, dtype=jnp.int32)
    single = row_ids % ROWS_DEV == picks[row_ids // ROWS_DEV]
    cuts = jnp.where(single[:, None], 0, cuts)
    endings = jnp.concatenate([cuts, jnp.ones((NROWS, 1), jnp.int32)], axis=1)
    counted = jnp.cumsum(endings, axis=1)
    unit_ends = jnp.arange(UNITS, dtype=jnp.int32) + 1
    slots = jnp.arange(UNITS, dtype=jnp.int32)
    matches = (endings[:, None, :] == 1) & (counted[:, None, :] == slots[None, :, None] + 1)
    stops = jnp.sum(jnp.where(matches, unit_ends[None, None, :], 0), axis=2)
    doc_total = counted[:, -1]
    stops = jnp.where(slots[None, :] < doc_total[:, None], stops, UNITS)
    previous = jnp.concatenate([jnp.zeros((NROWS, 1), jnp.int32), stops[:, :-1]], axis=1)
    return ((stops - previous) * (ROW_LEN // UNITS)).astype(jnp.int32)


def block_levels(own_key, extent, cuts, smallest, largest):
    level, own = 1.0, jax.random.fold_in(own_key, 6)
    for axis_at, shards_of in cuts:
        steps = jnp.exp(jax.random.uniform(jax.random.fold_in(own, axis_at), (shards_of,), jnp.float32, smallest / len(cuts), largest / len(cuts)))
        level = level * jnp.repeat(steps, extent[axis_at] // shards_of).reshape([-1 if axis == axis_at else 1 for axis in range(len(extent))])
    return level


def scatter_about(key, shape, width, most, shards=(), kind=jnp.bfloat16):
    entries = jax.random.normal(key, shape, jnp.float32) * width
    if len(shards) > 0:
        entries = block_levels(key, shape, shards, -0.22, 0.18) * entries
    return jnp.clip(entries, min=-most, max=most).astype(kind)


def setup_inputs(seed: int = 0) -> dict:
    arg_keys = jax.random.split(jax.random.key(seed), 14)
    inputs = scatter_about(arg_keys[0], (NROWS, ROW_LEN, D), 1.0, 6.0, ((0, 8), (1, 4)))
    doc_lengths = draw_doc_lengths(jax.random.fold_in(arg_keys[13], 71), 0)
    norm1_gain = jnp.clip(1.0 + 0.15 * jax.random.normal(arg_keys[2], (D,), jnp.float32), 0.25, 1.75)
    w_query = scatter_about(arg_keys[3], (D, D), D ** -0.5, 0.21875)
    w_key = scatter_about(arg_keys[4], (D, D), D ** -0.5, 0.21875)
    w_value = scatter_about(arg_keys[5], (D, D), D ** -0.5, 0.21875)
    head_mix_pre = scatter_about(arg_keys[6], (HEADS, HEADS), (HEADS // 4) ** -0.5, 3.5, (), jnp.float32)
    head_mix_post = scatter_about(arg_keys[7], (HEADS, HEADS), HEADS ** -0.5, 1.75, (), jnp.float32)
    w_attn_out = scatter_about(arg_keys[8], (D, D), (D // 32) ** -0.5, 1.25)
    norm2_gain = jnp.clip(1.0 + 0.15 * jax.random.normal(arg_keys[9], (D,), jnp.float32), 0.25, 1.75)
    w_ff_in = scatter_about(arg_keys[10], (D, FF), D ** -0.5, 0.21875)
    w_ff_out = scatter_about(arg_keys[11], (FF, D), FF ** -0.5, 0.109375)
    out_cotangent = scatter_about(arg_keys[12], (NROWS, ROW_LEN, D), 1.0, 6.0, ((0, 8), (1, 4)))
    return dict(inputs=inputs, doc_lengths=doc_lengths, norm1_gain=norm1_gain, w_query=w_query, w_key=w_key, w_value=w_value, head_mix_pre=head_mix_pre, head_mix_post=head_mix_post, w_attn_out=w_attn_out, norm2_gain=norm2_gain, w_ff_in=w_ff_in, w_ff_out=w_ff_out, out_cotangent=out_cotangent)


EPSILON = 1e-06
MASKED = -1e+30
PRECISE = lax.Precision.HIGHEST

@jax.custom_vjp
def low(v):
    return lax.optimization_barrier(v.astype(jnp.bfloat16)).astype(jnp.float32)

@jax.custom_vjp
def low_back(v):
    return v

def low_keep(v):
    return (low(v), None)

def low_pass(kept, grad):
    return (grad,)

def back_keep(v):
    return (v, None)

def back_low(kept, grad):
    return (low(grad),)
low.defvjp(low_keep, low_pass)
low_back.defvjp(back_keep, back_low)

def rms_norm(values, scales):
    factor = lax.rsqrt(lax.optimization_barrier(jnp.mean(values * values, axis=-1, keepdims=True)) + EPSILON)
    return values * factor * scales

def matmul(former, latter):
    return jnp.dot(former, latter, preferred_element_type=jnp.float32, precision=PRECISE)

def document_ids(lengths, positions):
    bounds = jnp.cumsum(lengths)
    return lax.optimization_barrier(jnp.sum((positions[:, None] >= bounds[None, :]).astype(jnp.int32), axis=1))

def attend_block(first_row, query_heads, key_heads, value_heads, documents, mix_pre, mix_post):
    block_rows = query_heads.shape[1]
    query_pos = first_row + jnp.arange(block_rows, dtype=jnp.int32)
    key_pos = jnp.arange(ROW_LEN, dtype=jnp.int32)
    query_docs = lax.dynamic_slice_in_dim(documents, first_row, block_rows)
    visible = (key_pos[None, :] <= query_pos[:, None]) & (documents[None, :] == query_docs[:, None])
    scaled = low_back(jnp.einsum('hqd,hkd->hqk', query_heads, key_heads, precision=PRECISE) * HEAD_DIM ** (-0.5))
    mixed_scores = jnp.einsum('hqk,hg->gqk', scaled, mix_pre, precision=PRECISE)
    mixed_scores = jnp.where(visible[None], mixed_scores, MASKED)
    soft_weights = jax.nn.softmax(mixed_scores, axis=-1)
    post_mix = low(jnp.einsum('gqk,gh->hqk', soft_weights, mix_post, precision=PRECISE))
    return jnp.einsum('hqk,hkd->hqd', post_mix, value_heads, precision=PRECISE)

def row_layer(row_in, lengths, gain_one, w_query, w_key, w_value, mix_pre, mix_post, w_attn_out, gain_two, w_ff_in, w_ff_out):
    documents = document_ids(lengths, jnp.arange(ROW_LEN, dtype=jnp.int32))
    normed_one = low(rms_norm(row_in, gain_one))

    def heads_of(weight):
        projected = low(low_back(matmul(normed_one, weight)))
        return projected.reshape(ROW_LEN, HEADS, HEAD_DIM).transpose(1, 0, 2)
    query_heads = heads_of(w_query)
    key_heads = heads_of(w_key)
    value_heads = heads_of(w_value)
    block_rows = min(512, ROW_LEN)
    block_count = ROW_LEN // block_rows
    starts = jnp.arange(block_count, dtype=jnp.int32) * block_rows
    query_blocks = query_heads.reshape(HEADS, block_count, block_rows, HEAD_DIM).transpose(1, 0, 2, 3)

    def one_block(pieces):
        return attend_block(pieces[0], pieces[1], key_heads, value_heads, documents, mix_pre, mix_post)
    outcomes = lax.map(jax.checkpoint(one_block), (starts, query_blocks))
    attended = low(low_back(outcomes.transpose(0, 2, 1, 3).reshape(ROW_LEN, D)))
    middle = row_in + low_back(matmul(attended, w_attn_out))
    normed_two = low(rms_norm(middle, gain_two))
    hidden = low_back(matmul(normed_two, w_ff_in))
    active = low(jax.nn.gelu(hidden))
    return middle + low_back(matmul(active, w_ff_out))

def reference(inputs, doc_lengths, norm1_gain, w_query, w_key, w_value, head_mix_pre, head_mix_post, w_attn_out, norm2_gain, w_ff_in, w_ff_out, out_cotangent):
    params = tuple((array_in.astype(jnp.float32) for array_in in (norm1_gain, w_query, w_key, w_value, head_mix_pre, head_mix_post, w_attn_out, norm2_gain, w_ff_in, w_ff_out)))

    def one_row(totals, pieces):
        row_in, lengths, cotangent = pieces

        def whole_layer(row_value, gain_one, query_w, key_w, value_w, mix_pre, mix_post, attn_w, gain_two, ff_in_w, ff_out_w):
            return row_layer(row_value, lengths, gain_one, query_w, key_w, value_w, mix_pre, mix_post, attn_w, gain_two, ff_in_w, ff_out_w)
        result, pullback = jax.vjp(whole_layer, row_in.astype(jnp.float32), params[0], params[1], params[2], params[3], params[4], params[5], params[6], params[7], params[8], params[9])
        gradients = pullback(cotangent.astype(jnp.float32))
        totals = tuple((running + addend for running, addend in zip(totals, gradients[1:])))
        return (totals, (result.astype(jnp.bfloat16), gradients[0].astype(jnp.bfloat16)))
    initial = tuple((jnp.zeros_like(array_in) for array_in in params))
    totals, (outputs, input_grads) = lax.scan(one_row, initial, (inputs, doc_lengths, out_cotangent))
    return (outputs, input_grads, totals[0], totals[1], totals[2], totals[3], totals[4], totals[5], totals[6], totals[7], totals[8], totals[9])
```

```python
import functools

import jax
import jax.numpy as jnp
from jax import lax
from jax.experimental import pallas as pl
from jax.experimental.pallas import tpu as pltpu
from jax.sharding import PartitionSpec as P

F32 = jnp.float32
BF16 = jnp.bfloat16
EPSILON = 1e-06
MASKED = -1e30
PER = 6


def dot(a, b):
    return jnp.dot(a, b, preferred_element_type=F32)


def fwd_kernel(tile, heads, per, tasks_row, info, place, pre, post, q_ref, k_ref, v_ref,
               att_ref, u_ref, inv_ref, p_out, qa, vt, s_all, u_acc, att_acc, top, mass, p_buf, sems):
    task, part = pl.program_id(0), pl.program_id(1)
    parts = heads // per
    width = q_ref.shape[2]
    size = width // heads
    first, count = info[task, 0], info[task, 1]
    row_len = k_ref.shape[1]

    @pl.when((task % tasks_row == 0) & (part == 0))
    def _():
        for c in range(row_len // tile):
            vt[:, c * tile:(c + 1) * tile] = v_ref[0, c * tile:(c + 1) * tile, :].T

    qt = q_ref[0].astype(F32).T
    for g in range(per):
        for h in range(heads):
            rows = slice(h * size, (h + 1) * size)
            qa[rows, g * tile:(g + 1) * tile] = (qt[rows] * (pre[h, part * per + g] * size ** -0.5)).astype(BF16)

    def cols(g):
        return slice(g * tile, (g + 1) * tile)

    def keys(j):
        return pl.ds(pl.multiple_of(place[first + j] * tile, tile), tile)

    last = count - 1
    causal = lax.broadcasted_iota(jnp.int32, (tile, tile), 0) <= lax.broadcasted_iota(jnp.int32, (tile, tile), 1)
    kj = k_ref[0, keys(last), :]
    for g in range(per):
        s = jnp.where(causal, dot(kj, qa[:, cols(g)]), MASKED)
        s_all[last, :, cols(g)] = s
        top[:, cols(g)] = jnp.max(s, axis=0, keepdims=True)

    def scores(j, carry):
        kj = k_ref[0, keys(j), :]
        for g in range(per):
            s = dot(kj, qa[:, cols(g)])
            s_all[j, :, cols(g)] = s
            top[:, cols(g)] = jnp.maximum(top[:, cols(g)], jnp.max(s, axis=0, keepdims=True))
        return carry

    lax.fori_loop(0, last, scores, 0)
    u_acc[...] = jnp.zeros_like(u_acc)
    mass[...] = jnp.zeros_like(mass)

    def copy(j, slot):
        return pltpu.make_async_copy(p_buf.at[slot], p_out.at[task, part, j], sems.at[slot])

    def sums(j, carry):
        slot = j % 2

        @pl.when(j >= 2)
        def _():
            copy(j, slot).wait()
        vj = vt[:, keys(j)]
        for g in range(per):
            p = jnp.exp(s_all[j, :, cols(g)] - top[:, cols(g)])
            mass[:, cols(g)] += jnp.sum(p, axis=0, keepdims=True)
            low = p.astype(BF16)
            p_buf[slot, :, cols(g)] = low
            u_acc[:, cols(g)] += dot(vj, low)
        copy(j, slot).start()
        return carry

    lax.fori_loop(0, count, sums, 0)

    inv = 1.0 / mass[...]
    inv_ref[0, 0] = inv
    u_ref[0, 0] = u_acc[...].astype(BF16)
    for h in range(heads):
        rows = slice(h * size, (h + 1) * size)
        acc = None
        for g in range(per):
            term = u_acc[rows, cols(g)] * (inv[:, cols(g)] * post[part * per + g, h])
            acc = term if acc is None else acc + term
        att_acc[rows] = jnp.where(part == 0, acc, acc + att_acc[rows])

    @pl.when(part == parts - 1)
    def _():
        att_ref[0] = att_acc[...].T.astype(BF16)

    @pl.when(count >= 2)
    def _():
        copy(0, count % 2).wait()
    copy(0, (count - 1) % 2).wait()


def fwd(info, place, pre, post, q, k, v, tile, per):
    tasks, _, width = q.shape
    rows, row_len, _ = k.shape
    heads = pre.shape[0]
    parts = heads // per
    tiles = row_len // tile
    wide = per * tile
    tasks_row = tasks // rows
    smem = pl.BlockSpec(memory_space=pltpu.SMEM)
    return pl.pallas_call(
        functools.partial(fwd_kernel, tile, heads, per, tasks_row),
        grid=(tasks, parts),
        in_specs=[
            smem, smem, smem, smem,
            pl.BlockSpec((1, tile, width), lambda t, p: (t, 0, 0)),
            pl.BlockSpec((1, row_len, width), lambda t, p: (t // tasks_row, 0, 0)),
            pl.BlockSpec((1, row_len, width), lambda t, p: (t // tasks_row, 0, 0)),
        ],
        out_specs=[
            pl.BlockSpec((1, tile, width), lambda t, p: (t, 0, 0)),
            pl.BlockSpec((1, 1, width, wide), lambda t, p: (t, p, 0, 0)),
            pl.BlockSpec((1, 1, 1, wide), lambda t, p: (t, p, 0, 0)),
            pl.BlockSpec(memory_space=pl.ANY),
        ],
        out_shape=[
            jax.ShapeDtypeStruct((tasks, tile, width), BF16),
            jax.ShapeDtypeStruct((tasks, parts, width, wide), BF16),
            jax.ShapeDtypeStruct((tasks, parts, 1, wide), F32),
            jax.ShapeDtypeStruct((tasks, parts, tiles, tile, wide), BF16),
        ],
        scratch_shapes=[
            pltpu.VMEM((width, wide), BF16),
            pltpu.VMEM((width, row_len), BF16),
            pltpu.VMEM((tiles, tile, wide), F32),
            pltpu.VMEM((width, wide), F32),
            pltpu.VMEM((width, tile), F32),
            pltpu.VMEM((1, wide), F32),
            pltpu.VMEM((1, wide), F32),
            pltpu.VMEM((2, tile, wide), BF16),
            pltpu.SemaphoreType.DMA((2,)),
        ],
        compiler_params=pltpu.CompilerParams(vmem_limit_bytes=60 * 2 ** 20),
        name="attention_forward",
    )(info, place, pre, post, q, k, v)


def bwd_kernel(tile, heads, per, tasks_row, info, place, pre, post, q_ref, da_ref, k_ref, v_ref, u_ref, inv_ref, pre_wide, post_wide, p_in,
               dq_ref, dk_ref, dv_ref, gpre_ref, gpost_ref,
               kt, qb, daa, dab, w_acc, dq_acc, dk_acc, dv_acc, delta, dm_all, p_buf, sems):
    task, part = pl.program_id(0), pl.program_id(1)
    parts = heads // per
    width = q_ref.shape[2]
    size = width // heads
    first, count = info[task, 0], info[task, 1]
    row_len = k_ref.shape[1]

    def cols(g):
        return slice(g * tile, (g + 1) * tile)

    def keys(j):
        return pl.ds(pl.multiple_of(place[first + j] * tile, tile), tile)

    def copy(j, slot):
        return pltpu.make_async_copy(p_in.at[task, part, j], p_buf.at[slot], sems.at[slot])

    copy(0, 0).start()

    @pl.when((task % tasks_row == 0) & (part == 0))
    def _():
        for c in range(row_len // tile):
            kt[:, c * tile:(c + 1) * tile] = k_ref[0, c * tile:(c + 1) * tile, :].T
        dk_acc[...] = jnp.zeros_like(dk_acc)
        dv_acc[...] = jnp.zeros_like(dv_acc)

    @pl.when((task == 0) & (part == 0))
    def _():
        gpre_ref[...] = jnp.zeros_like(gpre_ref)
        gpost_ref[...] = jnp.zeros_like(gpost_ref)

    w_acc[...] = jnp.zeros_like(w_acc)
    qf = q_ref[0].astype(F32)
    daf = da_ref[0].astype(F32)
    qt = qf.T
    dat = daf.T
    inv = inv_ref[0, 0]
    for g in range(per):
        qb[cols(g), :] = (qf * pre_wide[0, g:g + 1, :]).astype(BF16)
        inv_g = inv[:, cols(g)]
        d_g = None
        for h in range(heads):
            rows = slice(h * size, (h + 1) * size)
            scaled = dat[rows] * inv_g
            weight = post[part * per + g, h]
            daa[rows, cols(g)] = (scaled * weight).astype(BF16)
            e = jnp.sum(scaled * u_ref[0, 0, rows, cols(g)].astype(F32), axis=0, keepdims=True)
            gpost_ref[part, g, h:h + 1, :] += e
            d_g = e * weight if d_g is None else d_g + e * weight
        delta[:, cols(g)] = d_g * inv_g
        dab[cols(g), :] = daa[:, cols(g)].astype(F32).T.astype(BF16)

    def step(j, carry):
        slot = j % 2
        copy(j, slot).wait()

        @pl.when(j + 1 < count)
        def _():
            copy(j + 1, 1 - slot).start()
        vj = v_ref[0, keys(j), :]
        ktj = kt[:, keys(j)]
        for g in range(per):
            dp = dot(vj, daa[:, cols(g)])
            dm = (p_buf[slot, :, cols(g)].astype(F32) * (dp - delta[:, cols(g)])).astype(BF16)
            dm_all[:, cols(g)] = dm
            w_acc[:, cols(g)] += dot(ktj, dm)
        dv_acc[keys(j), :] += dot(p_buf[slot], dab[...])
        dk_acc[keys(j), :] += dot(dm_all[...], qb[...])
        return carry

    lax.fori_loop(0, count, step, 0)

    for h in range(heads):
        rows = slice(h * size, (h + 1) * size)
        acc = None
        for g in range(per):
            w = w_acc[rows, cols(g)]
            term = w * (pre[h, part * per + g] * size ** -0.5)
            acc = term if acc is None else acc + term
            gpre_ref[part, g, h:h + 1, :] += jnp.sum(w * qt[rows], axis=0, keepdims=True) * size ** -0.5
        dq_acc[rows] = jnp.where(part == 0, acc, acc + dq_acc[rows])

    @pl.when(part == parts - 1)
    def _():
        dq_ref[0] = dq_acc[...].T.astype(BF16)

    @pl.when((task % tasks_row == tasks_row - 1) & (part == parts - 1))
    def _():
        dk_ref[0] = dk_acc[...].astype(BF16)
        dv_ref[0] = dv_acc[...].astype(BF16)


def bwd(info, place, pre, post, q, da, k, v, u, inv, p, tile, per):
    tasks, _, width = q.shape
    rows, row_len, _ = k.shape
    heads = pre.shape[0]
    parts = heads // per
    tiles = row_len // tile
    wide = per * tile
    tasks_row = tasks // rows
    size = width // heads
    pre_wide = jnp.repeat(pre.T * size ** -0.5, size, axis=1).reshape(parts, per, width)
    post_wide = jnp.repeat(post, size, axis=1).reshape(parts, per, width)
    smem = pl.BlockSpec(memory_space=pltpu.SMEM)
    once = pl.Buffered(1)
    row_spec = pl.BlockSpec((1, row_len, width), lambda t, p: (t // tasks_row, 0, 0))
    out = pl.pallas_call(
        functools.partial(bwd_kernel, tile, heads, per, tasks_row),
        grid=(tasks, parts),
        in_specs=[
            smem, smem, smem, smem,
            pl.BlockSpec((1, tile, width), lambda t, p: (t, 0, 0)),
            pl.BlockSpec((1, tile, width), lambda t, p: (t, 0, 0)),
            pl.BlockSpec((1, row_len, width), lambda t, p: (t // tasks_row, 0, 0), pipeline_mode=once),
            pl.BlockSpec((1, row_len, width), lambda t, p: (t // tasks_row, 0, 0), pipeline_mode=once),
            pl.BlockSpec((1, 1, width, wide), lambda t, p: (t, p, 0, 0)),
            pl.BlockSpec((1, 1, 1, wide), lambda t, p: (t, p, 0, 0)),
            pl.BlockSpec((1, per, width), lambda t, p: (p, 0, 0)),
            pl.BlockSpec((1, per, width), lambda t, p: (p, 0, 0)),
            pl.BlockSpec(memory_space=pl.ANY),
        ],
        out_specs=[
            pl.BlockSpec((1, tile, width), lambda t, p: (t, 0, 0)),
            row_spec, row_spec,
            pl.BlockSpec((parts, per, heads, tile), lambda t, p: (0, 0, 0, 0)),
            pl.BlockSpec((parts, per, heads, tile), lambda t, p: (0, 0, 0, 0)),
        ],
        out_shape=[
            jax.ShapeDtypeStruct((tasks, tile, width), BF16),
            jax.ShapeDtypeStruct((rows, row_len, width), BF16),
            jax.ShapeDtypeStruct((rows, row_len, width), BF16),
            jax.ShapeDtypeStruct((parts, per, heads, tile), F32),
            jax.ShapeDtypeStruct((parts, per, heads, tile), F32),
        ],
        scratch_shapes=[
            pltpu.VMEM((width, row_len), BF16),
            pltpu.VMEM((wide, width), BF16),
            pltpu.VMEM((width, wide), BF16),
            pltpu.VMEM((wide, width), BF16),
            pltpu.VMEM((width, wide), F32),
            pltpu.VMEM((width, tile), F32),
            pltpu.VMEM((row_len, width), F32),
            pltpu.VMEM((row_len, width), F32),
            pltpu.VMEM((1, wide), F32),
            pltpu.VMEM((tile, wide), BF16),
            pltpu.VMEM((2, tile, wide), BF16),
            pltpu.SemaphoreType.DMA((2,)),
        ],
        compiler_params=pltpu.CompilerParams(vmem_limit_bytes=62 * 2 ** 20),
        name="attention_backward",
    )(info, place, pre, post, q, da, k, v, u, inv, pre_wide, post_wide, p)
    dq, dk, dv, gpre, gpost = out
    return dq, dk, dv, jnp.sum(gpre, axis=3).reshape(heads, heads).T, jnp.sum(gpost, axis=3).reshape(heads, heads)


def inverse_rms(values):
    return lax.rsqrt(jnp.mean(values * values, axis=-1, keepdims=True) + EPSILON)


def transposed_dot(a, b):
    return lax.dot_general(a, b, (((0,), (0,)), ((), ())), preferred_element_type=F32)


def dot_transposed(a, b):
    return lax.dot_general(a, b, (((1,), (1,)), ((), ())), preferred_element_type=F32)


def swap(value, axis, bit):
    return lax.ppermute(value, axis, [(i, i ^ bit) for i in range(lax.axis_size(axis))])


def bits_down(size):
    bit = size // 2
    while bit:
        yield bit
        bit //= 2


def gather_blocks(block, axis):
    masks, held = [0], block[None]
    for bit in bits_down(lax.axis_size(axis)):
        held = jnp.concatenate((held, swap(held, axis, bit)), axis=0)
        masks = masks + [m ^ bit for m in masks]
    return held, masks


def scatter_blocks(parts, masks, axis):
    held = {m: parts[i] for i, m in enumerate(masks)}
    for bit in reversed(list(bits_down(lax.axis_size(axis)))):
        away = sorted(m for m in held if m & bit)
        sent = jnp.stack([held[m].astype(BF16) for m in away])
        came = swap(sent, axis, bit)
        held = {m: v for m, v in held.items() if not m & bit}
        for i, m in enumerate(away):
            held[m ^ bit] = held[m ^ bit].astype(F32) + came[i].astype(F32)
    return held[0]


def scatter_grad(grad):
    groups, circle = lax.axis_size("dp"), lax.axis_size("blk")
    rows = grad.shape[0] // (groups * circle)
    held = grad.reshape(groups, circle, rows, -1)
    own = lax.axis_index("blk")
    bit = 1
    while bit < circle:
        halves = held.reshape(groups, circle // (2 * bit), 2, rows, -1)
        side = (own // bit) % 2
        kept = lax.dynamic_index_in_dim(halves, side, 2, keepdims=False)
        sent = lax.dynamic_index_in_dim(halves, 1 - side, 2, keepdims=False).astype(BF16)
        held = kept.astype(F32) + swap(sent, "blk", bit).astype(F32)
        bit *= 2
    held = held.reshape(groups, rows, -1)
    mine = lax.axis_index("dp")
    total = lax.dynamic_index_in_dim(held, mine, 0, keepdims=False)
    for step in range(1, groups):
        sent = lax.dynamic_index_in_dim(held, mine ^ step, 0, keepdims=False).astype(BF16)
        total = total + swap(sent, "dp", step).astype(F32)
    return total.reshape((rows,) + grad.shape[1:])


class Plan:
    def __init__(self, rows, span, circle):
        self.tile = min(256, span)
        self.rows, self.circle = rows, circle
        self.slots = span // self.tile
        self.tiles = self.slots * circle
        self.groups = {}
        for r in range(rows):
            for c in range(self.slots):
                route = tuple((b, self.worker(r, b * self.slots + c)) for b in range(circle))
                self.groups.setdefault(route, []).append((r, c))

    def worker(self, r, tile):
        lap, place = divmod(tile, self.circle)
        return place if (lap + r * (self.slots % 2)) % 2 == 0 else self.circle - 1 - place

    def table(self):
        found = [[[0] * self.circle for _ in range(self.slots)] for _ in range(self.rows)]
        for route, places in self.groups.items():
            for r, c in places:
                for b, d in route:
                    found[r][c][d] = b * self.slots + c
        return found

    def move(self, block, back=False):
        shape = block.shape
        cut = block.reshape((self.rows * self.slots, self.tile) + shape[2:])
        out = [None] * (self.rows * self.slots)
        for route, places in self.groups.items():
            at = [r * self.slots + c for r, c in places]
            piece = cut[jnp.array(at)] if len(at) < cut.shape[0] else cut
            pairs = [(d, b) for b, d in route] if back else list(route)
            if any(b != d for b, d in pairs):
                piece = lax.ppermute(piece, "blk", pairs)
            for i, a in enumerate(at):
                out[a] = piece[i]
        return jnp.stack(out)


def shards(
    inputs,
    doc_lengths,
    norm1_gain,
    w_query,
    w_key,
    w_value,
    head_mix_pre,
    head_mix_post,
    w_attn_out,
    norm2_gain,
    w_ff_in,
    w_ff_out,
    out_cotangent,
):
    rows, span, width = inputs.shape
    circle = lax.axis_size("blk")
    own = lax.axis_index("blk")
    plan = Plan(rows, span, circle)
    tile, slots, tiles = plan.tile, plan.slots, plan.tiles
    tasks = rows * slots
    row_len = span * circle

    gathered, masks = gather_blocks(inputs, "blk")
    cotangent = plan.move(out_cotangent).reshape(tasks * tile, width)

    place_of = [0] * circle
    for p, m in enumerate(masks):
        place_of[m] = p
    place_of = jnp.array(place_of, jnp.int32)
    key_place = place_of[jnp.arange(tiles, dtype=jnp.int32) // slots ^ own] * slots + jnp.arange(tiles, dtype=jnp.int32) % slots
    work = jnp.array(plan.table(), jnp.int32)[:, :, own]
    bounds = jnp.cumsum(doc_lengths, axis=1)
    begin = jnp.max(jnp.where(bounds[:, None, :] <= work[:, :, None] * tile, bounds[:, None, :], 0), axis=2) // tile
    info = jnp.stack((begin, work - begin + 1), axis=2).reshape(tasks, 2).astype(jnp.int32)
    places = key_place[work]

    x_all = gathered.transpose(1, 0, 2, 3).reshape(rows * row_len, width).astype(F32)
    scale_all = inverse_rms(x_all)
    normed_all = (x_all * scale_all * norm1_gain).astype(BF16)
    keys = jnp.dot(normed_all, w_key, preferred_element_type=F32).astype(BF16).reshape(rows, row_len, width)
    values = jnp.dot(normed_all, w_value, preferred_element_type=F32).astype(BF16).reshape(rows, row_len, width)

    def of_tasks(array):
        cut = array.reshape(rows, tiles, tile, width)
        picked = [lax.dynamic_index_in_dim(cut[r], places[r, c], 0, keepdims=False) for r in range(rows) for c in range(slots)]
        return jnp.concatenate(picked, axis=0)

    normed_own = of_tasks(normed_all)
    x_own = of_tasks(gathered.transpose(1, 0, 2, 3)).astype(F32)
    queries = jnp.dot(normed_own, w_query, preferred_element_type=F32).astype(BF16).reshape(tasks, tile, width)

    attended, sums, inverse, probs = fwd(info, key_place, head_mix_pre, head_mix_post, queries, keys, values, tile, PER)
    attended = attended.reshape(tasks * tile, width)

    middle = x_own + jnp.dot(attended, w_attn_out, preferred_element_type=F32)
    scale_two = inverse_rms(middle)
    normed_two = (middle * scale_two * norm2_gain).astype(BF16)
    hidden = jnp.dot(normed_two, w_ff_in, preferred_element_type=F32)
    active, pull_gelu = jax.vjp(jax.nn.gelu, hidden)
    active = active.astype(BF16)
    output = (middle + jnp.dot(active, w_ff_out, preferred_element_type=F32)).astype(BF16)
    output = plan.move(output.reshape(rows, span, width), back=True).reshape(rows, span, width)
    grad_ff_out = transposed_dot(active, cotangent)
    d_hidden = pull_gelu(dot_transposed(cotangent, w_ff_out))[0].astype(BF16)
    grad_ff_in = transposed_dot(normed_two, d_hidden)
    d_normed_two = dot_transposed(d_hidden, w_ff_in)
    grad_gain_two = jnp.sum(d_normed_two * middle * scale_two, axis=0)
    z = norm2_gain * d_normed_two
    d_middle = cotangent.astype(F32) + scale_two * z - middle * scale_two ** 3 * jnp.mean(z * middle, axis=1, keepdims=True)
    d_branch = d_middle.astype(BF16)
    grad_attn_out = transposed_dot(attended, d_branch)
    d_attended = dot_transposed(d_branch, w_attn_out).astype(BF16).reshape(tasks, tile, width)

    d_queries, d_keys, d_values, grad_pre, grad_post = bwd(
        info, key_place, head_mix_pre, head_mix_post, queries, d_attended, keys, values, sums, inverse, probs, tile, PER
    )
    d_queries = d_queries.reshape(tasks * tile, width)
    d_keys = d_keys.reshape(rows * row_len, width)
    d_values = d_values.reshape(rows * row_len, width)
    grad_query = transposed_dot(normed_own, d_queries)
    grad_key = transposed_dot(normed_all, d_keys)
    grad_value = transposed_dot(normed_all, d_values)

    def norm_one_back(d_normed, x):
        scale = inverse_rms(x)
        y = norm1_gain * d_normed
        gain = jnp.sum(d_normed * x * scale, axis=0)
        return scale * y - x * scale ** 3 * jnp.mean(y * x, axis=1, keepdims=True), gain

    d_all, gain_all = norm_one_back(dot_transposed(d_keys, w_key) + dot_transposed(d_values, w_value), x_all)
    d_own, gain_own = norm_one_back(dot_transposed(d_queries, w_query), x_own)
    d_own = (d_own + d_middle).reshape(tasks, tile, width)
    d_all = d_all.reshape(rows, tiles, tile, width)
    for r in range(rows):
        for c in range(slots):
            at = (r, places[r, c], 0, 0)
            d_all = lax.dynamic_update_slice(d_all, lax.dynamic_slice(d_all, at, (1, 1, tile, width)) + d_own[r * slots + c][None, None], at)
    d_all = d_all.reshape(rows, circle, span, width).transpose(1, 0, 2, 3)
    input_grad = scatter_blocks(d_all, masks, "blk").astype(BF16)

    small = lax.psum((gain_all + gain_own, grad_gain_two, grad_pre, grad_post), ("dp", "blk"))
    index = lax.axis_index("dp") * circle + own
    share = width // (lax.axis_size("dp") * circle)

    def part(gain):
        return lax.dynamic_slice_in_dim(gain, index * share, share)

    return (
        output,
        input_grad,
        part(small[0]),
        scatter_grad(grad_query),
        scatter_grad(grad_key),
        scatter_grad(grad_value),
        small[2],
        small[3],
        scatter_grad(grad_attn_out),
        part(small[1]),
        scatter_grad(grad_ff_in),
        scatter_grad(grad_ff_out),
    )


def solution(mesh):
    tokens = P("dp", "blk", None)
    split = P(("dp", "blk"), None)
    in_specs = (tokens, P("dp", None)) + (P(),) * 10 + (tokens,)
    out_specs = (tokens, tokens, P(("dp", "blk")), split, split, split, P(), P(), split, P(("dp", "blk")), split, split)
    return jax.shard_map(shards, mesh=mesh, in_specs=in_specs, out_specs=out_specs, check_vma=False)
```

```python
import functools

import jax
import jax.numpy as jnp
from jax import lax
from jax.experimental import pallas as pl
from jax.experimental.pallas import tpu as pltpu
from jax.sharding import PartitionSpec as P

F32 = jnp.float32
BF16 = jnp.bfloat16
EPSILON = 1e-06
MASKED = -1e30
PER = 6
MIB = 2 ** 20
ONCE = pl.Buffered(1)
SMEM = pl.BlockSpec(memory_space=pltpu.SMEM)
ANY = pl.BlockSpec(memory_space=pl.ANY)


def dot(a, b):
    return jnp.dot(a, b, preferred_element_type=F32)


def dot_t(a, b):
    return lax.dot_general(a, b, (((1,), (1,)), ((), ())), preferred_element_type=F32)


def t_dot(a, b):
    return lax.dot_general(a, b, (((0,), (0,)), ((), ())), preferred_element_type=F32)


def inverse_rms(values):
    return lax.rsqrt(jnp.mean(values * values, axis=-1, keepdims=True) + EPSILON)


def forward_kernel(tile, heads, per, slots, count_pieces, info, place, pre, post, gain, w_q, w_k, w_v, *refs):
    pieces = refs[:count_pieces]
    (att_ref, u_ref, inv_ref, q_ref, own_ref, p_out, v_out, kt_out, x_out,
     x_s, k_s, v_s, kt_s, vt_s, qa, s_all, u_acc, att_acc, top, mass, p_buf, sems, row_sems) = refs[count_pieces:]
    task, part = pl.program_id(0), pl.program_id(1)
    row = task // slots
    parts = heads // per
    width = q_ref.shape[2]
    size = width // heads
    first, count, spot = info[task, 0], info[task, 1], info[task, 2]
    span = pieces[0].shape[1]

    def row_copies():
        return (
            pltpu.make_async_copy(v_s, v_out.at[row], row_sems.at[0]),
            pltpu.make_async_copy(kt_s, kt_out.at[row], row_sems.at[1]),
            pltpu.make_async_copy(x_s, x_out.at[row], row_sems.at[2]),
        )

    @pl.when((task % slots == 0) & (part == 0))
    def _():
        for i, piece in enumerate(pieces):
            for c in range(span // tile):
                at = slice(i * span + c * tile, i * span + (c + 1) * tile)
                low = piece[0, c * tile:(c + 1) * tile, :]
                x_s[at, :] = low
                x = low.astype(F32)
                normed = (x * inverse_rms(x) * gain[...]).astype(BF16)
                k = dot(normed, w_k[...]).astype(BF16)
                k_s[at, :] = k
                kt_s[:, at] = k.T
                v = dot(normed, w_v[...]).astype(BF16)
                v_s[at, :] = v
                vt_s[:, at] = v.T
        for c in row_copies():
            c.start()

    @pl.when(part == 0)
    def _():
        low = x_s[pl.ds(pl.multiple_of(spot * tile, tile), tile), :]
        own_ref[0] = low
        x = low.astype(F32)
        normed = (x * inverse_rms(x) * gain[...]).astype(BF16)
        q_ref[0] = dot(normed, w_q[...]).astype(BF16)

    qt = q_ref[0].astype(F32).T
    for g in range(per):
        for h in range(heads):
            rows = slice(h * size, (h + 1) * size)
            qa[rows, g * tile:(g + 1) * tile] = (qt[rows] * (pre[h, part * per + g] * size ** -0.5)).astype(BF16)

    def cols(g):
        return slice(g * tile, (g + 1) * tile)

    def keys(j):
        return pl.ds(pl.multiple_of(place[first + j] * tile, tile), tile)

    last = count - 1
    causal = lax.broadcasted_iota(jnp.int32, (tile, tile), 0) <= lax.broadcasted_iota(jnp.int32, (tile, tile), 1)
    kj = k_s[keys(last), :]
    for g in range(per):
        s = jnp.where(causal, dot(kj, qa[:, cols(g)]), MASKED)
        s_all[last, :, cols(g)] = s
        top[:, cols(g)] = jnp.max(s, axis=0, keepdims=True)

    def scores(j, carry):
        kj = k_s[keys(j), :]
        for g in range(per):
            s = dot(kj, qa[:, cols(g)])
            s_all[j, :, cols(g)] = s
            top[:, cols(g)] = jnp.maximum(top[:, cols(g)], jnp.max(s, axis=0, keepdims=True))
        return carry

    lax.fori_loop(0, last, scores, 0)
    u_acc[...] = jnp.zeros_like(u_acc)
    mass[...] = jnp.zeros_like(mass)

    def copy(j, slot):
        return pltpu.make_async_copy(p_buf.at[slot], p_out.at[task, part, j], sems.at[slot])

    def sums(j, carry):
        slot = j % 2

        @pl.when(j >= 2)
        def _():
            copy(j, slot).wait()
        vj = vt_s[:, keys(j)]
        for g in range(per):
            p = jnp.exp(s_all[j, :, cols(g)] - top[:, cols(g)])
            mass[:, cols(g)] += jnp.sum(p, axis=0, keepdims=True)
            low = p.astype(BF16)
            p_buf[slot, :, cols(g)] = low
            u_acc[:, cols(g)] += dot(vj, low)
        copy(j, slot).start()
        return carry

    lax.fori_loop(0, count, sums, 0)

    inv = 1.0 / mass[...]
    inv_ref[0, 0] = inv
    u_ref[0, 0] = u_acc[...].astype(BF16)
    for h in range(heads):
        rows = slice(h * size, (h + 1) * size)
        acc = None
        for g in range(per):
            term = u_acc[rows, cols(g)] * (inv[:, cols(g)] * post[part * per + g, h])
            acc = term if acc is None else acc + term
        att_acc[rows] = jnp.where(part == 0, acc, acc + att_acc[rows])

    @pl.when(part == parts - 1)
    def _():
        att_ref[0] = att_acc[...].T.astype(BF16)

    @pl.when(count >= 2)
    def _():
        copy(0, count % 2).wait()
    copy(0, (count - 1) % 2).wait()

    @pl.when((task % slots == slots - 1) & (part == parts - 1))
    def _():
        for c in row_copies():
            c.wait()


def forward(info, place, pre, post, gain, w_q, w_k, w_v, pieces, tile):
    rows, span, width = pieces[0].shape
    row_len = span * len(pieces)
    heads = pre.shape[0]
    parts = heads // PER
    wide = PER * tile
    slots = span // tile
    tasks = rows * slots
    tiles = row_len // tile
    whole = pl.BlockSpec((width, width), lambda t, p: (0, 0), pipeline_mode=ONCE)
    task_spec = pl.BlockSpec((1, tile, width), lambda t, p: (t, 0, 0))
    pairs = tasks * tiles // 2
    return pl.pallas_call(
        functools.partial(forward_kernel, tile, heads, PER, slots, len(pieces)),
        grid=(tasks, parts),
        in_specs=[SMEM] * 4
        + [pl.BlockSpec((1, width), lambda t, p: (0, 0)), whole, whole, whole]
        + [pl.BlockSpec((1, span, width), lambda t, p: (t // slots, 0, 0), pipeline_mode=ONCE)] * len(pieces),
        out_specs=[
            task_spec,
            pl.BlockSpec((1, 1, width, wide), lambda t, p: (t, p, 0, 0)),
            pl.BlockSpec((1, 1, 1, wide), lambda t, p: (t, p, 0, 0)),
            task_spec, task_spec, ANY, ANY, ANY, ANY,
        ],
        out_shape=[
            jax.ShapeDtypeStruct((tasks, tile, width), BF16),
            jax.ShapeDtypeStruct((tasks, parts, width, wide), BF16),
            jax.ShapeDtypeStruct((tasks, parts, 1, wide), F32),
            jax.ShapeDtypeStruct((tasks, tile, width), BF16),
            jax.ShapeDtypeStruct((tasks, tile, width), BF16),
            jax.ShapeDtypeStruct((tasks, parts, tiles, tile, wide), BF16),
            jax.ShapeDtypeStruct((rows, row_len, width), BF16),
            jax.ShapeDtypeStruct((rows, width, row_len), BF16),
            jax.ShapeDtypeStruct((rows, row_len, width), BF16),
        ],
        scratch_shapes=[
            pltpu.VMEM((row_len, width), BF16),
            pltpu.VMEM((row_len, width), BF16),
            pltpu.VMEM((row_len, width), BF16),
            pltpu.VMEM((width, row_len), BF16),
            pltpu.VMEM((width, row_len), BF16),
            pltpu.VMEM((width, wide), BF16),
            pltpu.VMEM((tiles, tile, wide), F32),
            pltpu.VMEM((width, wide), F32),
            pltpu.VMEM((width, tile), F32),
            pltpu.VMEM((1, wide), F32),
            pltpu.VMEM((1, wide), F32),
            pltpu.VMEM((2, tile, wide), BF16),
            pltpu.SemaphoreType.DMA((2,)),
            pltpu.SemaphoreType.DMA((3,)),
        ],
        compiler_params=pltpu.CompilerParams(vmem_limit_bytes=60 * MIB),
        cost_estimate=pl.CostEstimate(flops=pairs * 4 * heads * width * tile * tile // 10, bytes_accessed=4 * MIB, transcendentals=0),
        name="attention_forward",
    )(info, place, pre, post, gain, w_q, w_k, w_v, *pieces)


def feed_forward_kernel(waves, step_tokens, gain, w_out, w_in_ref, w_back_ref, *refs):
    own, att, cot = refs[:waves], refs[waves:2 * waves], refs[2 * waves:3 * waves]
    (out_ref, d_att_ref, d_mid_ref, g_in_ref, g_back_ref, g_gain_ref,
     mid, n_two, n_two_t, cot_s, out_acc, d_acc, act_s, dh_s) = refs[3 * waves:]
    step, steps = pl.program_id(0), pl.num_programs(0)
    tokens, width = mid.shape
    each = tokens // waves

    @pl.when(step == 0)
    def _():
        for w in range(waves):
            for b in range(0, each, step_tokens):
                at, to = slice(b, b + step_tokens), slice(w * each + b, w * each + b + step_tokens)
                m = own[w][at, :].astype(F32) + dot(att[w][at, :], w_out[...])
                mid[to, :] = m
                n = (m * inverse_rms(m) * gain[...]).astype(BF16)
                n_two[to, :] = n
                n_two_t[:, to] = n.T
                cot_s[to, :] = cot[w][at, :]
        out_acc[...] = jnp.zeros_like(out_acc)
        d_acc[...] = jnp.zeros_like(d_acc)

    root = (2.0 / 3.141592653589793) ** 0.5

    @pl.when(step < steps - 1)
    def _():
        w_in, w_back = w_in_ref[...], w_back_ref[...]
        for b in range(0, tokens, step_tokens):
            at = slice(b, b + step_tokens)
            v = dot(n_two[at, :], w_in)
            d_active = dot_t(cot_s[at, :], w_back)
            square = v * v
            t = jnp.tanh(root * v * (1.0 + 0.044715 * square))
            half = 0.5 + 0.5 * t
            act = (v * half).astype(BF16)
            slope = half + (0.5 * root) * v * (1.0 - t * t) * (1.0 + (3 * 0.044715) * square)
            d_hidden = (slope * d_active).astype(BF16)
            act_s[at, :] = act
            dh_s[at, :] = d_hidden
            out_acc[at, :] += dot(act, w_back)
            d_acc[at, :] += dot_t(d_hidden, w_in)
        g_back_ref[...] = t_dot(act_s[...], cot_s[...]).astype(BF16)
        g_in_ref[...] = dot(n_two_t[...], dh_s[...]).astype(BF16)

    @pl.when(step == steps - 1)
    def _():
        total, grad_gain = None, None
        for w in range(waves):
            for b in range(0, each, step_tokens):
                at, to = slice(b, b + step_tokens), slice(w * each + b, w * each + b + step_tokens)
                m = mid[to, :]
                out_ref[to, :] = (m + out_acc[to, :]).astype(BF16)
                d = d_acc[to, :]
                r = inverse_rms(m)
                part = jnp.sum(d * m * r, axis=0, keepdims=True)
                grad_gain = part if grad_gain is None else grad_gain + part
                z = gain[...] * d
                d_mid = cot_s[to, :].astype(F32) + r * z - m * (r * r * r * jnp.mean(z * m, axis=1, keepdims=True))
                d_mid_ref[to, :] = d_mid
                branch = d_mid.astype(BF16)
                d_att_ref[to, :] = dot_t(branch, w_out[...]).astype(BF16)
                part = t_dot(att[w][at, :], branch)
                total = part if total is None else total + part
        g_in_ref[...] = total.astype(BF16)
        g_gain_ref[...] = grad_gain


def feed_forward(gain, w_out, w_in, w_back, own, att, cot, step_tokens=256):
    waves = len(own)
    each, width = own[0].shape
    tokens = waves * each
    inner = w_in.shape[1]
    chunks = inner // width
    step_tokens = min(step_tokens, each)
    rows = pl.BlockSpec((each, width), lambda i: (0, 0), pipeline_mode=ONCE)
    full = pl.BlockSpec((tokens, width), lambda i: (0, 0))
    vector = pl.BlockSpec((1, width), lambda i: (0, 0))
    across = pl.BlockSpec((width, width), lambda i: (0, jnp.minimum(i, chunks - 1)))
    along = pl.BlockSpec((width, width), lambda i: (jnp.minimum(i, chunks - 1), 0))
    return pl.pallas_call(
        functools.partial(feed_forward_kernel, waves, step_tokens),
        grid=(chunks + 1,),
        in_specs=[vector, pl.BlockSpec((width, width), lambda i: (0, 0), pipeline_mode=ONCE), across, along] + [rows] * (3 * waves),
        out_specs=[full, full, full, pl.BlockSpec((width, width), lambda i: (0, i)), along, vector],
        out_shape=[
            jax.ShapeDtypeStruct((tokens, width), BF16),
            jax.ShapeDtypeStruct((tokens, width), BF16),
            jax.ShapeDtypeStruct((tokens, width), F32),
            jax.ShapeDtypeStruct((width, inner + width), BF16),
            jax.ShapeDtypeStruct((inner, width), BF16),
            jax.ShapeDtypeStruct((1, width), F32),
        ],
        scratch_shapes=[
            pltpu.VMEM((tokens, width), F32),
            pltpu.VMEM((tokens, width), BF16),
            pltpu.VMEM((width, tokens), BF16),
            pltpu.VMEM((tokens, width), BF16),
            pltpu.VMEM((tokens, width), F32),
            pltpu.VMEM((tokens, width), F32),
            pltpu.VMEM((tokens, width), BF16),
            pltpu.VMEM((tokens, width), BF16),
        ],
        compiler_params=pltpu.CompilerParams(vmem_limit_bytes=60 * MIB),
        cost_estimate=pl.CostEstimate(flops=tokens * width * (12 * inner + 6 * width), bytes_accessed=40 * MIB, transcendentals=0),
        name="feed_forward",
    )(gain, w_out, w_in, w_back, *own, *att, *cot)


def backward_kernel(tile, heads, per, slots, info, place, pre, post, q_ref, da_ref, kt_ref, v_ref, u_ref, inv_ref, pre_wide, post_wide, p_in,
                    dq_ref, dk_ref, dv_ref, gpre_ref, gpost_ref,
                    qb, daa, dab, w_acc, dq_acc, dk_acc, dv_acc, delta, dm_all, p_buf, sems):
    task, part = pl.program_id(0), pl.program_id(1)
    parts = heads // per
    width = q_ref.shape[2]
    size = width // heads
    first, count = info[task, 0], info[task, 1]

    def cols(g):
        return slice(g * tile, (g + 1) * tile)

    def keys(j):
        return pl.ds(pl.multiple_of(place[first + j] * tile, tile), tile)

    def copy(j, slot):
        return pltpu.make_async_copy(p_in.at[task, part, j], p_buf.at[slot], sems.at[slot])

    copy(0, 0).start()

    @pl.when((task % slots == 0) & (part == 0))
    def _():
        dk_acc[...] = jnp.zeros_like(dk_acc)
        dv_acc[...] = jnp.zeros_like(dv_acc)

    @pl.when((task == 0) & (part == 0))
    def _():
        gpre_ref[...] = jnp.zeros_like(gpre_ref)
        gpost_ref[...] = jnp.zeros_like(gpost_ref)

    w_acc[...] = jnp.zeros_like(w_acc)
    qf = q_ref[0].astype(F32)
    daf = da_ref[0].astype(F32)
    qt = qf.T
    dat = daf.T
    inv = inv_ref[0, 0]
    for g in range(per):
        qb[cols(g), :] = (qf * pre_wide[0, g:g + 1, :]).astype(BF16)
        inv_g = inv[:, cols(g)]
        d_g = None
        for h in range(heads):
            rows = slice(h * size, (h + 1) * size)
            scaled = dat[rows] * inv_g
            weight = post[part * per + g, h]
            daa[rows, cols(g)] = (scaled * weight).astype(BF16)
            e = jnp.sum(scaled * u_ref[0, 0, rows, cols(g)].astype(F32), axis=0, keepdims=True)
            gpost_ref[part, g, h:h + 1, :] += e
            d_g = e * weight if d_g is None else d_g + e * weight
        delta[:, cols(g)] = d_g * inv_g
        column = jnp.broadcast_to(inv_g, (8, tile)).T[:, :1]
        dab[cols(g), :] = (daf * column * post_wide[0, g:g + 1, :]).astype(BF16)

    def step(j, carry):
        slot = j % 2
        copy(j, slot).wait()

        @pl.when(j + 1 < count)
        def _():
            copy(j + 1, 1 - slot).start()
        vj = v_ref[0, keys(j), :]
        ktj = kt_ref[0, :, keys(j)]
        for g in range(per):
            dp = dot(vj, daa[:, cols(g)])
            dm = (p_buf[slot, :, cols(g)].astype(F32) * (dp - delta[:, cols(g)])).astype(BF16)
            dm_all[:, cols(g)] = dm
            w_acc[:, cols(g)] += dot(ktj, dm)
        dv_acc[keys(j), :] += dot(p_buf[slot], dab[...])
        dk_acc[keys(j), :] += dot(dm_all[...], qb[...])
        return carry

    lax.fori_loop(0, count, step, 0)

    for h in range(heads):
        rows = slice(h * size, (h + 1) * size)
        acc = None
        for g in range(per):
            w = w_acc[rows, cols(g)]
            term = w * (pre[h, part * per + g] * size ** -0.5)
            acc = term if acc is None else acc + term
            gpre_ref[part, g, h:h + 1, :] += jnp.sum(w * qt[rows], axis=0, keepdims=True) * size ** -0.5
        dq_acc[rows] = jnp.where(part == 0, acc, acc + dq_acc[rows])

    @pl.when(part == parts - 1)
    def _():
        dq_ref[0] = dq_acc[...].T.astype(BF16)

    @pl.when((task % slots == slots - 1) & (part == parts - 1))
    def _():
        dk_ref[0] = dk_acc[...].astype(BF16)
        dv_ref[0] = dv_acc[...].astype(BF16)


def backward(info, place, pre, post, q, da, kt, v, u, inv, p, tile):
    tasks, _, width = q.shape
    rows, row_len, _ = v.shape
    heads = pre.shape[0]
    parts = heads // PER
    tiles = row_len // tile
    wide = PER * tile
    slots = tasks // rows
    size = width // heads
    pre_wide = jnp.repeat(pre.T * size ** -0.5, size, axis=1).reshape(parts, PER, width)
    post_wide = jnp.repeat(post, size, axis=1).reshape(parts, PER, width)
    task_spec = pl.BlockSpec((1, tile, width), lambda t, p: (t, 0, 0))
    mix_spec = pl.BlockSpec((1, PER, width), lambda t, p: (p, 0, 0))
    grad_spec = pl.BlockSpec((parts, PER, heads, tile), lambda t, p: (0, 0, 0, 0))
    row_spec = pl.BlockSpec((1, row_len, width), lambda t, p: (t // slots, 0, 0))
    pairs = tasks * tiles // 2
    dq, dk, dv, gpre, gpost = pl.pallas_call(
        functools.partial(backward_kernel, tile, heads, PER, slots),
        grid=(tasks, parts),
        in_specs=[
            SMEM, SMEM, SMEM, SMEM,
            task_spec, task_spec,
            pl.BlockSpec((1, width, row_len), lambda t, p: (t // slots, 0, 0), pipeline_mode=ONCE),
            pl.BlockSpec((1, row_len, width), lambda t, p: (t // slots, 0, 0), pipeline_mode=ONCE),
            pl.BlockSpec((1, 1, width, wide), lambda t, p: (t, p, 0, 0)),
            pl.BlockSpec((1, 1, 1, wide), lambda t, p: (t, p, 0, 0)),
            mix_spec, mix_spec, ANY,
        ],
        out_specs=[task_spec, row_spec, row_spec, grad_spec, grad_spec],
        out_shape=[
            jax.ShapeDtypeStruct((tasks, tile, width), BF16),
            jax.ShapeDtypeStruct((rows, row_len, width), BF16),
            jax.ShapeDtypeStruct((rows, row_len, width), BF16),
            jax.ShapeDtypeStruct((parts, PER, heads, tile), F32),
            jax.ShapeDtypeStruct((parts, PER, heads, tile), F32),
        ],
        scratch_shapes=[
            pltpu.VMEM((wide, width), BF16),
            pltpu.VMEM((width, wide), BF16),
            pltpu.VMEM((wide, width), BF16),
            pltpu.VMEM((width, wide), F32),
            pltpu.VMEM((width, tile), F32),
            pltpu.VMEM((row_len, width), F32),
            pltpu.VMEM((row_len, width), F32),
            pltpu.VMEM((1, wide), F32),
            pltpu.VMEM((tile, wide), BF16),
            pltpu.VMEM((2, tile, wide), BF16),
            pltpu.SemaphoreType.DMA((2,)),
        ],
        compiler_params=pltpu.CompilerParams(vmem_limit_bytes=60 * MIB),
        cost_estimate=pl.CostEstimate(flops=pairs * 8 * heads * width * tile * tile // 10, bytes_accessed=4 * MIB, transcendentals=0),
        name="attention_backward",
    )(info, place, pre, post, q, da, kt, v, u, inv, pre_wide, post_wide, p)
    return dq, dk, dv, jnp.sum(gpre, axis=3).reshape(heads, heads).T, jnp.sum(gpost, axis=3).reshape(heads, heads)


def input_kernel(tile, slots, carried, info, gain, w_q, w_k, w_v, extra, x_ref, dk_ref, dv_ref, dq_ref, mid_ref, *refs):
    earlier, refs = refs[:carried], refs[carried:]
    dx_ref, g_ref, d_s, g_acc, g_gain, g_prev, sem = refs
    row, block = pl.program_id(0), pl.program_id(1)
    begins = (row == 0) & (block == 0)
    ends = (row == pl.num_programs(0) - 1) & (block == pl.num_programs(1) - 1)
    width = w_q.shape[0]
    fetch = [pltpu.make_async_copy(e, g_prev, sem.at[0]) for e in earlier]

    @pl.when(begins)
    def _():
        for f in fetch:
            f.start()
        g_acc[...] = jnp.zeros_like(g_acc)
        g_gain[...] = jnp.zeros_like(g_gain)

    x = x_ref[0].astype(F32)
    s = inverse_rms(x)
    normed = (x * s * gain[...]).astype(BF16)
    normed_t = normed.T
    dk, dv = dk_ref[0], dv_ref[0]
    d_s[...] = dot_t(dk, w_k[...]) + dot_t(dv, w_v[...])
    g_acc[:, width:2 * width] += dot(normed_t, dk)
    g_acc[:, 2 * width:] += dot(normed_t, dv)

    def own_tiles(action):
        for c in range(slots):
            for b in range(slots):
                @pl.when(info[row * slots + c, 2] == block * slots + b)
                def _():
                    action(c, slice(b * tile, (b + 1) * tile))

    def add_queries(c, at):
        dq = dq_ref[c]
        d_s[at, :] += dot_t(dq, w_q[...])
        g_acc[:, :width] += dot(normed_t[:, at], dq)

    own_tiles(add_queries)
    d = d_s[...]
    g_gain[0:1, :] += jnp.sum(d * x * s, axis=0, keepdims=True)
    y = gain[...] * d
    d_s[...] = s * y - x * (s * s * s * jnp.mean(y * x, axis=1, keepdims=True))

    def add_middle(c, at):
        d_s[at, :] += mid_ref[c]

    own_tiles(add_middle)
    dx_ref[0] = d_s[...].astype(BF16)

    @pl.when(ends)
    def _():
        wide = 3 * width
        side = extra[...] + jnp.concatenate((g_gain[...].T, jnp.zeros((width, 120), F32)), axis=1)
        for f in fetch:
            f.wait()
            g_acc[...] += g_prev[:, :wide]
            side = side + g_prev[:, wide:]
        g_ref[:, :wide] = g_acc[...].astype(g_ref.dtype)
        g_ref[:, wide:] = side.astype(g_ref.dtype)


def input_side(info, gain, w_q, w_k, w_v, extra, x, dk, dv, dq, d_mid, earlier, tile, kind):
    rows, row_len, width = x.shape
    tasks = dq.shape[0]
    slots = tasks // rows
    span = slots * tile
    token_spec = pl.BlockSpec((1, span, width), lambda r, b: (r, b, 0))
    whole = pl.BlockSpec((width, width), lambda r, b: (0, 0), pipeline_mode=ONCE)
    vector = pl.BlockSpec((1, width), lambda r, b: (0, 0))
    task_spec = pl.BlockSpec((slots, tile, width), lambda r, b: (r, 0, 0))
    return pl.pallas_call(
        functools.partial(input_kernel, tile, slots, len(earlier)),
        grid=(rows, row_len // span),
        in_specs=[SMEM, vector, whole, whole, whole, pl.BlockSpec((width, 128), lambda r, b: (0, 0))]
        + [token_spec, token_spec, token_spec, task_spec, task_spec] + [ANY] * len(earlier),
        out_specs=[token_spec, pl.BlockSpec((width, 3 * width + 128), lambda r, b: (0, 0))],
        out_shape=[
            jax.ShapeDtypeStruct((rows, row_len, width), BF16),
            jax.ShapeDtypeStruct((width, 3 * width + 128), kind),
        ],
        scratch_shapes=[
            pltpu.VMEM((span, width), F32),
            pltpu.VMEM((width, 3 * width), F32),
            pltpu.VMEM((8, width), F32),
            pltpu.VMEM((width, 3 * width + 128), F32),
            pltpu.SemaphoreType.DMA((1,)),
        ],
        compiler_params=pltpu.CompilerParams(vmem_limit_bytes=60 * MIB),
        cost_estimate=pl.CostEstimate(flops=rows * row_len * width * width, bytes_accessed=2 * MIB, transcendentals=0),
        name="input_gradient",
    )(info, gain, w_q, w_k, w_v, extra, x, dk, dv, dq, d_mid, *earlier)


def swap(value, axis, bit):
    return lax.ppermute(value, axis, [(i, i ^ bit) for i in range(lax.axis_size(axis))])


def bits_of(axis):
    return [1 << b for b in range(lax.axis_size(axis).bit_length() - 1)]


def gather_pieces(block):
    masks, pieces = [0], [block]
    for bit in reversed(bits_of("blk")):
        pieces = pieces + [swap(piece, "blk", bit) for piece in pieces]
        masks = masks + [m ^ bit for m in masks]
    return pieces, masks


class Scatter:
    def __init__(self, parts, masks):
        self.held = dict(zip(masks, parts))
        self.bits = bits_of("blk")

    def step(self):
        bit = self.bits.pop(0)
        away = sorted(m for m in self.held if m & bit)
        came = {m: swap(self.held[m].astype(BF16), "blk", bit) for m in away}
        self.held = {m: v for m, v in self.held.items() if not m & bit}
        for m in away:
            self.held[m ^ bit] = self.held[m ^ bit].astype(F32) + came[m].astype(F32)

    def near(self):
        if len(self.bits) == len(bits_of("blk")):
            self.step()
        return self.held[max(self.held)]

    def finish(self):
        while self.bits:
            self.step()
        return self.held[0]


class Chain:
    def __init__(self, grad, order):
        self.dims = [("dp", b) for b in reversed(bits_of("dp"))] + [("blk", b) for b in reversed(bits_of("blk"))]
        self.order = list(order)
        self.shape = (grad.shape[0] >> len(self.dims),) + grad.shape[1:]
        self.held = grad.reshape((2,) * len(self.dims) + self.shape)

    def halve(self):
        axis, bit = which = self.order.pop(0)
        at = self.dims.index(which)
        del self.dims[at]
        side = (lax.axis_index(axis) // bit) % 2
        kept = lax.dynamic_index_in_dim(self.held, side, at, keepdims=False)
        sent = lax.dynamic_index_in_dim(self.held, 1 - side, at, keepdims=False).astype(BF16)
        total = kept.astype(F32) + swap(sent, axis, bit).astype(F32)
        self.held = total.astype(BF16) if self.order else total
        return self

    def finish(self):
        while self.order:
            self.halve()
        return self.held


def orders():
    core = ("blk", 1)
    near = [("dp", b) for b in bits_of("dp")[:2]] + [("blk", b) for b in bits_of("blk")[1:2]]
    far = [("dp", b) for b in bits_of("dp")[2:]] + [("blk", b) for b in bits_of("blk")[2:]]
    return [[core] + near[k:] + near[:k] + far for k in range(len(near))]


class Plan:
    def __init__(self, rows, span, circle):
        self.tile = min(256, span)
        self.rows, self.circle = rows, circle
        self.slots = span // self.tile
        self.tiles = self.slots * circle
        self.groups = {}
        for r in range(rows):
            for c in range(self.slots):
                route = tuple((b, self.worker(r, b * self.slots + c)) for b in range(circle))
                self.groups.setdefault(route, []).append((r, c))

    def worker(self, r, tile):
        lap, place = divmod(tile, self.circle)
        return place if (lap + r * (self.slots % 2)) % 2 == 0 else self.circle - 1 - place

    def table(self):
        found = [[[0] * self.circle for _ in range(self.slots)] for _ in range(self.rows)]
        for route, places in self.groups.items():
            for r, c in places:
                for b, d in route:
                    found[r][c][d] = b * self.slots + c
        return found

    def move(self, block, back=False):
        shape = block.shape
        cut = block.reshape((self.rows * self.slots, self.tile) + shape[2:])
        out = [None] * (self.rows * self.slots)
        for route, places in self.groups.items():
            at = [r * self.slots + c for r, c in places]
            piece = jnp.stack([cut[a] for a in at])
            pairs = [(d, b) for b, d in route] if back else list(route)
            if any(b != d for b, d in pairs):
                piece = lax.ppermute(piece, "blk", pairs)
            for i, a in enumerate(at):
                out[a] = piece[i]
        return out


def after(value, *others):
    return lax.optimization_barrier((value,) + others)[0]


def shards(
    inputs,
    doc_lengths,
    norm1_gain,
    w_query,
    w_key,
    w_value,
    head_mix_pre,
    head_mix_post,
    w_attn_out,
    norm2_gain,
    w_ff_in,
    w_ff_out,
    out_cotangent,
):
    rows, span, width = inputs.shape
    circle = lax.axis_size("blk")
    own = lax.axis_index("blk")
    plan = Plan(rows, span, circle)
    tile, slots, tiles = plan.tile, plan.slots, plan.tiles
    tasks = rows * slots
    waves = 2 if rows % 2 == 0 else 1
    rows_w, tasks_w = rows // waves, tasks // waves
    gain_one, gain_two = norm1_gain[None], norm2_gain[None]

    single = jnp.argmax(jnp.max(doc_lengths, axis=1)).astype(jnp.int32)
    every_row = jnp.arange(rows, dtype=jnp.int32)
    order = (every_row + single) % rows
    doc_lengths = doc_lengths[order]

    def take(array, n):
        picked = [lax.dynamic_index_in_dim(array, (single + r) % rows, 0, keepdims=True) for r in n]
        return picked[0] if len(picked) == 1 else jnp.concatenate(picked, axis=0)

    first_pieces, masks = gather_pieces(take(inputs, range(rows_w)))
    gathered = [first_pieces]
    for w in range(1, waves):
        block = after(take(inputs, range(w * rows_w, (w + 1) * rows_w)), *first_pieces)
        gathered.append([swap(block, "blk", m) if m else block for m in masks])

    place_of = [0] * circle
    for p, m in enumerate(masks):
        place_of[m] = p
    every = jnp.arange(tiles, dtype=jnp.int32)
    place = jnp.array(place_of, jnp.int32)[every // slots ^ own] * slots + every % slots
    work = jnp.array(plan.table(), jnp.int32)[:, :, own]
    bounds = jnp.cumsum(doc_lengths, axis=1)
    begin = jnp.max(jnp.where(bounds[:, None, :] <= work[:, :, None] * tile, bounds[:, None, :], 0), axis=2) // tile
    info = jnp.stack((begin, work - begin + 1, place[work]), axis=2).reshape(tasks, 3).astype(jnp.int32)
    infos = [info[w * tasks_w:(w + 1) * tasks_w] for w in range(waves)]

    ahead = []
    for w in range(waves):
        if w == waves - 1:
            cotangent = plan.move(take(after(out_cotangent, *[a[0] for a in ahead]), range(rows)))
        info_w = after(infos[w], ahead[-1][0]) if w else infos[w]
        ahead.append(forward(info_w, place, head_mix_pre, head_mix_post, gain_one, w_query, w_key, w_value, gathered[w], tile))

    def flat(tiles_list):
        return jnp.concatenate(tiles_list, axis=0)

    cotangent = [after(c, *[a[0] for a in ahead]) for c in cotangent]
    cots = [flat(cotangent[w * tasks_w:(w + 1) * tasks_w]) for w in range(waves)]
    output, d_attended, d_middle, grad_across, grad_along, grad_gain_two = feed_forward(
        gain_two, w_attn_out, w_ff_in, w_ff_out,
        [a[4].reshape(tasks_w * tile, width) for a in ahead], [a[0].reshape(tasks_w * tile, width) for a in ahead], cots,
    )
    output = jnp.stack(plan.move(output.reshape(rows, span, width), back=True)).reshape(rows, span, width)

    def restore(array):
        return lax.dynamic_slice_in_dim(jnp.concatenate((array, array), axis=0), (rows - single) % rows, rows)

    output = restore(output)
    d_attended = d_attended.reshape(waves, tasks_w, tile, width)
    d_middle = d_middle.reshape(waves, tasks_w, tile, width)

    routes = orders()
    chains = [Chain(grad_across, routes[0]), Chain(grad_along, routes[1 % len(routes)])]

    def halve(*which):
        for chain in which:
            if chain.order:
                chain.halve()

    heads = head_mix_pre.shape[0]
    devices = lax.axis_size("dp") * circle
    share = width // devices
    sums_of_x, earlier, mixes = [], [], 0
    halve(*chains)
    for w in range(waves):
        attended, sums, inverse, queries, x_own, probs, values, keys_t, x_all = ahead[w]
        info_w = after(infos[w], *earlier) if w else infos[w]
        d_queries, d_keys, d_values, grad_pre, grad_post = backward(
            info_w, place, head_mix_pre, head_mix_post, queries, d_attended[w], keys_t, values, sums, inverse, probs, tile
        )
        mixes = mixes + jnp.stack((grad_pre, grad_post)).reshape(-1)
        if w == waves - 1:
            lanes = -(-mixes.shape[0] // share)
            filled = jnp.concatenate((mixes, jnp.zeros(lanes * share - mixes.shape[0], F32))).reshape(share, lanes)
            columns = (jnp.zeros((width, 1), F32), grad_gain_two.reshape(width, 1), jnp.tile(filled, (devices, 1)))
            extra = jnp.concatenate(columns + (jnp.zeros((width, 126 - lanes), F32),), axis=1)
        else:
            extra = jnp.zeros((width, 128), F32)
        d_keys = after(d_keys, *[chain.held for chain in chains], *[s.near() for s in sums_of_x])
        halve(*chains)
        d_all, grad_qkv = input_side(
            infos[w], gain_one, w_query, w_key, w_value, extra, x_all, d_keys, d_values, d_queries, d_middle[w], earlier, tile,
            BF16 if w == waves - 1 else F32,
        )
        earlier = [grad_qkv]
        d_all = d_all.reshape(rows_w, circle, span, width)
        sums_of_x.append(Scatter([d_all[:, p] for p in range(circle)], masks))
    qkv = Chain(grad_qkv, routes[0])
    while qkv.order or any(chain.order for chain in chains):
        halve(qkv, *chains)
    input_grad = restore(jnp.concatenate([s.finish().astype(BF16) for s in sums_of_x], axis=0))
    total = qkv.held
    side = total[:, 3 * width:]
    mix_grads = side[:, 2:2 + lanes].reshape(-1)[:2 * heads * heads].reshape(2, heads, heads)
    across, along = chains[0].held, chains[1].held
    inner = w_ff_in.shape[1]
    return (
        output,
        input_grad,
        side[:, 0],
        total[:, :width],
        total[:, width:2 * width],
        total[:, 2 * width:3 * width],
        mix_grads[0],
        mix_grads[1],
        across[:, inner:],
        side[:, 1],
        across[:, :inner],
        along,
    )


def solution(mesh):
    tokens = P("dp", "blk", None)
    split = P(("dp", "blk"), None)
    in_specs = (tokens, P("dp", None)) + (P(),) * 10 + (tokens,)
    out_specs = (tokens, tokens, P(("dp", "blk")), split, split, split, P(), P(), split, P(("dp", "blk")), split, split)
    return jax.shard_map(shards, mesh=mesh, in_specs=in_specs, out_specs=out_specs, check_vma=False)
```

```python
import functools

import jax
import jax.numpy as jnp
from jax import lax
from jax.experimental import pallas as pl
from jax.experimental.pallas import tpu as pltpu
from jax.sharding import PartitionSpec as P

F32 = jnp.float32
BF16 = jnp.bfloat16
EPSILON = 1e-06
MASKED = -1e30
PER = 6
MIB = 2 ** 20
ONCE = pl.Buffered(1)
SMEM = pl.BlockSpec(memory_space=pltpu.SMEM)
ANY = pl.BlockSpec(memory_space=pl.ANY)


def dot(a, b):
    return jnp.dot(a, b, preferred_element_type=F32)


def dot_t(a, b):
    return lax.dot_general(a, b, (((1,), (1,)), ((), ())), preferred_element_type=F32)


def t_dot(a, b):
    return lax.dot_general(a, b, (((0,), (0,)), ((), ())), preferred_element_type=F32)


def inverse_rms(values):
    return lax.rsqrt(jnp.mean(values * values, axis=-1, keepdims=True) + EPSILON)


def forward_kernel(tile, heads, per, slots, count_pieces, info, place, pre, post, gain, w_q, w_k, w_v, *refs):
    pieces = refs[:count_pieces]
    (att_ref, u_ref, inv_ref, q_ref, own_ref, p_out, v_out, kt_out, x_out,
     x_s, k_s, v_s, kt_s, vt_s, qa, s_all, u_acc, att_acc, top, mass, p_buf, sems, row_sems) = refs[count_pieces:]
    task, part = pl.program_id(0), pl.program_id(1)
    row = task // slots
    parts = heads // per
    width = q_ref.shape[2]
    size = width // heads
    first, count, spot = info[task, 0], info[task, 1], info[task, 2]
    span = pieces[0].shape[1]

    def row_copies():
        return (
            pltpu.make_async_copy(v_s, v_out.at[row], row_sems.at[0]),
            pltpu.make_async_copy(kt_s, kt_out.at[row], row_sems.at[1]),
            pltpu.make_async_copy(x_s, x_out.at[row], row_sems.at[2]),
        )

    @pl.when((task % slots == 0) & (part == 0))
    def _():
        for i, piece in enumerate(pieces):
            for c in range(span // tile):
                at = slice(i * span + c * tile, i * span + (c + 1) * tile)
                low = piece[0, c * tile:(c + 1) * tile, :]
                x_s[at, :] = low
                x = low.astype(F32)
                normed = (x * inverse_rms(x) * gain[...]).astype(BF16)
                k = dot(normed, w_k[...]).astype(BF16)
                k_s[at, :] = k
                kt_s[:, at] = k.T
                v = dot(normed, w_v[...]).astype(BF16)
                v_s[at, :] = v
                vt_s[:, at] = v.T
        for c in row_copies():
            c.start()

    @pl.when(part == 0)
    def _():
        low = x_s[pl.ds(pl.multiple_of(spot * tile, tile), tile), :]
        own_ref[0] = low
        x = low.astype(F32)
        normed = (x * inverse_rms(x) * gain[...]).astype(BF16)
        q_ref[0] = dot(normed, w_q[...]).astype(BF16)

    qt = q_ref[0].astype(F32).T
    for g in range(per):
        for h in range(heads):
            rows = slice(h * size, (h + 1) * size)
            qa[rows, g * tile:(g + 1) * tile] = (qt[rows] * (pre[h, part * per + g] * size ** -0.5)).astype(BF16)

    def cols(g):
        return slice(g * tile, (g + 1) * tile)

    def keys(j):
        return pl.ds(pl.multiple_of(place[first + j] * tile, tile), tile)

    causal = lax.broadcasted_iota(jnp.int32, (tile, tile), 0) <= lax.broadcasted_iota(jnp.int32, (tile, tile), 1)
    twos, odd = count // 2, count % 2
    top[...] = jnp.full_like(top, MASKED)

    def scores(tiles, masked):
        kj = jnp.concatenate([k_s[keys(j), :] for j in tiles], axis=0)
        for g in range(per):
            s = dot(kj, qa[:, cols(g)])
            best = top[:, cols(g)]
            for i, j in enumerate(tiles):
                part_s = s[i * tile:(i + 1) * tile]
                if masked and i == len(tiles) - 1:
                    part_s = jnp.where(causal, part_s, MASKED)
                s_all[j, :, cols(g)] = part_s
                best = jnp.maximum(best, jnp.max(part_s, axis=0, keepdims=True))
            top[:, cols(g)] = best

    def score_pair(i, carry):
        scores((2 * i, 2 * i + 1), False)
        return carry

    lax.fori_loop(0, twos - 1 + odd, score_pair, 0)

    @pl.when(odd == 0)
    def _():
        scores((count - 2, count - 1), True)

    @pl.when(odd == 1)
    def _():
        scores((count - 1,), True)

    u_acc[...] = jnp.zeros_like(u_acc)
    mass[...] = jnp.zeros_like(mass)

    def copy(j, slot, i):
        return pltpu.make_async_copy(p_buf.at[slot, i], p_out.at[task, part, j], sems.at[slot, i])

    def sums(tiles, slot):
        vj = jnp.concatenate([vt_s[:, keys(j)] for j in tiles], axis=1)
        for g in range(per):
            low, weight = [], mass[:, cols(g)]
            for i, j in enumerate(tiles):
                p = jnp.exp(s_all[j, :, cols(g)] - top[:, cols(g)])
                weight = weight + jnp.sum(p, axis=0, keepdims=True)
                low.append(p.astype(BF16))
                p_buf[slot, i, :, cols(g)] = low[-1]
            mass[:, cols(g)] = weight
            u_acc[:, cols(g)] += dot(vj, jnp.concatenate(low, axis=0))
        for i, j in enumerate(tiles):
            copy(j, slot, i).start()

    def sum_pair(i, carry):
        slot = i % 2

        @pl.when(i >= 2)
        def _():
            copy(0, slot, 0).wait()
            copy(0, slot, 1).wait()
        sums((2 * i, 2 * i + 1), slot)
        return carry

    lax.fori_loop(0, twos, sum_pair, 0)

    @pl.when(odd == 1)
    def _():
        @pl.when(twos >= 2)
        def _():
            copy(0, twos % 2, 0).wait()
            copy(0, twos % 2, 1).wait()
        sums((count - 1,), twos % 2)

    inv = 1.0 / mass[...]
    inv_ref[0, 0] = inv
    u_ref[0, 0] = u_acc[...].astype(BF16)
    for h in range(heads):
        rows = slice(h * size, (h + 1) * size)
        acc = None
        for g in range(per):
            term = u_acc[rows, cols(g)] * (inv[:, cols(g)] * post[part * per + g, h])
            acc = term if acc is None else acc + term
        att_acc[rows] = jnp.where(part == 0, acc, acc + att_acc[rows])

    @pl.when(part == parts - 1)
    def _():
        att_ref[0] = att_acc[...].T.astype(BF16)

    @pl.when(twos >= 1)
    def _():
        copy(0, (twos - 1) % 2, 0).wait()
        copy(0, (twos - 1) % 2, 1).wait()

    @pl.when(odd == 1)
    def _():
        copy(0, twos % 2, 0).wait()

    @pl.when((odd == 0) & (twos >= 2))
    def _():
        copy(0, twos % 2, 0).wait()
        copy(0, twos % 2, 1).wait()

    @pl.when((task % slots == slots - 1) & (part == parts - 1))
    def _():
        for c in row_copies():
            c.wait()


def forward(info, place, pre, post, gain, w_q, w_k, w_v, pieces, tile):
    rows, span, width = pieces[0].shape
    row_len = span * len(pieces)
    heads = pre.shape[0]
    parts = heads // PER
    wide = PER * tile
    slots = span // tile
    tasks = rows * slots
    tiles = row_len // tile
    whole = pl.BlockSpec((width, width), lambda t, p: (0, 0), pipeline_mode=ONCE)
    task_spec = pl.BlockSpec((1, tile, width), lambda t, p: (t, 0, 0))
    pairs = tasks * tiles // 2
    return pl.pallas_call(
        functools.partial(forward_kernel, tile, heads, PER, slots, len(pieces)),
        grid=(tasks, parts),
        in_specs=[SMEM] * 4
        + [pl.BlockSpec((1, width), lambda t, p: (0, 0)), whole, whole, whole]
        + [pl.BlockSpec((1, span, width), lambda t, p: (t // slots, 0, 0), pipeline_mode=ONCE)] * len(pieces),
        out_specs=[
            task_spec,
            pl.BlockSpec((1, 1, width, wide), lambda t, p: (t, p, 0, 0)),
            pl.BlockSpec((1, 1, 1, wide), lambda t, p: (t, p, 0, 0)),
            task_spec, task_spec, ANY, ANY, ANY, ANY,
        ],
        out_shape=[
            jax.ShapeDtypeStruct((tasks, tile, width), BF16),
            jax.ShapeDtypeStruct((tasks, parts, width, wide), BF16),
            jax.ShapeDtypeStruct((tasks, parts, 1, wide), F32),
            jax.ShapeDtypeStruct((tasks, tile, width), BF16),
            jax.ShapeDtypeStruct((tasks, tile, width), BF16),
            jax.ShapeDtypeStruct((tasks, parts, tiles, tile, wide), BF16),
            jax.ShapeDtypeStruct((rows, row_len, width), BF16),
            jax.ShapeDtypeStruct((rows, width, row_len), BF16),
            jax.ShapeDtypeStruct((rows, row_len, width), BF16),
        ],
        scratch_shapes=[
            pltpu.VMEM((row_len, width), BF16),
            pltpu.VMEM((row_len, width), BF16),
            pltpu.VMEM((row_len, width), BF16),
            pltpu.VMEM((width, row_len), BF16),
            pltpu.VMEM((width, row_len), BF16),
            pltpu.VMEM((width, wide), BF16),
            pltpu.VMEM((tiles, tile, wide), F32),
            pltpu.VMEM((width, wide), F32),
            pltpu.VMEM((width, tile), F32),
            pltpu.VMEM((1, wide), F32),
            pltpu.VMEM((1, wide), F32),
            pltpu.VMEM((2, 2, tile, wide), BF16),
            pltpu.SemaphoreType.DMA((2, 2)),
            pltpu.SemaphoreType.DMA((3,)),
        ],
        compiler_params=pltpu.CompilerParams(vmem_limit_bytes=60 * MIB),
        cost_estimate=pl.CostEstimate(flops=pairs * 4 * heads * width * tile * tile // 10, bytes_accessed=4 * MIB, transcendentals=0),
        name="attention_forward",
    )(info, place, pre, post, gain, w_q, w_k, w_v, *pieces)


def feed_forward_kernel(waves, spots, gain, w_out, w_in_ref, w_back_ref, *refs):
    routes = 1 + max(route for route, _ in spots)
    own, att, cot = refs[:waves], refs[waves:2 * waves], refs[2 * waves:2 * waves + routes]
    out_refs, refs = refs[2 * waves + routes:2 * waves + 2 * routes], refs[2 * waves + 2 * routes:]
    (d_att_ref, d_mid_ref, g_in_ref, g_back_ref, g_gain_ref,
     mid, n_two, n_two_t, cot_s, out_acc, d_acc, act_s, dh_s) = refs
    step_tokens = cot[0].shape[1]
    step, steps = pl.program_id(0), pl.num_programs(0)
    tokens, width = mid.shape
    each = tokens // waves

    @pl.when(step == 0)
    def _():
        for w in range(waves):
            for b in range(0, each, step_tokens):
                at, to = slice(b, b + step_tokens), slice(w * each + b, w * each + b + step_tokens)
                m = own[w][at, :].astype(F32) + dot(att[w][at, :], w_out[...])
                mid[to, :] = m
                n = (m * inverse_rms(m) * gain[...]).astype(BF16)
                n_two[to, :] = n
                n_two_t[:, to] = n.T
                route, n = spots[(w * each + b) // step_tokens]
                cot_s[to, :] = cot[route][n]
        out_acc[...] = jnp.zeros_like(out_acc)
        d_acc[...] = jnp.zeros_like(d_acc)

    root = (2.0 / 3.141592653589793) ** 0.5

    @pl.when(step < steps - 1)
    def _():
        w_in, w_back = w_in_ref[...], w_back_ref[...]
        for b in range(0, tokens, step_tokens):
            at = slice(b, b + step_tokens)
            v = dot(n_two[at, :], w_in)
            d_active = dot_t(cot_s[at, :], w_back)
            square = v * v
            t = jnp.tanh(root * v * (1.0 + 0.044715 * square))
            half = 0.5 + 0.5 * t
            act = (v * half).astype(BF16)
            slope = half + (0.5 * root) * v * (1.0 - t * t) * (1.0 + (3 * 0.044715) * square)
            d_hidden = (slope * d_active).astype(BF16)
            act_s[at, :] = act
            dh_s[at, :] = d_hidden
            out_acc[at, :] += dot(act, w_back)
            d_acc[at, :] += dot_t(d_hidden, w_in)
        g_back_ref[...] = t_dot(act_s[...], cot_s[...])
        g_in_ref[...] = dot(n_two_t[...], dh_s[...]).astype(BF16)

    @pl.when(step == steps - 1)
    def _():
        total, grad_gain = None, None
        for w in range(waves):
            for b in range(0, each, step_tokens):
                at, to = slice(b, b + step_tokens), slice(w * each + b, w * each + b + step_tokens)
                m = mid[to, :]
                route, n = spots[(w * each + b) // step_tokens]
                out_refs[route][n] = (m + out_acc[to, :]).astype(BF16)
                d = d_acc[to, :]
                r = inverse_rms(m)
                part = jnp.sum(d * m * r, axis=0, keepdims=True)
                grad_gain = part if grad_gain is None else grad_gain + part
                z = gain[...] * d
                d_mid = cot_s[to, :].astype(F32) + r * z - m * (r * r * r * jnp.mean(z * m, axis=1, keepdims=True))
                d_mid_ref[to, :] = d_mid
                branch = d_mid.astype(BF16)
                d_att_ref[to, :] = dot_t(branch, w_out[...]).astype(BF16)
                part = t_dot(att[w][at, :], branch)
                total = part if total is None else total + part
        g_in_ref[...] = total.astype(BF16)
        g_gain_ref[...] = grad_gain


def feed_forward(gain, w_out, w_in, w_back, own, att, cot, spots):
    waves = len(own)
    each, width = own[0].shape
    tokens = waves * each
    inner = w_in.shape[1]
    chunks = inner // width
    rows = pl.BlockSpec((each, width), lambda i: (0, 0), pipeline_mode=ONCE)
    full = pl.BlockSpec((tokens, width), lambda i: (0, 0))
    vector = pl.BlockSpec((1, width), lambda i: (0, 0))
    across = pl.BlockSpec((width, width), lambda i: (0, jnp.minimum(i, chunks - 1)))
    along = pl.BlockSpec((width, width), lambda i: (jnp.minimum(i, chunks - 1), 0))
    return pl.pallas_call(
        functools.partial(feed_forward_kernel, waves, spots),
        grid=(chunks + 1,),
        in_specs=[vector, pl.BlockSpec((width, width), lambda i: (0, 0), pipeline_mode=ONCE), across, along]
        + [rows] * (2 * waves) + [pl.BlockSpec(c.shape, lambda i: (0, 0, 0), pipeline_mode=ONCE) for c in cot],
        out_specs=[pl.BlockSpec(c.shape, lambda i: (0, 0, 0)) for c in cot]
        + [full, full, pl.BlockSpec((width, width), lambda i: (0, i)), along, vector],
        out_shape=[jax.ShapeDtypeStruct(c.shape, BF16) for c in cot] + [
            jax.ShapeDtypeStruct((tokens, width), BF16),
            jax.ShapeDtypeStruct((tokens, width), F32),
            jax.ShapeDtypeStruct((width, inner + width), BF16),
            jax.ShapeDtypeStruct((inner, width), F32),
            jax.ShapeDtypeStruct((1, width), F32),
        ],
        scratch_shapes=[
            pltpu.VMEM((tokens, width), F32),
            pltpu.VMEM((tokens, width), BF16),
            pltpu.VMEM((width, tokens), BF16),
            pltpu.VMEM((tokens, width), BF16),
            pltpu.VMEM((tokens, width), F32),
            pltpu.VMEM((tokens, width), F32),
            pltpu.VMEM((tokens, width), BF16),
            pltpu.VMEM((tokens, width), BF16),
        ],
        compiler_params=pltpu.CompilerParams(vmem_limit_bytes=60 * MIB),
        cost_estimate=pl.CostEstimate(flops=tokens * width * (12 * inner + 6 * width), bytes_accessed=40 * MIB, transcendentals=0),
        name="feed_forward",
    )(gain, w_out, w_in, w_back, *own, *att, *cot)


def backward_kernel(tile, heads, per, slots, blocks, carried, share, info, place, pre, post, gain, gain_grad, w_q, w_k, w_v, q_ref, da_ref, mid_ref, u_ref, inv_ref,
                    pre_wide, post_wide, p_in, kt_in, v_in, x_in, *refs):
    earlier, refs = refs[:carried], refs[carried:]
    dx_out, refs = refs[:blocks], refs[blocks:]
    (g_out,
     kt_s, v_s, x_s, qb, daa, dab, w_acc, dq_acc, dq_s, dk_acc, dv_acc, delta, p_buf, gpre, gpost, d_s, dx_s, g_acc, g_gain,
     sems, row_sems, x_sems, dx_sems, g_sem) = refs
    task, part = pl.program_id(0), pl.program_id(1)
    tasks = pl.num_programs(0)
    row = task // slots
    parts = heads // per
    width = q_ref.shape[2]
    size = width // heads
    span = slots * tile
    first, count = info[task, 0], info[task, 1]
    begins = (task == 0) & (part == 0)
    opens = (task % slots == 0) & (part == 0)

    def cols(g):
        return slice(g * tile, (g + 1) * tile)

    def keys(j):
        return pl.ds(pl.multiple_of(place[first + j] * tile, tile), tile)

    def copy(j, slot, i):
        return pltpu.make_async_copy(p_in.at[task, part, j], p_buf.at[slot, i], sems.at[slot, i])

    def row_copies():
        return (
            pltpu.make_async_copy(v_in.at[row], v_s, row_sems.at[0]),
            pltpu.make_async_copy(kt_in.at[row], kt_s, row_sems.at[1]),
        )

    def x_copy(b, slot):
        return pltpu.make_async_copy(x_in.at[row, pl.ds(pl.multiple_of(b * span, span), span), :], x_s.at[slot], x_sems.at[slot])

    def dx_copy(b, slot):
        return pltpu.make_async_copy(dx_s.at[slot], dx_out[b].at[row], dx_sems.at[slot])

    fetch = [pltpu.make_async_copy(e, g_acc, g_sem.at[0]) for e in earlier]
    copy(0, 0, 0).start()

    @pl.when(count >= 2)
    def _():
        copy(1, 0, 1).start()

    @pl.when(opens)
    def _():
        for c in row_copies():
            c.start()
        dk_acc[...] = jnp.zeros_like(dk_acc)
        dv_acc[...] = jnp.zeros_like(dv_acc)

    @pl.when(begins)
    def _():
        for f in fetch:
            f.start()
        if not fetch:
            g_acc[...] = jnp.zeros_like(g_acc)
        g_gain[...] = jnp.zeros_like(g_gain)
        gpre[...] = jnp.zeros_like(gpre)
        gpost[...] = jnp.zeros_like(gpost)

    w_acc[...] = jnp.zeros_like(w_acc)
    qf = q_ref[0].astype(F32)
    daf = da_ref[0].astype(F32)
    qt = qf.T
    dat = daf.T
    inv = inv_ref[0, 0]
    for g in range(per):
        qb[cols(g), :] = (qf * pre_wide[0, g:g + 1, :]).astype(BF16)
        inv_g = inv[:, cols(g)]
        d_g = None
        for h in range(heads):
            rows = slice(h * size, (h + 1) * size)
            scaled = dat[rows] * inv_g
            weight = post[part * per + g, h]
            daa[rows, cols(g)] = (scaled * weight).astype(BF16)
            e = jnp.sum(scaled * u_ref[0, 0, rows, cols(g)].astype(F32), axis=0, keepdims=True)
            gpost[part, g, h:h + 1, :] += e
            d_g = e * weight if d_g is None else d_g + e * weight
        delta[:, cols(g)] = d_g * inv_g
        column = jnp.broadcast_to(inv_g, (8, tile)).T[:, :1]
        dab[cols(g), :] = (daf * column * post_wide[0, g:g + 1, :]).astype(BF16)

    @pl.when(opens)
    def _():
        for c in row_copies():
            c.wait()

    def step(tiles, slot):
        vj = jnp.concatenate([v_s[keys(j), :] for j in tiles], axis=0)
        ktj = jnp.concatenate([kt_s[:, keys(j)] for j in tiles], axis=1)
        n = len(tiles)
        dv = dot(jnp.concatenate([p_buf[slot, i] for i in range(n)], axis=0), dab[...])
        for i, j in enumerate(tiles):
            dv_acc[keys(j), :] += dv[i * tile:(i + 1) * tile]
        for g in range(per):
            dp = dot(vj, daa[:, cols(g)])
            dm = []
            for i in range(n):
                dm.append((p_buf[slot, i, :, cols(g)].astype(F32) * (dp[i * tile:(i + 1) * tile] - delta[:, cols(g)])).astype(BF16))
                p_buf[slot, i, :, cols(g)] = dm[-1]
            w_acc[:, cols(g)] += dot(ktj, jnp.concatenate(dm, axis=0))
        dk = dot(jnp.concatenate([p_buf[slot, i] for i in range(n)], axis=0), qb[...])
        for i, j in enumerate(tiles):
            dk_acc[keys(j), :] += dk[i * tile:(i + 1) * tile]

    def pair(i, carry):
        slot = i % 2
        copy(2 * i, slot, 0).wait()
        copy(2 * i, slot, 1).wait()

        @pl.when(2 * i + 2 < count)
        def _():
            copy(2 * i + 2, 1 - slot, 0).start()

        @pl.when(2 * i + 3 < count)
        def _():
            copy(2 * i + 3, 1 - slot, 1).start()
        step((2 * i, 2 * i + 1), slot)
        return carry

    lax.fori_loop(0, count // 2, pair, 0)

    @pl.when(count % 2 == 1)
    def _():
        slot = (count // 2) % 2
        copy(count - 1, slot, 0).wait()
        step((count - 1,), slot)

    closes = (task % slots == slots - 1) & (part == parts - 1)

    @pl.when(closes)
    def _():
        x_copy(0, 0).start()

    for h in range(heads):
        rows = slice(h * size, (h + 1) * size)
        acc = None
        for g in range(per):
            w = w_acc[rows, cols(g)]
            term = w * (pre[h, part * per + g] * size ** -0.5)
            acc = term if acc is None else acc + term
            gpre[part, g, h:h + 1, :] += jnp.sum(w * qt[rows], axis=0, keepdims=True) * size ** -0.5
        dq_acc[rows] = jnp.where(part == 0, acc, acc + dq_acc[rows])

    @pl.when(part == parts - 1)
    def _():
        dq_s[task % slots] = dq_acc[...].T.astype(BF16)

    @pl.when(closes & (row == 0))
    def _():
        for f in fetch:
            f.wait()

    @pl.when(closes)
    def _():
        def block(b, carry):
            slot = b % 2
            x_copy(b, slot).wait()

            @pl.when(b + 1 < blocks)
            def _():
                x_copy(b + 1, 1 - slot).start()
            here = pl.ds(pl.multiple_of(b * span, span), span)
            dk, dv = dk_acc[here, :].astype(BF16), dv_acc[here, :].astype(BF16)
            normed_t = []
            for i in range(slots):
                at = slice(i * tile, (i + 1) * tile)
                x = x_s[slot, at, :].astype(F32)
                normed_t.append((x * inverse_rms(x) * gain[...]).astype(BF16).T)
                d_s[at, :] = dot_t(dk[at], w_k[...])
                d_s[at, :] += dot_t(dv[at], w_v[...])
            normed_t = jnp.concatenate(normed_t, axis=1)
            g_acc[:, width:2 * width] += dot(normed_t, dk)
            g_acc[:, 2 * width:3 * width] += dot(normed_t, dv)

            def own_tiles(action):
                for c in range(slots):
                    for i in range(slots):
                        @pl.when(info[row * slots + c, 2] == b * slots + i)
                        def _():
                            action(c, slice(i * tile, (i + 1) * tile))

            def add_queries(c, at):
                dq = dq_s[c]
                d_s[at, :] += dot_t(dq, w_q[...])
                g_acc[:, :width] += dot(normed_t[:, at], dq)

            own_tiles(add_queries)
            for i in range(slots):
                at = slice(i * tile, (i + 1) * tile)
                d = d_s[at, :]
                x = x_s[slot, at, :].astype(F32)
                s = inverse_rms(x)
                g_gain[0:1, :] += jnp.sum(d * x * s, axis=0, keepdims=True)
                y = gain[...] * d
                d_s[at, :] = s * y - x * (s * s * s * jnp.mean(y * x, axis=1, keepdims=True))

            def add_middle(c, at):
                d_s[at, :] += mid_ref[c]

            own_tiles(add_middle)

            @pl.when(b >= 2)
            def _():
                dx_copy(0, slot).wait()
            dx_s[slot] = d_s[...].astype(BF16)
            for i in range(blocks):
                @pl.when(b == i)
                def _():
                    dx_copy(i, slot).start()
            return carry

        lax.fori_loop(0, blocks, block, 0)
        for slot in range(min(2, blocks)):
            dx_copy(0, slot).wait()

    @pl.when((task == tasks - 1) & (part == parts - 1))
    def _():
        lanes = g_acc.shape[1] - 3 * width
        both = jnp.concatenate((g_gain[0:1, :], gain_grad[...], jnp.zeros((6, width), F32)), axis=0)
        g_acc[:, 3 * width:] += jnp.concatenate((both.T, jnp.zeros((width, lanes - 8), F32)), axis=1)
        line = lax.broadcasted_iota(jnp.int32, (share, lanes), 0)
        mixes = jnp.zeros((share, lanes), F32)
        for n, grads in enumerate((gpre, gpost)):
            for g in range(heads):
                summed = jnp.sum(grads[g // per, g % per], axis=1, keepdims=True)
                at = n * heads + g
                vector = jnp.concatenate((jnp.zeros((2 + heads * (at // share), 1), F32), summed), axis=0)
                vector = jnp.concatenate((vector, jnp.zeros((lanes - vector.shape[0], 1), F32)), axis=0)
                spread = jnp.broadcast_to(vector, (lanes, lanes)).T[:1]
                mixes = jnp.where(line == at % share, mixes + spread, mixes)
        for d in range(width // share):
            g_acc[d * share:(d + 1) * share, 3 * width:] += mixes
        store = pltpu.make_async_copy(g_acc, g_out, g_sem.at[0])
        store.start()
        store.wait()


def backward(info, place, pre, post, gain, gain_grad, share, w_q, w_k, w_v, q, da, d_mid, kt, v, x, u, inv, p, earlier, tile):
    tasks, _, width = q.shape
    rows, row_len, _ = v.shape
    heads = pre.shape[0]
    parts = heads // PER
    tiles = row_len // tile
    wide = PER * tile
    slots = tasks // rows
    span = slots * tile
    blocks = row_len // span
    size = width // heads
    pre_wide = jnp.repeat(pre.T * size ** -0.5, size, axis=1).reshape(parts, PER, width)
    post_wide = jnp.repeat(post, size, axis=1).reshape(parts, PER, width)
    task_spec = pl.BlockSpec((1, tile, width), lambda t, p: (t, 0, 0), pipeline_mode=ONCE)
    mix_spec = pl.BlockSpec((1, PER, width), lambda t, p: (p, 0, 0))
    vector = pl.BlockSpec((1, width), lambda t, p: (0, 0))
    whole = pl.BlockSpec((width, width), lambda t, p: (0, 0), pipeline_mode=ONCE)
    pairs = tasks * tiles // 2
    out = pl.pallas_call(
        functools.partial(backward_kernel, tile, heads, PER, slots, blocks, len(earlier), share),
        grid=(tasks, parts),
        in_specs=[
            SMEM, SMEM, SMEM, SMEM,
            vector, vector, whole, whole, whole,
            task_spec, task_spec,
            pl.BlockSpec((slots, tile, width), lambda t, p: (t // slots, 0, 0), pipeline_mode=ONCE),
            pl.BlockSpec((1, 1, width, wide), lambda t, p: (t, p, 0, 0)),
            pl.BlockSpec((1, 1, 1, wide), lambda t, p: (t, p, 0, 0)),
            mix_spec, mix_spec, ANY, ANY, ANY, ANY,
        ] + [ANY] * len(earlier),
        out_specs=[ANY] * (blocks + 1),
        out_shape=[jax.ShapeDtypeStruct((rows, span, width), BF16)] * blocks + [
            jax.ShapeDtypeStruct((width, 3 * width + 128), F32),
        ],
        scratch_shapes=[
            pltpu.VMEM((width, row_len), BF16),
            pltpu.VMEM((row_len, width), BF16),
            pltpu.VMEM((2, span, width), BF16),
            pltpu.VMEM((wide, width), BF16),
            pltpu.VMEM((width, wide), BF16),
            pltpu.VMEM((wide, width), BF16),
            pltpu.VMEM((width, wide), F32),
            pltpu.VMEM((width, tile), F32),
            pltpu.VMEM((slots, tile, width), BF16),
            pltpu.VMEM((row_len, width), F32),
            pltpu.VMEM((row_len, width), F32),
            pltpu.VMEM((1, wide), F32),
            pltpu.VMEM((2, 2, tile, wide), BF16),
            pltpu.VMEM((parts, PER, heads, tile), F32),
            pltpu.VMEM((parts, PER, heads, tile), F32),
            pltpu.VMEM((span, width), F32),
            pltpu.VMEM((2, span, width), BF16),
            pltpu.VMEM((width, 3 * width + 128), F32),
            pltpu.VMEM((8, width), F32),
            pltpu.SemaphoreType.DMA((2, 2)),
            pltpu.SemaphoreType.DMA((2,)),
            pltpu.SemaphoreType.DMA((2,)),
            pltpu.SemaphoreType.DMA((2,)),
            pltpu.SemaphoreType.DMA((1,)),
        ],
        compiler_params=pltpu.CompilerParams(vmem_limit_bytes=63 * MIB),
        cost_estimate=pl.CostEstimate(flops=pairs * 8 * heads * width * tile * tile // 10, bytes_accessed=4 * MIB, transcendentals=0),
        name="attention_backward",
    )(info, place, pre, post, gain, gain_grad, w_q, w_k, w_v, q, da, d_mid, u, inv, pre_wide, post_wide, p, kt, v, x, *earlier)
    return out[:blocks], out[blocks]


def swap(value, axis, bit):
    return lax.ppermute(value, axis, [(i, i ^ bit) for i in range(lax.axis_size(axis))])


def bits_of(axis):
    return [1 << b for b in range(lax.axis_size(axis).bit_length() - 1)]


def gather_pieces(block):
    masks, pieces = [0], [block]
    for bit in reversed(bits_of("blk")):
        pieces = pieces + [swap(piece, "blk", bit) for piece in pieces]
        masks = masks + [m ^ bit for m in masks]
    return pieces, masks


class Scatter:
    def __init__(self, parts, masks, stages):
        self.held = dict(zip(masks, parts))
        self.stages = list(stages)

    def send(self):
        self.every = sum(self.stages.pop(0))
        self.came = {m: swap(v.astype(BF16), "blk", m & self.every) for m, v in sorted(self.held.items()) if m & self.every}

    def await_(self, *until):
        self.came = {m: after(v, *until) for m, v in self.came.items()}

    def pending(self):
        return list(self.came.values())

    def receive(self):
        came = self.came
        kept = {m: v for m, v in self.held.items() if not m & self.every}
        self.held = {k: sum([v.astype(F32) for m, v in came.items() if m & ~self.every == k], kept[k].astype(F32)) for k in kept}


class Chain:
    def __init__(self, grad, stages):
        self.circle = lax.axis_size("blk")
        self.world = self.circle * lax.axis_size("dp")
        self.bits = [1 << b for b in reversed(range(self.world.bit_length() - 1))]
        listed = [[b * self.circle if axis == "dp" else b for axis, b in stage] for stage in stages]
        rest = [b for b in reversed(self.bits) if not any(b in stage for stage in listed)]
        self.stages = listed + [rest[i:i + 2] for i in range(0, len(rest), 2)]
        self.shape = (grad.shape[0] // self.world,) + grad.shape[1:]
        self.held = grad.reshape((2,) * len(self.bits) + self.shape)

    def send(self):
        stage = self.stages.pop(0)
        own = lax.axis_index("dp") * self.circle + lax.axis_index("blk")

        def piece(flips):
            picked = self.held
            for bit, flip in zip(stage, flips):
                at = places[bit]
                side = (own // bit) % 2
                picked = lax.dynamic_slice_in_dim(picked, 1 - side if flip else side, 1, at)
            return picked.reshape(left)

        places = {bit: self.bits.index(bit) for bit in stage}
        remaining = [b for b in self.bits if b not in stage]
        left = (2,) * len(remaining) + self.shape
        self.terms = []
        for n in range(1 << len(stage)):
            flips = [(n >> i) & 1 for i in range(len(stage))]
            mask = sum(bit for bit, flip in zip(stage, flips) if flip)
            term = piece(flips)
            if mask:
                pairs = [(i, i ^ mask) for i in range(self.world)]
                term = lax.ppermute(term.astype(BF16), ("dp", "blk"), pairs)
            self.terms.append(term)
        self.bits = remaining

    def halves(self, at, stages):
        made = []
        for cut, order in zip((slice(None, at), slice(at, None)), stages):
            part = object.__new__(Chain)
            part.circle, part.world, part.bits = self.circle, self.world, list(self.bits)
            part.stages = [[b * self.circle if axis == "dp" else b for axis, b in stage] for stage in order]
            part.held = self.held[..., cut]
            part.shape = part.held.shape[len(self.bits):]
            made.append(part)
        return made

    def await_(self, *until):
        self.terms = self.terms[:1] + [after(term, *until) for term in self.terms[1:]]

    def pending(self):
        return self.terms[1:]

    def receive(self):
        total = self.terms[0].astype(F32)
        for term in self.terms[1:]:
            total = total + term.astype(F32)
        self.held = total.astype(BF16) if self.stages else total


class Exchange(Chain):
    def send(self):
        if len(self.stages) > 1:
            return super().send()
        self.stages = []
        groups = lax.axis_size("dp")
        self.terms = lax.all_to_all(self.held.reshape((groups,) + self.shape), "dp", 0, 0, tiled=True)

    def await_(self, *until):
        if isinstance(self.terms, list):
            return super().await_(*until)
        self.terms = after(self.terms, *until)

    def pending(self):
        return super().pending() if isinstance(self.terms, list) else [self.terms]

    def receive(self):
        if isinstance(self.terms, list):
            return super().receive()
        self.held = jnp.sum(self.terms.astype(F32), axis=0)


class Plan:
    def __init__(self, rows, span, circle):
        self.tile = min(256, span)
        self.rows, self.circle = rows, circle
        self.slots = span // self.tile
        self.tiles = self.slots * circle
        self.groups = {}
        for r in range(rows):
            for c in range(self.slots):
                route = tuple((b, self.worker(r, b * self.slots + c)) for b in range(circle))
                self.groups.setdefault(route, []).append((r, c))

    def worker(self, r, tile):
        lap, place = divmod(tile, self.circle)
        return place if (lap + r * (self.slots % 2)) % 2 == 0 else self.circle - 1 - place

    def table(self):
        found = [[[0] * self.circle for _ in range(self.slots)] for _ in range(self.rows)]
        for route, places in self.groups.items():
            for r, c in places:
                for b, d in route:
                    found[r][c][d] = b * self.slots + c
        return found

    def spots(self):
        found = {}
        for n, places in enumerate(self.groups.values()):
            for i, place in enumerate(places):
                found[place] = (n, i)
        return [found[r, c] for r in range(self.rows) for c in range(self.slots)]

    def move(self, tiles, back=False):
        out = []
        for route, piece in zip(self.groups, tiles):
            pairs = [(d, b) for b, d in route] if back else list(route)
            out.append(lax.ppermute(piece, "blk", pairs) if any(b != d for b, d in pairs) else piece)
        return out


def after(value, *others):
    return lax.optimization_barrier((value,) + others)[0]


def shards(
    inputs,
    doc_lengths,
    norm1_gain,
    w_query,
    w_key,
    w_value,
    head_mix_pre,
    head_mix_post,
    w_attn_out,
    norm2_gain,
    w_ff_in,
    w_ff_out,
    out_cotangent,
):
    rows, span, width = inputs.shape
    circle = lax.axis_size("blk")
    own = lax.axis_index("blk")
    plan = Plan(rows, span, circle)
    tile, slots, tiles = plan.tile, plan.slots, plan.tiles
    tasks = rows * slots
    waves = 2 if rows % 2 == 0 else 1
    rows_w, tasks_w = rows // waves, tasks // waves
    gain_one, gain_two = norm1_gain[None], norm2_gain[None]

    single = jnp.argmax(jnp.max(doc_lengths, axis=1)).astype(jnp.int32)
    every_row = jnp.arange(rows, dtype=jnp.int32)
    order = (every_row + single) % rows
    doc_lengths = doc_lengths[order]

    def take(array, n):
        picked = [lax.dynamic_index_in_dim(array, (single + r) % rows, 0, keepdims=True) for r in n]
        return picked[0] if len(picked) == 1 else jnp.concatenate(picked, axis=0)

    first_pieces, masks = gather_pieces(take(inputs, range(rows_w)))
    gathered = [first_pieces]
    for w in range(1, waves):
        block = after(take(inputs, range(w * rows_w, (w + 1) * rows_w)), *first_pieces)
        gathered.append([swap(block, "blk", m) if m else block for m in masks])

    place_of = [0] * circle
    for p, m in enumerate(masks):
        place_of[m] = p
    every = jnp.arange(tiles, dtype=jnp.int32)
    place = jnp.array(place_of, jnp.int32)[every // slots ^ own] * slots + every % slots
    work = jnp.array(plan.table(), jnp.int32)[:, :, own]
    bounds = jnp.cumsum(doc_lengths, axis=1)
    begin = jnp.max(jnp.where(bounds[:, None, :] <= work[:, :, None] * tile, bounds[:, None, :], 0), axis=2) // tile
    info = jnp.stack((begin, work - begin + 1, place[work]), axis=2).reshape(tasks, 3).astype(jnp.int32)
    infos = [info[w * tasks_w:(w + 1) * tasks_w] for w in range(waves)]

    ahead = []
    for w in range(waves):
        if w == waves - 1:
            source = take(after(out_cotangent, *[a[0] for a in ahead]), range(rows)).reshape(rows, slots, tile, width)
            cotangent = plan.move([jnp.stack([source[r, c] for r, c in places]) for places in plan.groups.values()])
        info_w = after(infos[w], ahead[-1][0]) if w else infos[w]
        ahead.append(forward(info_w, place, head_mix_pre, head_mix_post, gain_one, w_query, w_key, w_value, gathered[w], tile))

    cotangent = [after(c, *[a[0] for a in ahead]) for c in cotangent]
    spots = plan.spots()
    *output, d_attended, d_middle, grad_across, grad_along, grad_gain_two = feed_forward(
        gain_two, w_attn_out, w_ff_in, w_ff_out,
        [a[4].reshape(tasks_w * tile, width) for a in ahead], [a[0].reshape(tasks_w * tile, width) for a in ahead], cotangent, spots,
    )
    d_attended = d_attended.reshape(waves, tasks_w, tile, width)
    d_middle = d_middle.reshape(waves, tasks_w, tile, width)

    def restore(listed):
        if rows == 2:
            return jnp.stack([jnp.where(single == 0, listed[r], listed[1 - r]) for r in range(2)])
        array = jnp.stack(listed)
        return array[(every_row - single) % rows]

    blk, dp = [("blk", b) for b in bits_of("blk")], [("dp", b) for b in bits_of("dp")]
    chains = [Exchange(grad_across, [blk[i:i + 2] for i in range(0, len(blk), 2)] + [dp])]
    for chain in chains:
        chain.send()
    along = lax.psum_scatter(grad_along, ("dp", "blk"), scatter_dimension=0, tiled=True)
    output = plan.move(output, back=True)
    heads = head_mix_pre.shape[0]
    devices = lax.axis_size("dp") * circle
    share = width // devices
    input_rows, earlier = [], []
    for w in range(waves):
        attended, sums, inverse, queries, x_own, probs, values, keys_t, x_all = ahead[w]
        info_w = infos[w]
        if w:
            info_w = after(info_w, *earlier, *output, *[chain.held for chain in chains])
        last = w == waves - 1
        d_x, grad_qkv = backward(
            info_w, place, head_mix_pre, head_mix_post, gain_one, grad_gain_two * last, share, w_query, w_key, w_value,
            queries, d_attended[w], d_middle[w], keys_t, values, x_all, sums, inverse, probs, earlier, tile,
        )
        if not last:
            output = [after(o, grad_qkv) for o in output]
        for pending in chains + input_rows:
            pending.await_(grad_qkv, *([] if last else output))
        if not last:
            for pending in chains + input_rows:
                pending.receive()
        earlier = [grad_qkv]
        input_rows.append(Scatter(d_x, masks, [[b] for b in bits_of("blk")] if last else [bits_of("blk")]))
        if not last:
            for pending in chains + input_rows:
                pending.send()
    spots = dict(zip([(r, c) for r in range(rows) for c in range(slots)], spots))
    output = restore([jnp.concatenate([output[spots[r, c][0]][spots[r, c][1]] for c in range(slots)]) for r in range(rows)])
    for pending in chains + input_rows[:-1]:
        grad_qkv = after(grad_qkv, *pending.pending())
    qkv = Chain(grad_qkv, [blk[:1]])
    for pending in [qkv, input_rows[-1]]:
        pending.send()
        pending.receive()
    for pending in chains + input_rows[:-1]:
        pending.receive()
    rest = [[b] for b in blk[1:] + dp[2:]]
    halves = qkv.halves(2 * width - 3 * 128, [[[b] for b in dp[:2]] + rest, [[b] for b in dp[1::-1]] + rest])
    every = [*halves, *chains, *input_rows]
    while any(pending.stages for pending in every):
        active = [pending for pending in every if pending.stages]
        for pending in active:
            pending.send()
        for pending in active:
            pending.receive()
    input_rows = [pending.held[0] for pending in input_rows]
    input_grad = restore([v[r].astype(BF16) for v in input_rows for r in range(rows_w)])
    total = jnp.concatenate([half.held for half in halves], axis=1)
    side = total[:, 3 * width:]
    mix_grads = [[side[at % share, 2 + heads * (at // share):][:heads] for at in range(n * heads, (n + 1) * heads)] for n in range(2)]
    across = chains[0].held
    inner = w_ff_in.shape[1]
    return (
        output,
        input_grad,
        side[:, 0],
        total[:, :width],
        total[:, width:2 * width],
        total[:, 2 * width:3 * width],
        jnp.stack(mix_grads[0], axis=1),
        jnp.stack(mix_grads[1]),
        across[:, inner:],
        side[:, 1],
        across[:, :inner],
        along,
    )


def solution(mesh):
    tokens = P("dp", "blk", None)
    split = P(("dp", "blk"), None)
    in_specs = (tokens, P("dp", None)) + (P(),) * 10 + (tokens,)
    out_specs = (tokens, tokens, P(("dp", "blk")), split, split, split, P(), P(), split, P(("dp", "blk")), split, split)
    return jax.shard_map(shards, mesh=mesh, in_specs=in_specs, out_specs=out_specs, check_vma=False)
```

```python
import functools

import jax
import jax.numpy as jnp
from jax import lax
from jax.experimental import pallas as pl
from jax.experimental.pallas import tpu as pltpu
from jax.sharding import PartitionSpec as P

F32 = jnp.float32
BF16 = jnp.bfloat16
EPSILON = 1e-06
MASKED = -1e30
PER = 6
MIB = 2 ** 20
ONCE = pl.Buffered(1)
SMEM = pl.BlockSpec(memory_space=pltpu.SMEM)
ANY = pl.BlockSpec(memory_space=pl.ANY)


def dot(a, b):
    return jnp.dot(a, b, preferred_element_type=F32)


def dot_t(a, b):
    return lax.dot_general(a, b, (((1,), (1,)), ((), ())), preferred_element_type=F32)


def t_dot(a, b):
    return lax.dot_general(a, b, (((0,), (0,)), ((), ())), preferred_element_type=F32)


def inverse_rms(values):
    return lax.rsqrt(jnp.mean(values * values, axis=-1, keepdims=True) + EPSILON)


def forward_kernel(tile, heads, per, slots, count_pieces, info, place, pre, post, gain, w_q, w_k, w_v, *refs):
    pieces = refs[:count_pieces]
    (att_ref, u_ref, inv_ref, q_ref, own_ref, p_out, v_out, kt_out, x_out,
     x_s, k_s, v_s, kt_s, vt_s, qa, s_all, u_acc, att_acc, top, mass, p_buf, sems, row_sems) = refs[count_pieces:]
    task, part = pl.program_id(0), pl.program_id(1)
    row = task // slots
    parts = heads // per
    width = q_ref.shape[2]
    size = width // heads
    first, count, spot = info[task, 0], info[task, 1], info[task, 2]
    span = pieces[0].shape[1]

    def row_copies():
        return (
            pltpu.make_async_copy(v_s, v_out.at[row], row_sems.at[0]),
            pltpu.make_async_copy(kt_s, kt_out.at[row], row_sems.at[1]),
            pltpu.make_async_copy(x_s, x_out.at[row], row_sems.at[2]),
        )

    @pl.when((task % slots == 0) & (part == 0))
    def _():
        for i, piece in enumerate(pieces):
            for c in range(span // tile):
                at = slice(i * span + c * tile, i * span + (c + 1) * tile)
                low = piece[0, c * tile:(c + 1) * tile, :]
                x_s[at, :] = low
                x = low.astype(F32)
                normed = (x * inverse_rms(x) * gain[...]).astype(BF16)
                k = dot(normed, w_k[...]).astype(BF16)
                k_s[at, :] = k
                kt_s[:, at] = k.T
                v = dot(normed, w_v[...]).astype(BF16)
                v_s[at, :] = v
                vt_s[:, at] = v.T
        for c in row_copies():
            c.start()

    @pl.when(part == 0)
    def _():
        low = x_s[pl.ds(pl.multiple_of(spot * tile, tile), tile), :]
        own_ref[0] = low
        x = low.astype(F32)
        normed = (x * inverse_rms(x) * gain[...]).astype(BF16)
        q_ref[0] = dot(normed, w_q[...]).astype(BF16)

    qt = q_ref[0].astype(F32).T
    for g in range(per):
        for h in range(heads):
            rows = slice(h * size, (h + 1) * size)
            qa[rows, g * tile:(g + 1) * tile] = (qt[rows] * (pre[h, part * per + g] * size ** -0.5)).astype(BF16)

    def cols(g):
        return slice(g * tile, (g + 1) * tile)

    def keys(j):
        return pl.ds(pl.multiple_of(place[first + j] * tile, tile), tile)

    causal = lax.broadcasted_iota(jnp.int32, (tile, tile), 0) <= lax.broadcasted_iota(jnp.int32, (tile, tile), 1)
    twos, odd = count // 2, count % 2
    top[...] = jnp.full_like(top, MASKED)

    def scores(tiles, masked):
        kj = jnp.concatenate([k_s[keys(j), :] for j in tiles], axis=0)
        for g in range(per):
            s = dot(kj, qa[:, cols(g)])
            best = top[:, cols(g)]
            for i, j in enumerate(tiles):
                part_s = s[i * tile:(i + 1) * tile]
                if masked and i == len(tiles) - 1:
                    part_s = jnp.where(causal, part_s, MASKED)
                s_all[j, :, cols(g)] = part_s
                best = jnp.maximum(best, jnp.max(part_s, axis=0, keepdims=True))
            top[:, cols(g)] = best

    def score_pair(i, carry):
        scores((2 * i, 2 * i + 1), False)
        return carry

    lax.fori_loop(0, twos - 1 + odd, score_pair, 0)

    @pl.when(odd == 0)
    def _():
        scores((count - 2, count - 1), True)

    @pl.when(odd == 1)
    def _():
        scores((count - 1,), True)

    u_acc[...] = jnp.zeros_like(u_acc)
    mass[...] = jnp.zeros_like(mass)

    def copy(j, slot, i):
        return pltpu.make_async_copy(p_buf.at[slot, i], p_out.at[task, part, j], sems.at[slot, i])

    def sums(tiles, slot):
        vj = jnp.concatenate([vt_s[:, keys(j)] for j in tiles], axis=1)
        for g in range(per):
            low, weight = [], mass[:, cols(g)]
            for i, j in enumerate(tiles):
                p = jnp.exp(s_all[j, :, cols(g)] - top[:, cols(g)])
                weight = weight + jnp.sum(p, axis=0, keepdims=True)
                low.append(p.astype(BF16))
                p_buf[slot, i, :, cols(g)] = low[-1]
            mass[:, cols(g)] = weight
            u_acc[:, cols(g)] += dot(vj, jnp.concatenate(low, axis=0))
        for i, j in enumerate(tiles):
            copy(j, slot, i).start()

    def sum_pair(i, carry):
        slot = i % 2

        @pl.when(i >= 2)
        def _():
            copy(0, slot, 0).wait()
            copy(0, slot, 1).wait()
        sums((2 * i, 2 * i + 1), slot)
        return carry

    lax.fori_loop(0, twos, sum_pair, 0)

    @pl.when(odd == 1)
    def _():
        @pl.when(twos >= 2)
        def _():
            copy(0, twos % 2, 0).wait()
            copy(0, twos % 2, 1).wait()
        sums((count - 1,), twos % 2)

    inv = 1.0 / mass[...]
    inv_ref[0, 0] = inv
    u_ref[0, 0] = u_acc[...].astype(BF16)
    for h in range(heads):
        rows = slice(h * size, (h + 1) * size)
        acc = None
        for g in range(per):
            term = u_acc[rows, cols(g)] * (inv[:, cols(g)] * post[part * per + g, h])
            acc = term if acc is None else acc + term
        att_acc[rows] = jnp.where(part == 0, acc, acc + att_acc[rows])

    @pl.when(part == parts - 1)
    def _():
        att_ref[0] = att_acc[...].T.astype(BF16)

    @pl.when(twos >= 1)
    def _():
        copy(0, (twos - 1) % 2, 0).wait()
        copy(0, (twos - 1) % 2, 1).wait()

    @pl.when(odd == 1)
    def _():
        copy(0, twos % 2, 0).wait()

    @pl.when((odd == 0) & (twos >= 2))
    def _():
        copy(0, twos % 2, 0).wait()
        copy(0, twos % 2, 1).wait()

    @pl.when((task % slots == slots - 1) & (part == parts - 1))
    def _():
        for c in row_copies():
            c.wait()


def forward(info, place, pre, post, gain, w_q, w_k, w_v, pieces, tile):
    rows, span, width = pieces[0].shape
    row_len = span * len(pieces)
    heads = pre.shape[0]
    parts = heads // PER
    wide = PER * tile
    slots = span // tile
    tasks = rows * slots
    tiles = row_len // tile
    whole = pl.BlockSpec((width, width), lambda t, p: (0, 0), pipeline_mode=ONCE)
    task_spec = pl.BlockSpec((1, tile, width), lambda t, p: (t, 0, 0))
    pairs = tasks * tiles // 2
    return pl.pallas_call(
        functools.partial(forward_kernel, tile, heads, PER, slots, len(pieces)),
        grid=(tasks, parts),
        in_specs=[SMEM] * 4
        + [pl.BlockSpec((1, width), lambda t, p: (0, 0)), whole, whole, whole]
        + [pl.BlockSpec((1, span, width), lambda t, p: (t // slots, 0, 0), pipeline_mode=ONCE)] * len(pieces),
        out_specs=[
            task_spec,
            pl.BlockSpec((1, 1, width, wide), lambda t, p: (t, p, 0, 0)),
            pl.BlockSpec((1, 1, 1, wide), lambda t, p: (t, p, 0, 0)),
            task_spec, task_spec, ANY, ANY, ANY, ANY,
        ],
        out_shape=[
            jax.ShapeDtypeStruct((tasks, tile, width), BF16),
            jax.ShapeDtypeStruct((tasks, parts, width, wide), BF16),
            jax.ShapeDtypeStruct((tasks, parts, 1, wide), F32),
            jax.ShapeDtypeStruct((tasks, tile, width), BF16),
            jax.ShapeDtypeStruct((tasks, tile, width), BF16),
            jax.ShapeDtypeStruct((tasks, parts, tiles, tile, wide), BF16),
            jax.ShapeDtypeStruct((rows, row_len, width), BF16),
            jax.ShapeDtypeStruct((rows, width, row_len), BF16),
            jax.ShapeDtypeStruct((rows, row_len, width), BF16),
        ],
        scratch_shapes=[
            pltpu.VMEM((row_len, width), BF16),
            pltpu.VMEM((row_len, width), BF16),
            pltpu.VMEM((row_len, width), BF16),
            pltpu.VMEM((width, row_len), BF16),
            pltpu.VMEM((width, row_len), BF16),
            pltpu.VMEM((width, wide), BF16),
            pltpu.VMEM((tiles, tile, wide), F32),
            pltpu.VMEM((width, wide), F32),
            pltpu.VMEM((width, tile), F32),
            pltpu.VMEM((1, wide), F32),
            pltpu.VMEM((1, wide), F32),
            pltpu.VMEM((2, 2, tile, wide), BF16),
            pltpu.SemaphoreType.DMA((2, 2)),
            pltpu.SemaphoreType.DMA((3,)),
        ],
        compiler_params=pltpu.CompilerParams(vmem_limit_bytes=60 * MIB),
        cost_estimate=pl.CostEstimate(flops=pairs * 4 * heads * width * tile * tile // 10, bytes_accessed=4 * MIB, transcendentals=0),
        name="attention_forward",
    )(info, place, pre, post, gain, w_q, w_k, w_v, *pieces)


def feed_forward_kernel(waves, spots, gain, w_out, w_in_ref, w_back_ref, *refs):
    routes = 1 + max(route for route, _ in spots)
    own, att, cot = refs[:waves], refs[waves:2 * waves], refs[2 * waves:2 * waves + routes]
    out_refs, refs = refs[2 * waves + routes:2 * waves + 2 * routes], refs[2 * waves + 2 * routes:]
    (d_att_ref, d_mid_ref, g_in_ref, g_back_ref, g_gain_ref,
     mid, n_two, n_two_t, cot_s, out_acc, d_acc, act_s, dh_s) = refs
    step_tokens = cot[0].shape[1]
    step, steps = pl.program_id(0), pl.num_programs(0)
    tokens, width = mid.shape
    each = tokens // waves

    @pl.when(step == 0)
    def _():
        for w in range(waves):
            for b in range(0, each, step_tokens):
                at, to = slice(b, b + step_tokens), slice(w * each + b, w * each + b + step_tokens)
                m = own[w][at, :].astype(F32) + dot(att[w][at, :], w_out[...])
                mid[to, :] = m
                n = (m * inverse_rms(m) * gain[...]).astype(BF16)
                n_two[to, :] = n
                n_two_t[:, to] = n.T
                route, n = spots[(w * each + b) // step_tokens]
                cot_s[to, :] = cot[route][n]
        out_acc[...] = jnp.zeros_like(out_acc)
        d_acc[...] = jnp.zeros_like(d_acc)

    root = (2.0 / 3.141592653589793) ** 0.5

    @pl.when(step < steps - 1)
    def _():
        w_in, w_back = w_in_ref[...], w_back_ref[...]
        for b in range(0, tokens, step_tokens):
            at = slice(b, b + step_tokens)
            v = dot(n_two[at, :], w_in)
            d_active = dot_t(cot_s[at, :], w_back)
            square = v * v
            t = jnp.tanh(root * v * (1.0 + 0.044715 * square))
            half = 0.5 + 0.5 * t
            act = (v * half).astype(BF16)
            slope = half + (0.5 * root) * v * (1.0 - t * t) * (1.0 + (3 * 0.044715) * square)
            d_hidden = (slope * d_active).astype(BF16)
            act_s[at, :] = act
            dh_s[at, :] = d_hidden
            out_acc[at, :] += dot(act, w_back)
            d_acc[at, :] += dot_t(d_hidden, w_in)
        g_back_ref[...] = t_dot(act_s[...], cot_s[...])
        g_in_ref[...] = dot(n_two_t[...], dh_s[...]).astype(BF16)

    @pl.when(step == steps - 1)
    def _():
        total, grad_gain = None, None
        for w in range(waves):
            for b in range(0, each, step_tokens):
                at, to = slice(b, b + step_tokens), slice(w * each + b, w * each + b + step_tokens)
                m = mid[to, :]
                route, n = spots[(w * each + b) // step_tokens]
                out_refs[route][n] = (m + out_acc[to, :]).astype(BF16)
                d = d_acc[to, :]
                r = inverse_rms(m)
                part = jnp.sum(d * m * r, axis=0, keepdims=True)
                grad_gain = part if grad_gain is None else grad_gain + part
                z = gain[...] * d
                d_mid = cot_s[to, :].astype(F32) + r * z - m * (r * r * r * jnp.mean(z * m, axis=1, keepdims=True))
                d_mid_ref[to, :] = d_mid
                branch = d_mid.astype(BF16)
                d_att_ref[to, :] = dot_t(branch, w_out[...]).astype(BF16)
                part = t_dot(att[w][at, :], branch)
                total = part if total is None else total + part
        g_in_ref[...] = total.astype(BF16)
        g_gain_ref[...] = grad_gain


def feed_forward(gain, w_out, w_in, w_back, own, att, cot, spots):
    waves = len(own)
    each, width = own[0].shape
    tokens = waves * each
    inner = w_in.shape[1]
    chunks = inner // width
    rows = pl.BlockSpec((each, width), lambda i: (0, 0), pipeline_mode=ONCE)
    full = pl.BlockSpec((tokens, width), lambda i: (0, 0))
    vector = pl.BlockSpec((1, width), lambda i: (0, 0))
    across = pl.BlockSpec((width, width), lambda i: (0, jnp.minimum(i, chunks - 1)))
    along = pl.BlockSpec((width, width), lambda i: (jnp.minimum(i, chunks - 1), 0))
    return pl.pallas_call(
        functools.partial(feed_forward_kernel, waves, spots),
        grid=(chunks + 1,),
        in_specs=[vector, pl.BlockSpec((width, width), lambda i: (0, 0), pipeline_mode=ONCE), across, along]
        + [rows] * (2 * waves) + [pl.BlockSpec(c.shape, lambda i: (0, 0, 0), pipeline_mode=ONCE) for c in cot],
        out_specs=[pl.BlockSpec(c.shape, lambda i: (0, 0, 0)) for c in cot]
        + [full, full, pl.BlockSpec((width, width), lambda i: (0, i)), along, vector],
        out_shape=[jax.ShapeDtypeStruct(c.shape, BF16) for c in cot] + [
            jax.ShapeDtypeStruct((tokens, width), BF16),
            jax.ShapeDtypeStruct((tokens, width), F32),
            jax.ShapeDtypeStruct((width, inner + width), BF16),
            jax.ShapeDtypeStruct((inner, width), F32),
            jax.ShapeDtypeStruct((1, width), F32),
        ],
        scratch_shapes=[
            pltpu.VMEM((tokens, width), F32),
            pltpu.VMEM((tokens, width), BF16),
            pltpu.VMEM((width, tokens), BF16),
            pltpu.VMEM((tokens, width), BF16),
            pltpu.VMEM((tokens, width), F32),
            pltpu.VMEM((tokens, width), F32),
            pltpu.VMEM((tokens, width), BF16),
            pltpu.VMEM((tokens, width), BF16),
        ],
        compiler_params=pltpu.CompilerParams(vmem_limit_bytes=60 * MIB),
        cost_estimate=pl.CostEstimate(flops=tokens * width * (12 * inner + 6 * width), bytes_accessed=40 * MIB, transcendentals=0),
        name="feed_forward",
    )(gain, w_out, w_in, w_back, *own, *att, *cot)


def backward_kernel(tile, heads, per, slots, blocks, carried, share, info, place, pre, post, gain, gain_grad, w_q, w_k, w_v, q_ref, da_ref, mid_ref, u_ref, inv_ref,
                    pre_wide, post_wide, p_in, kt_in, v_in, x_in, *refs):
    earlier, refs = refs[:carried], refs[carried:]
    dx_out, refs = refs[:blocks], refs[blocks:]
    (g_out,
     kt_s, v_s, x_s, qb, daa, dab, w_acc, dq_acc, dq_s, dk_acc, dv_acc, delta, p_buf, gpre, gpost, d_s, dx_s, g_acc, g_gain,
     sems, row_sems, x_sems, dx_sems, g_sem) = refs
    task, part = pl.program_id(0), pl.program_id(1)
    tasks = pl.num_programs(0)
    row = task // slots
    parts = heads // per
    width = q_ref.shape[2]
    size = width // heads
    span = slots * tile
    first, count = info[task, 0], info[task, 1]
    begins = (task == 0) & (part == 0)
    opens = (task % slots == 0) & (part == 0)

    def cols(g):
        return slice(g * tile, (g + 1) * tile)

    def keys(j):
        return pl.ds(pl.multiple_of(place[first + j] * tile, tile), tile)

    def copy(j, slot, i):
        return pltpu.make_async_copy(p_in.at[task, part, j], p_buf.at[slot, i], sems.at[slot, i])

    def row_copies():
        return (
            pltpu.make_async_copy(v_in.at[row], v_s, row_sems.at[0]),
            pltpu.make_async_copy(kt_in.at[row], kt_s, row_sems.at[1]),
        )

    def x_copy(b, slot):
        return pltpu.make_async_copy(x_in.at[row, pl.ds(pl.multiple_of(b * span, span), span), :], x_s.at[slot], x_sems.at[slot])

    def dx_copy(b, slot):
        return pltpu.make_async_copy(dx_s.at[slot], dx_out[b].at[row], dx_sems.at[slot])

    fetch = [pltpu.make_async_copy(e, g_acc, g_sem.at[0]) for e in earlier]
    copy(0, 0, 0).start()

    @pl.when(count >= 2)
    def _():
        copy(1, 0, 1).start()

    @pl.when(opens)
    def _():
        for c in row_copies():
            c.start()
        dk_acc[...] = jnp.zeros_like(dk_acc)
        dv_acc[...] = jnp.zeros_like(dv_acc)

    @pl.when(begins)
    def _():
        for f in fetch:
            f.start()
        if not fetch:
            g_acc[...] = jnp.zeros_like(g_acc)
        g_gain[...] = jnp.zeros_like(g_gain)
        gpre[...] = jnp.zeros_like(gpre)
        gpost[...] = jnp.zeros_like(gpost)

    w_acc[...] = jnp.zeros_like(w_acc)
    qf = q_ref[0].astype(F32)
    daf = da_ref[0].astype(F32)
    qt = qf.T
    dat = daf.T
    inv = inv_ref[0, 0]
    for g in range(per):
        qb[cols(g), :] = (qf * pre_wide[0, g:g + 1, :]).astype(BF16)
        inv_g = inv[:, cols(g)]
        d_g = None
        for h in range(heads):
            rows = slice(h * size, (h + 1) * size)
            scaled = dat[rows] * inv_g
            weight = post[part * per + g, h]
            daa[rows, cols(g)] = (scaled * weight).astype(BF16)
            e = jnp.sum(scaled * u_ref[0, 0, rows, cols(g)].astype(F32), axis=0, keepdims=True)
            gpost[part, g, h:h + 1, :] += e
            d_g = e * weight if d_g is None else d_g + e * weight
        delta[:, cols(g)] = d_g * inv_g
        column = jnp.broadcast_to(inv_g, (8, tile)).T[:, :1]
        dab[cols(g), :] = (daf * column * post_wide[0, g:g + 1, :]).astype(BF16)

    @pl.when(opens)
    def _():
        for c in row_copies():
            c.wait()

    def step(tiles, slot):
        vj = jnp.concatenate([v_s[keys(j), :] for j in tiles], axis=0)
        ktj = jnp.concatenate([kt_s[:, keys(j)] for j in tiles], axis=1)
        n = len(tiles)
        dv = dot(jnp.concatenate([p_buf[slot, i] for i in range(n)], axis=0), dab[...])
        for i, j in enumerate(tiles):
            dv_acc[keys(j), :] += dv[i * tile:(i + 1) * tile]
        for g in range(per):
            dp = dot(vj, daa[:, cols(g)])
            dm = []
            for i in range(n):
                dm.append((p_buf[slot, i, :, cols(g)].astype(F32) * (dp[i * tile:(i + 1) * tile] - delta[:, cols(g)])).astype(BF16))
                p_buf[slot, i, :, cols(g)] = dm[-1]
            w_acc[:, cols(g)] += dot(ktj, jnp.concatenate(dm, axis=0))
        dk = dot(jnp.concatenate([p_buf[slot, i] for i in range(n)], axis=0), qb[...])
        for i, j in enumerate(tiles):
            dk_acc[keys(j), :] += dk[i * tile:(i + 1) * tile]

    def pair(i, carry):
        slot = i % 2
        copy(2 * i, slot, 0).wait()
        copy(2 * i, slot, 1).wait()

        @pl.when(2 * i + 2 < count)
        def _():
            copy(2 * i + 2, 1 - slot, 0).start()

        @pl.when(2 * i + 3 < count)
        def _():
            copy(2 * i + 3, 1 - slot, 1).start()
        step((2 * i, 2 * i + 1), slot)
        return carry

    lax.fori_loop(0, count // 2, pair, 0)

    @pl.when(count % 2 == 1)
    def _():
        slot = (count // 2) % 2
        copy(count - 1, slot, 0).wait()
        step((count - 1,), slot)

    closes = (task % slots == slots - 1) & (part == parts - 1)

    @pl.when(closes)
    def _():
        x_copy(0, 0).start()

    for h in range(heads):
        rows = slice(h * size, (h + 1) * size)
        acc = None
        for g in range(per):
            w = w_acc[rows, cols(g)]
            term = w * (pre[h, part * per + g] * size ** -0.5)
            acc = term if acc is None else acc + term
            gpre[part, g, h:h + 1, :] += jnp.sum(w * qt[rows], axis=0, keepdims=True) * size ** -0.5
        dq_acc[rows] = jnp.where(part == 0, acc, acc + dq_acc[rows])

    @pl.when(part == parts - 1)
    def _():
        dq_s[task % slots] = dq_acc[...].T.astype(BF16)

    @pl.when(closes & (row == 0))
    def _():
        for f in fetch:
            f.wait()

    @pl.when(closes)
    def _():
        def block(b, carry):
            slot = b % 2
            x_copy(b, slot).wait()

            @pl.when(b + 1 < blocks)
            def _():
                x_copy(b + 1, 1 - slot).start()
            here = pl.ds(pl.multiple_of(b * span, span), span)
            dk, dv = dk_acc[here, :].astype(BF16), dv_acc[here, :].astype(BF16)
            normed_t = []
            for i in range(slots):
                at = slice(i * tile, (i + 1) * tile)
                x = x_s[slot, at, :].astype(F32)
                normed_t.append((x * inverse_rms(x) * gain[...]).astype(BF16).T)
                d_s[at, :] = dot_t(dk[at], w_k[...])
                d_s[at, :] += dot_t(dv[at], w_v[...])
            normed_t = jnp.concatenate(normed_t, axis=1)
            g_acc[:, width:2 * width] += dot(normed_t, dk)
            g_acc[:, 2 * width:3 * width] += dot(normed_t, dv)

            def own_tiles(action):
                for c in range(slots):
                    for i in range(slots):
                        @pl.when(info[row * slots + c, 2] == b * slots + i)
                        def _():
                            action(c, slice(i * tile, (i + 1) * tile))

            def add_queries(c, at):
                dq = dq_s[c]
                d_s[at, :] += dot_t(dq, w_q[...])
                g_acc[:, :width] += dot(normed_t[:, at], dq)

            own_tiles(add_queries)
            for i in range(slots):
                at = slice(i * tile, (i + 1) * tile)
                d = d_s[at, :]
                x = x_s[slot, at, :].astype(F32)
                s = inverse_rms(x)
                g_gain[0:1, :] += jnp.sum(d * x * s, axis=0, keepdims=True)
                y = gain[...] * d
                d_s[at, :] = s * y - x * (s * s * s * jnp.mean(y * x, axis=1, keepdims=True))

            def add_middle(c, at):
                d_s[at, :] += mid_ref[c]

            own_tiles(add_middle)

            @pl.when(b >= 2)
            def _():
                dx_copy(0, slot).wait()
            dx_s[slot] = d_s[...].astype(BF16)
            for i in range(blocks):
                @pl.when(b == i)
                def _():
                    dx_copy(i, slot).start()
            return carry

        lax.fori_loop(0, blocks, block, 0)
        for slot in range(min(2, blocks)):
            dx_copy(0, slot).wait()

    @pl.when((task == tasks - 1) & (part == parts - 1))
    def _():
        lanes = g_acc.shape[1] - 3 * width
        both = jnp.concatenate((g_gain[0:1, :], gain_grad[...], jnp.zeros((6, width), F32)), axis=0)
        g_acc[:, 3 * width:] += jnp.concatenate((both.T, jnp.zeros((width, lanes - 8), F32)), axis=1)
        line = lax.broadcasted_iota(jnp.int32, (share, lanes), 0)
        mixes = jnp.zeros((share, lanes), F32)
        for n, grads in enumerate((gpre, gpost)):
            for g in range(heads):
                summed = jnp.sum(grads[g // per, g % per], axis=1, keepdims=True)
                at = n * heads + g
                vector = jnp.concatenate((jnp.zeros((2 + heads * (at // share), 1), F32), summed), axis=0)
                vector = jnp.concatenate((vector, jnp.zeros((lanes - vector.shape[0], 1), F32)), axis=0)
                spread = jnp.broadcast_to(vector, (lanes, lanes)).T[:1]
                mixes = jnp.where(line == at % share, mixes + spread, mixes)
        for d in range(width // share):
            g_acc[d * share:(d + 1) * share, 3 * width:] += mixes
        store = pltpu.make_async_copy(g_acc, g_out, g_sem.at[0])
        store.start()
        store.wait()


def widened(pre, post, width):
    heads = pre.shape[0]
    size = width // heads
    parts = heads // PER
    pre_wide = jnp.repeat(pre.T * size ** -0.5, size, axis=1).reshape(parts, PER, width)
    return pre_wide, jnp.repeat(post, size, axis=1).reshape(parts, PER, width)


def backward(info, place, pre, post, pre_wide, post_wide, gain, gain_grad, share, w_q, w_k, w_v, q, da, d_mid, wave, kt, v, x, u, inv, p, earlier, tile):
    tasks, _, width = q.shape
    rows, row_len, _ = v.shape
    heads = pre.shape[0]
    parts = heads // PER
    tiles = row_len // tile
    wide = PER * tile
    slots = tasks // rows
    span = slots * tile
    blocks = row_len // span
    task_spec = pl.BlockSpec((1, tile, width), lambda t, p: (t, 0, 0), pipeline_mode=ONCE)
    mix_spec = pl.BlockSpec((1, PER, width), lambda t, p: (p, 0, 0))
    vector = pl.BlockSpec((1, width), lambda t, p: (0, 0))
    whole = pl.BlockSpec((width, width), lambda t, p: (0, 0), pipeline_mode=ONCE)
    pairs = tasks * tiles // 2
    out = pl.pallas_call(
        functools.partial(backward_kernel, tile, heads, PER, slots, blocks, len(earlier), share),
        grid=(tasks, parts),
        in_specs=[
            SMEM, SMEM, SMEM, SMEM,
            vector, vector, whole, whole, whole,
            task_spec,
            pl.BlockSpec((1, tile, width), lambda t, p: (wave * tasks + t, 0, 0), pipeline_mode=ONCE),
            pl.BlockSpec((slots, tile, width), lambda t, p: (wave * rows + t // slots, 0, 0), pipeline_mode=ONCE),
            pl.BlockSpec((1, 1, width, wide), lambda t, p: (t, p, 0, 0)),
            pl.BlockSpec((1, 1, 1, wide), lambda t, p: (t, p, 0, 0)),
            mix_spec, mix_spec, ANY, ANY, ANY, ANY,
        ] + [ANY] * len(earlier),
        out_specs=[ANY] * (blocks + 1),
        out_shape=[jax.ShapeDtypeStruct((rows, span, width), BF16)] * blocks + [
            jax.ShapeDtypeStruct((width, 3 * width + 128), F32),
        ],
        scratch_shapes=[
            pltpu.VMEM((width, row_len), BF16),
            pltpu.VMEM((row_len, width), BF16),
            pltpu.VMEM((2, span, width), BF16),
            pltpu.VMEM((wide, width), BF16),
            pltpu.VMEM((width, wide), BF16),
            pltpu.VMEM((wide, width), BF16),
            pltpu.VMEM((width, wide), F32),
            pltpu.VMEM((width, tile), F32),
            pltpu.VMEM((slots, tile, width), BF16),
            pltpu.VMEM((row_len, width), F32),
            pltpu.VMEM((row_len, width), F32),
            pltpu.VMEM((1, wide), F32),
            pltpu.VMEM((2, 2, tile, wide), BF16),
            pltpu.VMEM((parts, PER, heads, tile), F32),
            pltpu.VMEM((parts, PER, heads, tile), F32),
            pltpu.VMEM((span, width), F32),
            pltpu.VMEM((2, span, width), BF16),
            pltpu.VMEM((width, 3 * width + 128), F32),
            pltpu.VMEM((8, width), F32),
            pltpu.SemaphoreType.DMA((2, 2)),
            pltpu.SemaphoreType.DMA((2,)),
            pltpu.SemaphoreType.DMA((2,)),
            pltpu.SemaphoreType.DMA((2,)),
            pltpu.SemaphoreType.DMA((1,)),
        ],
        compiler_params=pltpu.CompilerParams(vmem_limit_bytes=63 * MIB),
        cost_estimate=pl.CostEstimate(flops=pairs * 8 * heads * width * tile * tile // 10, bytes_accessed=4 * MIB, transcendentals=0),
        name="attention_backward",
    )(info, place, pre, post, gain, gain_grad, w_q, w_k, w_v, q, da, d_mid, u, inv, pre_wide, post_wide, p, kt, v, x, *earlier)
    return out[:blocks], out[blocks]


def swap(value, axis, bit):
    return lax.ppermute(value, axis, [(i, i ^ bit) for i in range(lax.axis_size(axis))])


def bits_of(axis):
    return [1 << b for b in range(lax.axis_size(axis).bit_length() - 1)]


def gather_pieces(block):
    masks, pieces = [0], [block]
    for bit in reversed(bits_of("blk")):
        pieces = pieces + [swap(piece, "blk", bit) for piece in pieces]
        masks = masks + [m ^ bit for m in masks]
    return pieces, masks


class Scatter:
    def __init__(self, parts, masks, stages):
        self.held = dict(zip(masks, parts))
        self.stages = list(stages)

    def send(self):
        self.every = sum(self.stages.pop(0))
        self.came = {m: swap(v.astype(BF16), "blk", m & self.every) for m, v in sorted(self.held.items()) if m & self.every}

    def await_(self, *until):
        self.came = {m: after(v, *until) for m, v in self.came.items()}

    def pending(self):
        return list(self.came.values())

    def receive(self):
        came = self.came
        kept = {m: v for m, v in self.held.items() if not m & self.every}
        self.held = {k: sum([v.astype(F32) for m, v in came.items() if m & ~self.every == k], kept[k].astype(F32)) for k in kept}


class Chain:
    def __init__(self, grad, stages):
        self.circle = lax.axis_size("blk")
        self.world = self.circle * lax.axis_size("dp")
        self.bits = [1 << b for b in reversed(range(self.world.bit_length() - 1))]
        listed = [[b * self.circle if axis == "dp" else b for axis, b in stage] for stage in stages]
        rest = [b for b in reversed(self.bits) if not any(b in stage for stage in listed)]
        self.stages = listed + [rest[i:i + 2] for i in range(0, len(rest), 2)]
        self.shape = (grad.shape[0] // self.world,) + grad.shape[1:]
        self.held = grad.reshape((2,) * len(self.bits) + self.shape)

    def send(self):
        stage = self.stages.pop(0)
        own = lax.axis_index("dp") * self.circle + lax.axis_index("blk")

        def piece(flips):
            picked = self.held
            for bit, flip in zip(stage, flips):
                at = places[bit]
                side = (own // bit) % 2
                picked = lax.dynamic_slice_in_dim(picked, 1 - side if flip else side, 1, at)
            return picked.reshape(left)

        places = {bit: self.bits.index(bit) for bit in stage}
        remaining = [b for b in self.bits if b not in stage]
        left = (2,) * len(remaining) + self.shape
        self.terms, self.sent = [], []
        for n in range(1 << len(stage)):
            flips = [(n >> i) & 1 for i in range(len(stage))]
            mask = sum(bit for bit, flip in zip(stage, flips) if flip)
            term = piece(flips)
            if mask:
                pairs = [(i, i ^ mask) for i in range(self.world)]
                self.sent.append(term.astype(BF16))
                term = lax.ppermute(self.sent[-1], ("dp", "blk"), pairs)
            self.terms.append(term)
        self.bits = remaining

    def halves(self, at, stages):
        made = []
        for cut, order in zip((slice(None, at), slice(at, None)), stages):
            part = object.__new__(Chain)
            part.circle, part.world, part.bits = self.circle, self.world, list(self.bits)
            part.stages = [[b * self.circle if axis == "dp" else b for axis, b in stage] for stage in order]
            part.held = self.held[..., cut]
            part.shape = part.held.shape[len(self.bits):]
            made.append(part)
        return made

    def await_(self, *until):
        self.terms = self.terms[:1] + [after(term, *until) for term in self.terms[1:]]

    def pending(self):
        return self.terms[1:]

    def receive(self):
        total = self.terms[0].astype(F32)
        for term in self.terms[1:]:
            total = total + term.astype(F32)
        self.held = total.astype(BF16) if self.stages else total


class Exchange(Chain):
    def send(self):
        if len(self.stages) > 1:
            return super().send()
        self.stages = []
        groups = lax.axis_size("dp")
        self.terms = lax.all_to_all(self.held.reshape((groups,) + self.shape), "dp", 0, 0, tiled=True)

    def await_(self, *until):
        if isinstance(self.terms, list):
            return super().await_(*until)
        self.terms = after(self.terms, *until)

    def pending(self):
        return super().pending() if isinstance(self.terms, list) else [self.terms]

    def receive(self):
        if isinstance(self.terms, list):
            return super().receive()
        self.held = jnp.sum(self.terms.astype(F32), axis=0)


class Plan:
    def __init__(self, rows, span, circle):
        self.tile = min(256, span)
        self.rows, self.circle = rows, circle
        self.slots = span // self.tile
        self.tiles = self.slots * circle
        self.groups = {}
        for r in range(rows):
            for c in range(self.slots):
                route = tuple((b, self.worker(r, b * self.slots + c)) for b in range(circle))
                self.groups.setdefault(route, []).append((r, c))

    def worker(self, r, tile):
        lap, place = divmod(tile, self.circle)
        return place if (lap + r * (self.slots % 2)) % 2 == 0 else self.circle - 1 - place

    def table(self):
        found = [[[0] * self.circle for _ in range(self.slots)] for _ in range(self.rows)]
        for route, places in self.groups.items():
            for r, c in places:
                for b, d in route:
                    found[r][c][d] = b * self.slots + c
        return found

    def spots(self):
        found = {}
        for n, places in enumerate(self.groups.values()):
            for i, place in enumerate(places):
                found[place] = (n, i)
        return [found[r, c] for r in range(self.rows) for c in range(self.slots)]

    def move(self, tiles, back=False):
        out = []
        for route, piece in zip(self.groups, tiles):
            pairs = [(d, b) for b, d in route] if back else list(route)
            out.append(lax.ppermute(piece, "blk", pairs) if any(b != d for b, d in pairs) else piece)
        return out


def after(value, *others):
    return lax.optimization_barrier((value,) + others)[0]


def shards(
    inputs,
    doc_lengths,
    norm1_gain,
    w_query,
    w_key,
    w_value,
    head_mix_pre,
    head_mix_post,
    w_attn_out,
    norm2_gain,
    w_ff_in,
    w_ff_out,
    out_cotangent,
):
    rows, span, width = inputs.shape
    circle = lax.axis_size("blk")
    own = lax.axis_index("blk")
    plan = Plan(rows, span, circle)
    tile, slots, tiles = plan.tile, plan.slots, plan.tiles
    tasks = rows * slots
    waves = 2 if rows % 2 == 0 else 1
    rows_w, tasks_w = rows // waves, tasks // waves
    gain_one, gain_two = norm1_gain[None], norm2_gain[None]

    single = jnp.argmax(jnp.max(doc_lengths, axis=1)).astype(jnp.int32)
    every_row = jnp.arange(rows, dtype=jnp.int32)
    order = (every_row + single) % rows
    doc_lengths = doc_lengths[order]

    def take(array, n):
        picked = [lax.dynamic_index_in_dim(array, (single + r) % rows, 0, keepdims=True) for r in n]
        return picked[0] if len(picked) == 1 else jnp.concatenate(picked, axis=0)

    first_pieces, masks = gather_pieces(take(inputs, range(rows_w)))
    gathered = [first_pieces]
    for w in range(1, waves):
        block = after(take(inputs, range(w * rows_w, (w + 1) * rows_w)), *first_pieces)
        gathered.append([swap(block, "blk", m) if m else block for m in masks])

    place_of = [0] * circle
    for p, m in enumerate(masks):
        place_of[m] = p
    every = jnp.arange(tiles, dtype=jnp.int32)
    place = jnp.array(place_of, jnp.int32)[every // slots ^ own] * slots + every % slots
    work = jnp.array(plan.table(), jnp.int32)[:, :, own]
    bounds = jnp.cumsum(doc_lengths, axis=1)
    begin = jnp.max(jnp.where(bounds[:, None, :] <= work[:, :, None] * tile, bounds[:, None, :], 0), axis=2) // tile
    info = jnp.stack((begin, work - begin + 1, place[work]), axis=2).reshape(tasks, 3).astype(jnp.int32)
    infos = [info[w * tasks_w:(w + 1) * tasks_w] for w in range(waves)]

    pre_wide, post_wide = widened(head_mix_pre, head_mix_post, width)
    no_gain = jnp.zeros((1, width), F32)
    infos[0] = after(infos[0], pre_wide, post_wide, no_gain, *infos[1:])
    ahead = []
    for w in range(waves):
        if w == waves - 1:
            source = take(after(out_cotangent, *[a[0] for a in ahead]), range(rows)).reshape(rows, slots, tile, width)
            cotangent = plan.move([jnp.stack([source[r, c] for r, c in places]) for places in plan.groups.values()])
        info_w = after(infos[w], ahead[-1][0]) if w else infos[w]
        ahead.append(forward(info_w, place, head_mix_pre, head_mix_post, gain_one, w_query, w_key, w_value, gathered[w], tile))

    cotangent = [after(c, *[a[0] for a in ahead]) for c in cotangent]
    spots = plan.spots()
    *output, d_attended, d_middle, grad_across, grad_along, grad_gain_two = feed_forward(
        gain_two, w_attn_out, w_ff_in, w_ff_out,
        [a[4].reshape(tasks_w * tile, width) for a in ahead], [a[0].reshape(tasks_w * tile, width) for a in ahead], cotangent, spots,
    )
    d_attended = d_attended.reshape(tasks, tile, width)
    d_middle = d_middle.reshape(tasks, tile, width)

    def restore(listed):
        if rows == 2:
            return jnp.stack([jnp.where(single == 0, listed[r], listed[1 - r]) for r in range(2)])
        array = jnp.stack(listed)
        return array[(every_row - single) % rows]

    blk, dp = [("blk", b) for b in bits_of("blk")], [("dp", b) for b in bits_of("dp")]
    chains = [Exchange(grad_across, [blk[i:i + 2] for i in range(0, len(blk), 2)] + [dp])]
    for chain in chains:
        chain.send()
    along = lax.psum_scatter(grad_along, ("dp", "blk"), scatter_dimension=0, tiled=True)
    output = plan.move(output, back=True)
    heads = head_mix_pre.shape[0]
    devices = lax.axis_size("dp") * circle
    share = width // devices
    input_rows, earlier = [], []
    for w in range(waves):
        attended, sums, inverse, queries, x_own, probs, values, keys_t, x_all = ahead[w]
        info_w = infos[w]
        if w:
            info_w = after(info_w, *earlier, *output, *[chain.held for chain in chains])
        last = w == waves - 1
        d_x, grad_qkv = backward(
            info_w, place, head_mix_pre, head_mix_post, pre_wide, post_wide, gain_one, grad_gain_two if last else no_gain, share,
            w_query, w_key, w_value, queries, d_attended, d_middle, w, keys_t, values, x_all, sums, inverse, probs, earlier, tile,
        )
        if not last:
            output = [after(o, grad_qkv) for o in output]
        for pending in chains + input_rows:
            pending.await_(grad_qkv, *([] if last else output))
        if not last:
            for pending in chains + input_rows:
                pending.receive()
        earlier = [grad_qkv]
        input_rows.append(Scatter(d_x, masks, [[b] for b in bits_of("blk")] if last else [bits_of("blk")]))
        if not last:
            for pending in chains + input_rows:
                pending.send()
    for pending in chains + input_rows[:-1]:
        grad_qkv = after(grad_qkv, *pending.pending())
    grad_qkv, along = lax.optimization_barrier((grad_qkv, along))
    qkv = Chain(grad_qkv, [blk[:1]])
    for pending in [qkv, input_rows[-1]]:
        pending.send()
        pending.receive()
    rest = [[b] for b in blk[1:] + dp[2:]]
    halves = qkv.halves(2 * width - 3 * 128, [[[b] for b in dp[:2]] + rest, [[b] for b in dp[1::-1]] + rest])
    input_rows[-1].send()
    for half in halves:
        half.send()
    sent = [s for half in halves for s in half.sent]
    for pending in chains + input_rows[:-1]:
        pending.await_(*sent)
        pending.receive()
        while pending.stages:
            pending.send()
            pending.receive()
    spots = dict(zip([(r, c) for r in range(rows) for c in range(slots)], spots))
    output = [after(o, *sent) for o in output]
    output = restore([jnp.concatenate([output[spots[r, c][0]][spots[r, c][1]] for c in range(slots)]) for r in range(rows)])
    across = chains[0].held
    inner = w_ff_in.shape[1]
    across = (across[:, :inner], across[:, inner:])
    ready = [pending.held[0].astype(BF16) for pending in input_rows[:-1]]
    for half in halves:
        half.receive()
    while any(half.stages for half in halves):
        for half in halves:
            half.send()
        for half in halves:
            half.receive()
    final = input_rows[-1]
    final.receive()
    while final.stages:
        final.send()
        final.receive()
    input_grad = restore([v[r] for v in ready + [final.held[0].astype(BF16)] for r in range(rows_w)])
    total = jnp.concatenate([half.held for half in halves], axis=1)
    side = total[:, 3 * width:]
    mix_grads = [[side[at % share, 2 + heads * (at // share):][:heads] for at in range(n * heads, (n + 1) * heads)] for n in range(2)]
    return (
        output,
        input_grad,
        side[:, 0],
        total[:, :width],
        total[:, width:2 * width],
        total[:, 2 * width:3 * width],
        jnp.stack(mix_grads[0], axis=1),
        jnp.stack(mix_grads[1]),
        across[1],
        side[:, 1],
        across[0],
        along,
    )


def solution(mesh):
    tokens = P("dp", "blk", None)
    split = P(("dp", "blk"), None)
    in_specs = (tokens, P("dp", None)) + (P(),) * 10 + (tokens,)
    out_specs = (tokens, tokens, P(("dp", "blk")), split, split, split, P(), P(), split, P(("dp", "blk")), split, split)
    return jax.shard_map(shards, mesh=mesh, in_specs=in_specs, out_specs=out_specs, check_vma=False)
```

```python
import functools

import jax
import jax.numpy as jnp
from jax import lax
from jax.experimental import pallas as pl
from jax.experimental.pallas import tpu as pltpu
from jax.sharding import PartitionSpec as P

F32 = jnp.float32
BF16 = jnp.bfloat16
EPSILON = 1e-06
MASKED = -1e30
PER = 6
MIB = 2 ** 20
ONCE = pl.Buffered(1)
SMEM = pl.BlockSpec(memory_space=pltpu.SMEM)
ANY = pl.BlockSpec(memory_space=pl.ANY)


def dot(a, b):
    return jnp.dot(a, b, preferred_element_type=F32)


def dot_t(a, b):
    return lax.dot_general(a, b, (((1,), (1,)), ((), ())), preferred_element_type=F32)


def t_dot(a, b):
    return lax.dot_general(a, b, (((0,), (0,)), ((), ())), preferred_element_type=F32)


def inverse_rms(values):
    return lax.rsqrt(jnp.mean(values * values, axis=-1, keepdims=True) + EPSILON)


def forward_kernel(tile, heads, per, slots, count_pieces, info, place, pre, post, gain, w_q, w_k, w_v, *refs):
    pieces = refs[:count_pieces]
    (att_ref, u_ref, inv_ref, q_ref, own_ref, p_out, v_out, kt_out, x_out,
     x_s, k_s, v_s, kt_s, vt_s, qa, s_all, u_acc, att_acc, top, mass, p_buf, sems, row_sems) = refs[count_pieces:]
    task, part = pl.program_id(0), pl.program_id(1)
    row = task // slots
    parts = heads // per
    width = q_ref.shape[2]
    size = width // heads
    first, count, spot = info[task, 0], info[task, 1], info[task, 2]
    span = pieces[0].shape[1]

    def row_copies():
        return (
            pltpu.make_async_copy(v_s, v_out.at[row], row_sems.at[0]),
            pltpu.make_async_copy(kt_s, kt_out.at[row], row_sems.at[1]),
            pltpu.make_async_copy(x_s, x_out.at[row], row_sems.at[2]),
        )

    @pl.when((task % slots == 0) & (part == 0))
    def _():
        for i, piece in enumerate(pieces):
            for c in range(span // tile):
                at = slice(i * span + c * tile, i * span + (c + 1) * tile)
                low = piece[0, c * tile:(c + 1) * tile, :]
                x_s[at, :] = low
                x = low.astype(F32)
                normed = (x * inverse_rms(x) * gain[...]).astype(BF16)
                k = dot(normed, w_k[...]).astype(BF16)
                k_s[at, :] = k
                kt_s[:, at] = k.T
                v = dot(normed, w_v[...]).astype(BF16)
                v_s[at, :] = v
                vt_s[:, at] = v.T
        for c in row_copies():
            c.start()

    @pl.when(part == 0)
    def _():
        low = x_s[pl.ds(pl.multiple_of(spot * tile, tile), tile), :]
        own_ref[0] = low
        x = low.astype(F32)
        normed = (x * inverse_rms(x) * gain[...]).astype(BF16)
        q_ref[0] = dot(normed, w_q[...]).astype(BF16)

    qt = q_ref[0].astype(F32).T
    for g in range(per):
        for h in range(heads):
            rows = slice(h * size, (h + 1) * size)
            qa[rows, g * tile:(g + 1) * tile] = (qt[rows] * (pre[h, part * per + g] * size ** -0.5)).astype(BF16)

    def cols(g):
        return slice(g * tile, (g + 1) * tile)

    def keys(j):
        return pl.ds(pl.multiple_of(place[first + j] * tile, tile), tile)

    causal = lax.broadcasted_iota(jnp.int32, (tile, tile), 0) <= lax.broadcasted_iota(jnp.int32, (tile, tile), 1)
    twos, odd = count // 2, count % 2
    top[...] = jnp.full_like(top, MASKED)

    def scores(tiles, masked):
        kj = jnp.concatenate([k_s[keys(j), :] for j in tiles], axis=0)
        for g in range(per):
            s = dot(kj, qa[:, cols(g)])
            best = top[:, cols(g)]
            for i, j in enumerate(tiles):
                part_s = s[i * tile:(i + 1) * tile]
                if masked and i == len(tiles) - 1:
                    part_s = jnp.where(causal, part_s, MASKED)
                s_all[j, :, cols(g)] = part_s
                best = jnp.maximum(best, jnp.max(part_s, axis=0, keepdims=True))
            top[:, cols(g)] = best

    def score_pair(i, carry):
        scores((2 * i, 2 * i + 1), False)
        return carry

    lax.fori_loop(0, twos - 1 + odd, score_pair, 0)

    @pl.when(odd == 0)
    def _():
        scores((count - 2, count - 1), True)

    @pl.when(odd == 1)
    def _():
        scores((count - 1,), True)

    u_acc[...] = jnp.zeros_like(u_acc)
    mass[...] = jnp.zeros_like(mass)

    def copy(j, slot, i):
        return pltpu.make_async_copy(p_buf.at[slot, i], p_out.at[task, part, j], sems.at[slot, i])

    def sums(tiles, slot):
        vj = jnp.concatenate([vt_s[:, keys(j)] for j in tiles], axis=1)
        for g in range(per):
            low, weight = [], mass[:, cols(g)]
            for i, j in enumerate(tiles):
                p = jnp.exp(s_all[j, :, cols(g)] - top[:, cols(g)])
                weight = weight + jnp.sum(p, axis=0, keepdims=True)
                low.append(p.astype(BF16))
                p_buf[slot, i, :, cols(g)] = low[-1]
            mass[:, cols(g)] = weight
            u_acc[:, cols(g)] += dot(vj, jnp.concatenate(low, axis=0))
        for i, j in enumerate(tiles):
            copy(j, slot, i).start()

    def sum_pair(i, carry):
        slot = i % 2

        @pl.when(i >= 2)
        def _():
            copy(0, slot, 0).wait()
            copy(0, slot, 1).wait()
        sums((2 * i, 2 * i + 1), slot)
        return carry

    lax.fori_loop(0, twos, sum_pair, 0)

    @pl.when(odd == 1)
    def _():
        @pl.when(twos >= 2)
        def _():
            copy(0, twos % 2, 0).wait()
            copy(0, twos % 2, 1).wait()
        sums((count - 1,), twos % 2)

    inv = 1.0 / mass[...]
    inv_ref[0, 0] = inv
    u_ref[0, 0] = u_acc[...].astype(BF16)
    for h in range(heads):
        rows = slice(h * size, (h + 1) * size)
        acc = None
        for g in range(per):
            term = u_acc[rows, cols(g)] * (inv[:, cols(g)] * post[part * per + g, h])
            acc = term if acc is None else acc + term
        att_acc[rows] = jnp.where(part == 0, acc, acc + att_acc[rows])

    @pl.when(part == parts - 1)
    def _():
        att_ref[0] = att_acc[...].T.astype(BF16)

    @pl.when(twos >= 1)
    def _():
        copy(0, (twos - 1) % 2, 0).wait()
        copy(0, (twos - 1) % 2, 1).wait()

    @pl.when(odd == 1)
    def _():
        copy(0, twos % 2, 0).wait()

    @pl.when((odd == 0) & (twos >= 2))
    def _():
        copy(0, twos % 2, 0).wait()
        copy(0, twos % 2, 1).wait()

    @pl.when((task % slots == slots - 1) & (part == parts - 1))
    def _():
        for c in row_copies():
            c.wait()


def forward(info, place, pre, post, gain, w_q, w_k, w_v, pieces, tile):
    rows, span, width = pieces[0].shape
    row_len = span * len(pieces)
    heads = pre.shape[0]
    parts = heads // PER
    wide = PER * tile
    slots = span // tile
    tasks = rows * slots
    tiles = row_len // tile
    whole = pl.BlockSpec((width, width), lambda t, p: (0, 0), pipeline_mode=ONCE)
    task_spec = pl.BlockSpec((1, tile, width), lambda t, p: (t, 0, 0))
    pairs = tasks * tiles // 2
    return pl.pallas_call(
        functools.partial(forward_kernel, tile, heads, PER, slots, len(pieces)),
        grid=(tasks, parts),
        in_specs=[SMEM] * 4
        + [pl.BlockSpec((1, width), lambda t, p: (0, 0)), whole, whole, whole]
        + [pl.BlockSpec((1, span, width), lambda t, p: (t // slots, 0, 0), pipeline_mode=ONCE)] * len(pieces),
        out_specs=[
            task_spec,
            pl.BlockSpec((1, 1, width, wide), lambda t, p: (t, p, 0, 0)),
            pl.BlockSpec((1, 1, 1, wide), lambda t, p: (t, p, 0, 0)),
            task_spec, task_spec, ANY, ANY, ANY, ANY,
        ],
        out_shape=[
            jax.ShapeDtypeStruct((tasks, tile, width), BF16),
            jax.ShapeDtypeStruct((tasks, parts, width, wide), BF16),
            jax.ShapeDtypeStruct((tasks, parts, 1, wide), F32),
            jax.ShapeDtypeStruct((tasks, tile, width), BF16),
            jax.ShapeDtypeStruct((tasks, tile, width), BF16),
            jax.ShapeDtypeStruct((tasks, parts, tiles, tile, wide), BF16),
            jax.ShapeDtypeStruct((rows, row_len, width), BF16),
            jax.ShapeDtypeStruct((rows, width, row_len), BF16),
            jax.ShapeDtypeStruct((rows, row_len, width), BF16),
        ],
        scratch_shapes=[
            pltpu.VMEM((row_len, width), BF16),
            pltpu.VMEM((row_len, width), BF16),
            pltpu.VMEM((row_len, width), BF16),
            pltpu.VMEM((width, row_len), BF16),
            pltpu.VMEM((width, row_len), BF16),
            pltpu.VMEM((width, wide), BF16),
            pltpu.VMEM((tiles, tile, wide), F32),
            pltpu.VMEM((width, wide), F32),
            pltpu.VMEM((width, tile), F32),
            pltpu.VMEM((1, wide), F32),
            pltpu.VMEM((1, wide), F32),
            pltpu.VMEM((2, 2, tile, wide), BF16),
            pltpu.SemaphoreType.DMA((2, 2)),
            pltpu.SemaphoreType.DMA((3,)),
        ],
        compiler_params=pltpu.CompilerParams(vmem_limit_bytes=60 * MIB),
        cost_estimate=pl.CostEstimate(flops=pairs * 4 * heads * width * tile * tile // 10, bytes_accessed=4 * MIB, transcendentals=0),
        name="attention_forward",
    )(info, place, pre, post, gain, w_q, w_k, w_v, *pieces)


def feed_forward_kernel(waves, spots, gain, w_out, w_in_ref, w_back_ref, *refs):
    routes = 1 + max(route for route, _ in spots)
    own, att, cot = refs[:waves], refs[waves:2 * waves], refs[2 * waves:2 * waves + routes]
    out_refs, refs = refs[2 * waves + routes:2 * waves + 2 * routes], refs[2 * waves + 2 * routes:]
    (d_att_ref, d_mid_ref, g_in_ref, g_back_ref, g_gain_ref,
     mid, n_two, n_two_t, cot_s, out_acc, d_acc, act_s, dh_s) = refs
    step_tokens = cot[0].shape[1]
    step, steps = pl.program_id(0), pl.num_programs(0)
    tokens, width = mid.shape
    each = tokens // waves

    @pl.when(step == 0)
    def _():
        for w in range(waves):
            for b in range(0, each, step_tokens):
                at, to = slice(b, b + step_tokens), slice(w * each + b, w * each + b + step_tokens)
                m = own[w][at, :].astype(F32) + dot(att[w][at, :], w_out[...])
                mid[to, :] = m
                n = (m * inverse_rms(m) * gain[...]).astype(BF16)
                n_two[to, :] = n
                n_two_t[:, to] = n.T
                route, n = spots[(w * each + b) // step_tokens]
                cot_s[to, :] = cot[route][n]
        out_acc[...] = jnp.zeros_like(out_acc)
        d_acc[...] = jnp.zeros_like(d_acc)

    root = (2.0 / 3.141592653589793) ** 0.5

    @pl.when(step < steps - 1)
    def _():
        w_in, w_back = w_in_ref[...], w_back_ref[...]
        for b in range(0, tokens, step_tokens):
            at = slice(b, b + step_tokens)
            v = dot(n_two[at, :], w_in)
            d_active = dot_t(cot_s[at, :], w_back)
            square = v * v
            t = jnp.tanh(root * v * (1.0 + 0.044715 * square))
            half = 0.5 + 0.5 * t
            act = (v * half).astype(BF16)
            slope = half + (0.5 * root) * v * (1.0 - t * t) * (1.0 + (3 * 0.044715) * square)
            d_hidden = (slope * d_active).astype(BF16)
            act_s[at, :] = act
            dh_s[at, :] = d_hidden
            out_acc[at, :] += dot(act, w_back)
            d_acc[at, :] += dot_t(d_hidden, w_in)
        g_back_ref[...] = t_dot(act_s[...], cot_s[...])
        g_in_ref[...] = dot(n_two_t[...], dh_s[...]).astype(BF16)

    @pl.when(step == steps - 1)
    def _():
        total, grad_gain = None, None
        for w in range(waves):
            for b in range(0, each, step_tokens):
                at, to = slice(b, b + step_tokens), slice(w * each + b, w * each + b + step_tokens)
                m = mid[to, :]
                route, n = spots[(w * each + b) // step_tokens]
                out_refs[route][n] = (m + out_acc[to, :]).astype(BF16)
                d = d_acc[to, :]
                r = inverse_rms(m)
                part = jnp.sum(d * m * r, axis=0, keepdims=True)
                grad_gain = part if grad_gain is None else grad_gain + part
                z = gain[...] * d
                d_mid = cot_s[to, :].astype(F32) + r * z - m * (r * r * r * jnp.mean(z * m, axis=1, keepdims=True))
                d_mid_ref[to, :] = d_mid
                branch = d_mid.astype(BF16)
                d_att_ref[to, :] = dot_t(branch, w_out[...]).astype(BF16)
                part = t_dot(att[w][at, :], branch)
                total = part if total is None else total + part
        g_in_ref[...] = total.astype(BF16)
        g_gain_ref[...] = grad_gain


def feed_forward(gain, w_out, w_in, w_back, own, att, cot, spots):
    waves = len(own)
    each, width = own[0].shape
    tokens = waves * each
    inner = w_in.shape[1]
    chunks = inner // width
    rows = pl.BlockSpec((each, width), lambda i: (0, 0), pipeline_mode=ONCE)
    full = pl.BlockSpec((tokens, width), lambda i: (0, 0))
    vector = pl.BlockSpec((1, width), lambda i: (0, 0))
    across = pl.BlockSpec((width, width), lambda i: (0, jnp.minimum(i, chunks - 1)))
    along = pl.BlockSpec((width, width), lambda i: (jnp.minimum(i, chunks - 1), 0))
    return pl.pallas_call(
        functools.partial(feed_forward_kernel, waves, spots),
        grid=(chunks + 1,),
        in_specs=[vector, pl.BlockSpec((width, width), lambda i: (0, 0), pipeline_mode=ONCE), across, along]
        + [rows] * (2 * waves) + [pl.BlockSpec(c.shape, lambda i: (0, 0, 0), pipeline_mode=ONCE) for c in cot],
        out_specs=[pl.BlockSpec(c.shape, lambda i: (0, 0, 0)) for c in cot]
        + [full, full, pl.BlockSpec((width, width), lambda i: (0, i)), along, vector],
        out_shape=[jax.ShapeDtypeStruct(c.shape, BF16) for c in cot] + [
            jax.ShapeDtypeStruct((tokens, width), BF16),
            jax.ShapeDtypeStruct((tokens, width), F32),
            jax.ShapeDtypeStruct((width, inner + width), BF16),
            jax.ShapeDtypeStruct((inner, width), F32),
            jax.ShapeDtypeStruct((1, width), F32),
        ],
        scratch_shapes=[
            pltpu.VMEM((tokens, width), F32),
            pltpu.VMEM((tokens, width), BF16),
            pltpu.VMEM((width, tokens), BF16),
            pltpu.VMEM((tokens, width), BF16),
            pltpu.VMEM((tokens, width), F32),
            pltpu.VMEM((tokens, width), F32),
            pltpu.VMEM((tokens, width), BF16),
            pltpu.VMEM((tokens, width), BF16),
        ],
        compiler_params=pltpu.CompilerParams(vmem_limit_bytes=60 * MIB),
        cost_estimate=pl.CostEstimate(flops=tokens * width * (12 * inner + 6 * width), bytes_accessed=40 * MIB, transcendentals=0),
        name="feed_forward",
    )(gain, w_out, w_in, w_back, *own, *att, *cot)


def backward_kernel(tile, heads, per, slots, blocks, carried, share, info, place, pre, post, gain, gain_grad, w_q, w_k, w_v, q_ref, da_ref, mid_ref, u_ref, inv_ref,
                    pre_wide, post_wide, p_in, kt_in, v_in, x_in, *refs):
    earlier, refs = refs[:carried], refs[carried:]
    dx_out, refs = refs[:blocks], refs[blocks:]
    (g_out,
     kt_s, v_s, x_s, qb, daa, dab, w_acc, dq_acc, dq_s, dk_acc, dv_acc, delta, p_buf, gpre, gpost, d_s, dx_s, g_acc, g_gain,
     sems, row_sems, x_sems, dx_sems, g_sem) = refs
    task, part = pl.program_id(0), pl.program_id(1)
    tasks = pl.num_programs(0)
    row = task // slots
    parts = heads // per
    width = q_ref.shape[2]
    size = width // heads
    span = slots * tile
    first, count = info[task, 0], info[task, 1]
    begins = (task == 0) & (part == 0)
    opens = (task % slots == 0) & (part == 0)

    def cols(g):
        return slice(g * tile, (g + 1) * tile)

    def keys(j):
        return pl.ds(pl.multiple_of(place[first + j] * tile, tile), tile)

    def copy(j, slot, i):
        return pltpu.make_async_copy(p_in.at[task, part, j], p_buf.at[slot, i], sems.at[slot, i])

    def row_copies():
        return (
            pltpu.make_async_copy(v_in.at[row], v_s, row_sems.at[0]),
            pltpu.make_async_copy(kt_in.at[row], kt_s, row_sems.at[1]),
        )

    def x_copy(b, slot):
        return pltpu.make_async_copy(x_in.at[row, pl.ds(pl.multiple_of(b * span, span), span), :], x_s.at[slot], x_sems.at[slot])

    def dx_copy(b, slot):
        return pltpu.make_async_copy(dx_s.at[slot], dx_out[b].at[row], dx_sems.at[slot])

    fetch = [pltpu.make_async_copy(e, g_acc, g_sem.at[0]) for e in earlier]
    copy(0, 0, 0).start()

    @pl.when(count >= 2)
    def _():
        copy(1, 0, 1).start()

    @pl.when(opens)
    def _():
        for c in row_copies():
            c.start()
        dk_acc[...] = jnp.zeros_like(dk_acc)
        dv_acc[...] = jnp.zeros_like(dv_acc)

    @pl.when(begins)
    def _():
        for f in fetch:
            f.start()
        if not fetch:
            g_acc[...] = jnp.zeros_like(g_acc)
        g_gain[...] = jnp.zeros_like(g_gain)
        gpre[...] = jnp.zeros_like(gpre)
        gpost[...] = jnp.zeros_like(gpost)

    w_acc[...] = jnp.zeros_like(w_acc)
    qf = q_ref[0].astype(F32)
    daf = da_ref[0].astype(F32)
    qt = qf.T
    dat = daf.T
    inv = inv_ref[0, 0]
    for g in range(per):
        qb[cols(g), :] = (qf * pre_wide[0, g:g + 1, :]).astype(BF16)
        inv_g = inv[:, cols(g)]
        d_g = None
        for h in range(heads):
            rows = slice(h * size, (h + 1) * size)
            scaled = dat[rows] * inv_g
            weight = post[part * per + g, h]
            daa[rows, cols(g)] = (scaled * weight).astype(BF16)
            e = jnp.sum(scaled * u_ref[0, 0, rows, cols(g)].astype(F32), axis=0, keepdims=True)
            gpost[part, g, h:h + 1, :] += e
            d_g = e * weight if d_g is None else d_g + e * weight
        delta[:, cols(g)] = d_g * inv_g
        column = jnp.broadcast_to(inv_g, (8, tile)).T[:, :1]
        dab[cols(g), :] = (daf * column * post_wide[0, g:g + 1, :]).astype(BF16)

    @pl.when(opens)
    def _():
        for c in row_copies():
            c.wait()

    def step(tiles, slot):
        vj = jnp.concatenate([v_s[keys(j), :] for j in tiles], axis=0)
        ktj = jnp.concatenate([kt_s[:, keys(j)] for j in tiles], axis=1)
        n = len(tiles)
        dv = dot(jnp.concatenate([p_buf[slot, i] for i in range(n)], axis=0), dab[...])
        for i, j in enumerate(tiles):
            dv_acc[keys(j), :] += dv[i * tile:(i + 1) * tile]
        for g in range(per):
            dp = dot(vj, daa[:, cols(g)])
            dm = []
            for i in range(n):
                dm.append((p_buf[slot, i, :, cols(g)].astype(F32) * (dp[i * tile:(i + 1) * tile] - delta[:, cols(g)])).astype(BF16))
                p_buf[slot, i, :, cols(g)] = dm[-1]
            w_acc[:, cols(g)] += dot(ktj, jnp.concatenate(dm, axis=0))
        dk = dot(jnp.concatenate([p_buf[slot, i] for i in range(n)], axis=0), qb[...])
        for i, j in enumerate(tiles):
            dk_acc[keys(j), :] += dk[i * tile:(i + 1) * tile]

    def pair(i, carry):
        slot = i % 2
        copy(2 * i, slot, 0).wait()
        copy(2 * i, slot, 1).wait()

        @pl.when(2 * i + 2 < count)
        def _():
            copy(2 * i + 2, 1 - slot, 0).start()

        @pl.when(2 * i + 3 < count)
        def _():
            copy(2 * i + 3, 1 - slot, 1).start()
        step((2 * i, 2 * i + 1), slot)
        return carry

    lax.fori_loop(0, count // 2, pair, 0)

    @pl.when(count % 2 == 1)
    def _():
        slot = (count // 2) % 2
        copy(count - 1, slot, 0).wait()
        step((count - 1,), slot)

    closes = (task % slots == slots - 1) & (part == parts - 1)

    @pl.when(closes)
    def _():
        x_copy(0, 0).start()

    for h in range(heads):
        rows = slice(h * size, (h + 1) * size)
        acc = None
        for g in range(per):
            w = w_acc[rows, cols(g)]
            term = w * (pre[h, part * per + g] * size ** -0.5)
            acc = term if acc is None else acc + term
            gpre[part, g, h:h + 1, :] += jnp.sum(w * qt[rows], axis=0, keepdims=True) * size ** -0.5
        dq_acc[rows] = jnp.where(part == 0, acc, acc + dq_acc[rows])

    @pl.when(part == parts - 1)
    def _():
        dq_s[task % slots] = dq_acc[...].T.astype(BF16)

    @pl.when(closes & (row == 0))
    def _():
        for f in fetch:
            f.wait()

    @pl.when(closes)
    def _():
        def block(b, carry):
            slot = b % 2
            x_copy(b, slot).wait()

            @pl.when(b + 1 < blocks)
            def _():
                x_copy(b + 1, 1 - slot).start()
            here = pl.ds(pl.multiple_of(b * span, span), span)
            dk, dv = dk_acc[here, :].astype(BF16), dv_acc[here, :].astype(BF16)
            normed_t = []
            for i in range(slots):
                at = slice(i * tile, (i + 1) * tile)
                x = x_s[slot, at, :].astype(F32)
                normed_t.append((x * inverse_rms(x) * gain[...]).astype(BF16).T)
                d_s[at, :] = dot_t(dk[at], w_k[...])
                d_s[at, :] += dot_t(dv[at], w_v[...])
            normed_t = jnp.concatenate(normed_t, axis=1)
            g_acc[:, width:2 * width] += dot(normed_t, dk)
            g_acc[:, 2 * width:3 * width] += dot(normed_t, dv)

            def own_tiles(action):
                for c in range(slots):
                    for i in range(slots):
                        @pl.when(info[row * slots + c, 2] == b * slots + i)
                        def _():
                            action(c, slice(i * tile, (i + 1) * tile))

            def add_queries(c, at):
                dq = dq_s[c]
                d_s[at, :] += dot_t(dq, w_q[...])
                g_acc[:, :width] += dot(normed_t[:, at], dq)

            own_tiles(add_queries)
            for i in range(slots):
                at = slice(i * tile, (i + 1) * tile)
                d = d_s[at, :]
                x = x_s[slot, at, :].astype(F32)
                s = inverse_rms(x)
                g_gain[0:1, :] += jnp.sum(d * x * s, axis=0, keepdims=True)
                y = gain[...] * d
                d_s[at, :] = s * y - x * (s * s * s * jnp.mean(y * x, axis=1, keepdims=True))

            def add_middle(c, at):
                d_s[at, :] += mid_ref[c]

            own_tiles(add_middle)

            @pl.when(b >= 2)
            def _():
                dx_copy(0, slot).wait()
            dx_s[slot] = d_s[...].astype(BF16)
            for i in range(blocks):
                @pl.when(b == i)
                def _():
                    dx_copy(i, slot).start()
            return carry

        lax.fori_loop(0, blocks, block, 0)
        for slot in range(min(2, blocks)):
            dx_copy(0, slot).wait()

    @pl.when((task == tasks - 1) & (part == parts - 1))
    def _():
        lanes = g_acc.shape[1] - 3 * width
        both = jnp.concatenate((g_gain[0:1, :], gain_grad[...], jnp.zeros((6, width), F32)), axis=0)
        g_acc[:, 3 * width:] += jnp.concatenate((both.T, jnp.zeros((width, lanes - 8), F32)), axis=1)
        line = lax.broadcasted_iota(jnp.int32, (share, lanes), 0)
        mixes = jnp.zeros((share, lanes), F32)
        for n, grads in enumerate((gpre, gpost)):
            for g in range(heads):
                summed = jnp.sum(grads[g // per, g % per], axis=1, keepdims=True)
                at = n * heads + g
                vector = jnp.concatenate((jnp.zeros((2 + heads * (at // share), 1), F32), summed), axis=0)
                vector = jnp.concatenate((vector, jnp.zeros((lanes - vector.shape[0], 1), F32)), axis=0)
                spread = jnp.broadcast_to(vector, (lanes, lanes)).T[:1]
                mixes = jnp.where(line == at % share, mixes + spread, mixes)
        for d in range(width // share):
            g_acc[d * share:(d + 1) * share, 3 * width:] += mixes
        store = pltpu.make_async_copy(g_acc, g_out, g_sem.at[0])
        store.start()
        store.wait()


def widened(pre, post, width):
    heads = pre.shape[0]
    size = width // heads
    parts = heads // PER
    pre_wide = jnp.repeat(pre.T * size ** -0.5, size, axis=1).reshape(parts, PER, width)
    return pre_wide, jnp.repeat(post, size, axis=1).reshape(parts, PER, width)


def backward(info, place, pre, post, pre_wide, post_wide, gain, gain_grad, share, w_q, w_k, w_v, q, da, d_mid, wave, kt, v, x, u, inv, p, earlier, tile):
    tasks, _, width = q.shape
    rows, row_len, _ = v.shape
    heads = pre.shape[0]
    parts = heads // PER
    tiles = row_len // tile
    wide = PER * tile
    slots = tasks // rows
    span = slots * tile
    blocks = row_len // span
    task_spec = pl.BlockSpec((1, tile, width), lambda t, p: (t, 0, 0), pipeline_mode=ONCE)
    mix_spec = pl.BlockSpec((1, PER, width), lambda t, p: (p, 0, 0))
    vector = pl.BlockSpec((1, width), lambda t, p: (0, 0))
    whole = pl.BlockSpec((width, width), lambda t, p: (0, 0), pipeline_mode=ONCE)
    pairs = tasks * tiles // 2
    out = pl.pallas_call(
        functools.partial(backward_kernel, tile, heads, PER, slots, blocks, len(earlier), share),
        grid=(tasks, parts),
        in_specs=[
            SMEM, SMEM, SMEM, SMEM,
            vector, vector, whole, whole, whole,
            task_spec,
            pl.BlockSpec((1, tile, width), lambda t, p: (wave * tasks + t, 0, 0), pipeline_mode=ONCE),
            pl.BlockSpec((slots, tile, width), lambda t, p: (wave * rows + t // slots, 0, 0), pipeline_mode=ONCE),
            pl.BlockSpec((1, 1, width, wide), lambda t, p: (t, p, 0, 0)),
            pl.BlockSpec((1, 1, 1, wide), lambda t, p: (t, p, 0, 0)),
            mix_spec, mix_spec, ANY, ANY, ANY, ANY,
        ] + [ANY] * len(earlier),
        out_specs=[ANY] * (blocks + 1),
        out_shape=[jax.ShapeDtypeStruct((rows, span, width), BF16)] * blocks + [
            jax.ShapeDtypeStruct((width, 3 * width + 128), F32),
        ],
        scratch_shapes=[
            pltpu.VMEM((width, row_len), BF16),
            pltpu.VMEM((row_len, width), BF16),
            pltpu.VMEM((2, span, width), BF16),
            pltpu.VMEM((wide, width), BF16),
            pltpu.VMEM((width, wide), BF16),
            pltpu.VMEM((wide, width), BF16),
            pltpu.VMEM((width, wide), F32),
            pltpu.VMEM((width, tile), F32),
            pltpu.VMEM((slots, tile, width), BF16),
            pltpu.VMEM((row_len, width), F32),
            pltpu.VMEM((row_len, width), F32),
            pltpu.VMEM((1, wide), F32),
            pltpu.VMEM((2, 2, tile, wide), BF16),
            pltpu.VMEM((parts, PER, heads, tile), F32),
            pltpu.VMEM((parts, PER, heads, tile), F32),
            pltpu.VMEM((span, width), F32),
            pltpu.VMEM((2, span, width), BF16),
            pltpu.VMEM((width, 3 * width + 128), F32),
            pltpu.VMEM((8, width), F32),
            pltpu.SemaphoreType.DMA((2, 2)),
            pltpu.SemaphoreType.DMA((2,)),
            pltpu.SemaphoreType.DMA((2,)),
            pltpu.SemaphoreType.DMA((2,)),
            pltpu.SemaphoreType.DMA((1,)),
        ],
        compiler_params=pltpu.CompilerParams(vmem_limit_bytes=63 * MIB),
        cost_estimate=pl.CostEstimate(flops=pairs * 8 * heads * width * tile * tile // 10, bytes_accessed=4 * MIB, transcendentals=0),
        name="attention_backward",
    )(info, place, pre, post, gain, gain_grad, w_q, w_k, w_v, q, da, d_mid, u, inv, pre_wide, post_wide, p, kt, v, x, *earlier)
    return out[:blocks], out[blocks]


def swap(value, axis, bit):
    return lax.ppermute(value, axis, [(i, i ^ bit) for i in range(lax.axis_size(axis))])


def bits_of(axis):
    return [1 << b for b in range(lax.axis_size(axis).bit_length() - 1)]


def gather_pieces(block):
    masks, pieces = [0], [block]
    for bit in reversed(bits_of("blk")):
        pieces = pieces + [swap(piece, "blk", bit) for piece in pieces]
        masks = masks + [m ^ bit for m in masks]
    return pieces, masks


class Scatter:
    def __init__(self, parts, masks, stages):
        self.held = dict(zip(masks, parts))
        self.stages = list(stages)

    def send(self):
        self.every = sum(self.stages.pop(0))
        self.came = {m: swap(v.astype(BF16), "blk", m & self.every) for m, v in sorted(self.held.items()) if m & self.every}

    def await_(self, *until):
        self.came = {m: after(v, *until) for m, v in self.came.items()}

    def pending(self):
        return list(self.came.values())

    def receive(self):
        came = self.came
        kept = {m: v for m, v in self.held.items() if not m & self.every}
        self.held = {k: sum([v.astype(F32) for m, v in came.items() if m & ~self.every == k], kept[k].astype(F32)) for k in kept}


class Chain:
    def __init__(self, grad, stages):
        self.circle = lax.axis_size("blk")
        self.world = self.circle * lax.axis_size("dp")
        self.bits = [1 << b for b in reversed(range(self.world.bit_length() - 1))]
        listed = [[b * self.circle if axis == "dp" else b for axis, b in stage] for stage in stages]
        rest = [b for b in reversed(self.bits) if not any(b in stage for stage in listed)]
        self.stages = listed + [rest[i:i + 2] for i in range(0, len(rest), 2)]
        self.shape = (grad.shape[0] // self.world,) + grad.shape[1:]
        self.held = grad.reshape((2,) * len(self.bits) + self.shape)

    def send(self):
        stage = self.stages.pop(0)
        own = lax.axis_index("dp") * self.circle + lax.axis_index("blk")

        def piece(flips):
            picked = self.held
            for bit, flip in zip(stage, flips):
                at = places[bit]
                side = (own // bit) % 2
                picked = lax.dynamic_slice_in_dim(picked, 1 - side if flip else side, 1, at)
            return picked.reshape(left)

        places = {bit: self.bits.index(bit) for bit in stage}
        remaining = [b for b in self.bits if b not in stage]
        left = (2,) * len(remaining) + self.shape
        self.terms, self.sent = [], []
        for n in range(1 << len(stage)):
            flips = [(n >> i) & 1 for i in range(len(stage))]
            mask = sum(bit for bit, flip in zip(stage, flips) if flip)
            term = piece(flips)
            if mask:
                pairs = [(i, i ^ mask) for i in range(self.world)]
                self.sent.append(term.astype(BF16))
                term = lax.ppermute(self.sent[-1], ("dp", "blk"), pairs)
            self.terms.append(term)
        self.bits = remaining

    def halves(self, at, stages):
        made = []
        for cut, order in zip((slice(None, at), slice(at, None)), stages):
            part = object.__new__(Chain)
            part.circle, part.world, part.bits = self.circle, self.world, list(self.bits)
            part.stages = [[b * self.circle if axis == "dp" else b for axis, b in stage] for stage in order]
            part.held = self.held[..., cut]
            part.shape = part.held.shape[len(self.bits):]
            made.append(part)
        return made

    def await_(self, *until):
        self.terms = self.terms[:1] + [after(term, *until) for term in self.terms[1:]]

    def pending(self):
        return self.terms[1:]

    def receive(self):
        total = self.terms[0].astype(F32)
        for term in self.terms[1:]:
            total = total + term.astype(F32)
        self.held = total.astype(BF16) if self.stages else total


class Exchange(Chain):
    def send(self):
        if len(self.stages) > 1:
            return super().send()
        self.stages = []
        groups = lax.axis_size("dp")
        self.terms = lax.all_to_all(self.held.reshape((groups,) + self.shape), "dp", 0, 0, tiled=True)

    def await_(self, *until):
        if isinstance(self.terms, list):
            return super().await_(*until)
        self.terms = after(self.terms, *until)

    def pending(self):
        return super().pending() if isinstance(self.terms, list) else [self.terms]

    def receive(self):
        if isinstance(self.terms, list):
            return super().receive()
        self.held = jnp.sum(self.terms.astype(F32), axis=0)


class Plan:
    def __init__(self, rows, span, circle):
        self.tile = min(256, span)
        self.rows, self.circle = rows, circle
        self.slots = span // self.tile
        self.tiles = self.slots * circle
        self.groups = {}
        for r in range(rows):
            for c in range(self.slots):
                route = tuple((b, self.worker(r, b * self.slots + c)) for b in range(circle))
                self.groups.setdefault(route, []).append((r, c))

    def worker(self, r, tile):
        lap, place = divmod(tile, self.circle)
        return place if (lap + r * (self.slots % 2)) % 2 == 0 else self.circle - 1 - place

    def table(self):
        found = [[[0] * self.circle for _ in range(self.slots)] for _ in range(self.rows)]
        for route, places in self.groups.items():
            for r, c in places:
                for b, d in route:
                    found[r][c][d] = b * self.slots + c
        return found

    def spots(self):
        found = {}
        for n, places in enumerate(self.groups.values()):
            for i, place in enumerate(places):
                found[place] = (n, i)
        return [found[r, c] for r in range(self.rows) for c in range(self.slots)]

    def move(self, tiles, back=False):
        out = []
        for route, piece in zip(self.groups, tiles):
            pairs = [(d, b) for b, d in route] if back else list(route)
            out.append(lax.ppermute(piece, "blk", pairs) if any(b != d for b, d in pairs) else piece)
        return out


def after(value, *others):
    return lax.optimization_barrier((value,) + others)[0]


def shards(
    inputs,
    doc_lengths,
    norm1_gain,
    w_query,
    w_key,
    w_value,
    head_mix_pre,
    head_mix_post,
    w_attn_out,
    norm2_gain,
    w_ff_in,
    w_ff_out,
    out_cotangent,
):
    rows, span, width = inputs.shape
    circle = lax.axis_size("blk")
    own = lax.axis_index("blk")
    plan = Plan(rows, span, circle)
    tile, slots, tiles = plan.tile, plan.slots, plan.tiles
    tasks = rows * slots
    waves = 2 if rows % 2 == 0 else 1
    rows_w, tasks_w = rows // waves, tasks // waves
    gain_one, gain_two = norm1_gain[None], norm2_gain[None]

    single = jnp.argmax(jnp.max(doc_lengths, axis=1)).astype(jnp.int32)
    every_row = jnp.arange(rows, dtype=jnp.int32)
    order = (every_row + single) % rows
    doc_lengths = doc_lengths[order]

    def take(array, n):
        picked = [lax.dynamic_index_in_dim(array, (single + r) % rows, 0, keepdims=True) for r in n]
        return picked[0] if len(picked) == 1 else jnp.concatenate(picked, axis=0)

    first_pieces, masks = gather_pieces(take(inputs, range(rows_w)))
    gathered = [first_pieces]
    for w in range(1, waves):
        block = after(take(inputs, range(w * rows_w, (w + 1) * rows_w)), *first_pieces[:2])
        gathered.append([swap(block, "blk", m) if m else block for m in masks])

    place_of = [0] * circle
    for p, m in enumerate(masks):
        place_of[m] = p
    every = jnp.arange(tiles, dtype=jnp.int32)
    place = jnp.array(place_of, jnp.int32)[every // slots ^ own] * slots + every % slots
    work = jnp.array(plan.table(), jnp.int32)[:, :, own]
    bounds = jnp.cumsum(doc_lengths, axis=1)
    begin = jnp.max(jnp.where(bounds[:, None, :] <= work[:, :, None] * tile, bounds[:, None, :], 0), axis=2) // tile
    info = jnp.stack((begin, work - begin + 1, place[work]), axis=2).reshape(tasks, 3).astype(jnp.int32)
    infos = [info[w * tasks_w:(w + 1) * tasks_w] for w in range(waves)]

    pre_wide, post_wide = widened(head_mix_pre, head_mix_post, width)
    no_gain = jnp.zeros((1, width), F32)
    infos[0] = after(infos[0], pre_wide, post_wide, no_gain, *infos[1:])
    ahead = []
    for w in range(waves):
        if w == waves - 1:
            source = take(after(out_cotangent, *[a[0] for a in ahead]), range(rows)).reshape(rows, slots, tile, width)
            cotangent = plan.move([jnp.stack([source[r, c] for r, c in places]) for places in plan.groups.values()])
        info_w = after(infos[w], ahead[-1][0]) if w else infos[w]
        ahead.append(forward(info_w, place, head_mix_pre, head_mix_post, gain_one, w_query, w_key, w_value, gathered[w], tile))

    cotangent = [after(c, *[a[0] for a in ahead]) for c in cotangent]
    spots = plan.spots()
    *output, d_attended, d_middle, grad_across, grad_along, grad_gain_two = feed_forward(
        gain_two, w_attn_out, w_ff_in, w_ff_out,
        [a[4].reshape(tasks_w * tile, width) for a in ahead], [a[0].reshape(tasks_w * tile, width) for a in ahead], cotangent, spots,
    )
    d_attended = d_attended.reshape(tasks, tile, width)
    d_middle = d_middle.reshape(tasks, tile, width)

    def restore(listed):
        if rows == 2:
            return jnp.stack([jnp.where(single == 0, listed[r], listed[1 - r]) for r in range(2)])
        array = jnp.stack(listed)
        return array[(every_row - single) % rows]

    blk, dp = [("blk", b) for b in bits_of("blk")], [("dp", b) for b in bits_of("dp")]
    chains = [Exchange(grad_across, [blk[i:i + 2] for i in range(0, len(blk), 2)] + [dp])]
    for chain in chains:
        chain.send()
    along = lax.psum_scatter(grad_along, ("dp", "blk"), scatter_dimension=0, tiled=True)
    output = plan.move(output, back=True)
    heads = head_mix_pre.shape[0]
    devices = lax.axis_size("dp") * circle
    share = width // devices
    input_rows, earlier = [], []
    for w in range(waves):
        attended, sums, inverse, queries, x_own, probs, values, keys_t, x_all = ahead[w]
        info_w = infos[w]
        if w:
            info_w = after(info_w, *earlier, *output, *[chain.held for chain in chains])
        last = w == waves - 1
        d_x, grad_qkv = backward(
            info_w, place, head_mix_pre, head_mix_post, pre_wide, post_wide, gain_one, grad_gain_two if last else no_gain, share,
            w_query, w_key, w_value, queries, d_attended, d_middle, w, keys_t, values, x_all, sums, inverse, probs, earlier, tile,
        )
        if not last:
            output = [after(o, grad_qkv) for o in output]
        for pending in chains + input_rows:
            pending.await_(grad_qkv, *([] if last else output))
        if not last:
            for pending in chains + input_rows:
                pending.receive()
        earlier = [grad_qkv]
        input_rows.append(Scatter(d_x, masks, [[b] for b in bits_of("blk")] if last else [bits_of("blk")]))
        if not last:
            for pending in chains + input_rows:
                pending.send()
    for pending in chains + input_rows[:-1]:
        grad_qkv = after(grad_qkv, *pending.pending())
    grad_qkv, along = lax.optimization_barrier((grad_qkv, along))
    qkv = Chain(grad_qkv, [blk[:1]])
    for pending in [qkv, input_rows[-1]]:
        pending.send()
        pending.receive()
    rest = [[b] for b in blk[1:] + dp[2:]]
    halves = qkv.halves(2 * width - 3 * 128, [[[b] for b in dp[:2]] + rest, [[b] for b in dp[1::-1]] + rest])
    for half in halves:
        half.send()
    input_rows[-1].send()
    sent = [s for half in halves for s in half.sent]
    for pending in chains + input_rows[:-1]:
        pending.await_(*sent)
        pending.receive()
        while pending.stages:
            pending.send()
            pending.receive()
    spots = dict(zip([(r, c) for r in range(rows) for c in range(slots)], spots))
    output = [after(o, *sent) for o in output]
    output = restore([jnp.concatenate([output[spots[r, c][0]][spots[r, c][1]] for c in range(slots)]) for r in range(rows)])
    across = chains[0].held
    inner = w_ff_in.shape[1]
    across = (across[:, :inner], across[:, inner:])
    ready = [pending.held[0].astype(BF16) for pending in input_rows[:-1]]
    for half in halves:
        half.receive()
    while any(half.stages for half in halves):
        for half in halves:
            half.send()
        for half in halves:
            half.receive()
    final = input_rows[-1]
    final.receive()
    while final.stages:
        final.send()
        final.receive()
    input_grad = restore([v[r] for v in ready + [final.held[0].astype(BF16)] for r in range(rows_w)])
    total = jnp.concatenate([half.held for half in halves], axis=1)
    side = total[:, 3 * width:]
    mix_grads = [[side[at % share, 2 + heads * (at // share):][:heads] for at in range(n * heads, (n + 1) * heads)] for n in range(2)]
    return (
        output,
        input_grad,
        side[:, 0],
        total[:, :width],
        total[:, width:2 * width],
        total[:, 2 * width:3 * width],
        jnp.stack(mix_grads[0], axis=1),
        jnp.stack(mix_grads[1]),
        across[1],
        side[:, 1],
        across[0],
        along,
    )


def solution(mesh):
    tokens = P("dp", "blk", None)
    split = P(("dp", "blk"), None)
    in_specs = (tokens, P("dp", None)) + (P(),) * 10 + (tokens,)
    out_specs = (tokens, tokens, P(("dp", "blk")), split, split, split, P(), P(), split, P(("dp", "blk")), split, split)
    return jax.shard_map(shards, mesh=mesh, in_specs=in_specs, out_specs=out_specs, check_vma=False)
```
